32 devices in a mesh: groups: 2 (over y), panels: 4 (over z), cols: 2 (over x), phase: 2 (over core).
Axes of the slice: x: 2, y: 2, z: 4, core: 2. Of those that a mesh axis runs over, the one named last changes fastest.
Arguments:
- base_points: float32 [3, 512], P(None, ('groups', 'panels', 'cols')), parts along dimension 1, may hold values from -6 to 6
- control_points: float32 [3, 2048], replicated, may hold values from -6 to 6
- morph_weights: float32 [4, 3, 2048], P('groups'), parts along dimension 0, may hold values from -0.15 to 0.15
- connectivity: int32 [3, 1024], P(None, ('groups', 'panels', 'cols')), parts along dimension 1, may hold values from 0 to 255, as said below
- free_flags: int32 [1024], P(('groups', 'panels', 'cols')), parts along dimension 0, may hold values 0 or 1
- station_owner: int32 [1024, 1], P(('groups', 'panels', 'cols')), parts along dimension 0, may hold values from 0 to 7; in each aligned block of 64 rows (0 to 63, 64 to 127, ...) at most 20 rows name the same one
- variant_order: int32 [4], P('groups'), parts along dimension 0, may hold values from 0 to 1, each once
- load_velocity: float32 [64, 3], replicated, may hold values from -5 to 5
Outputs:
- shear: float32 [4, 64, 1024], P(('groups', 'phase'), None, ('panels', 'cols')), parts along dimension 0
- moment: float32 [4, 64, 1024], P(('groups', 'phase'), None, ('panels', 'cols')), parts along dimension 0
The draws below stay inside these ranges and needn't reach their ends.
There are 2 independent parts, one for each index of `groups`. The reference program is written for one: setup_inputs(seed, part) draws one part's arguments, and reference() takes and returns one part's arrays. A program takes and returns all parts, laid end to end along the dimension named above; an argument that names none is the same for every part. Nothing has to cross between parts.
Inputs may be any that keep to these rules, and one draw needn't show every extreme that they name: `connectivity`: the vertices of panel i lie in block i // 64 of 32 consecutive vertices: from (i // 64) * 32 to (i // 64 + 1) * 32 - 1. `station_owner`: among the panels of one device (aligned blocks of 64 panels) no station owner is named more than 20 times. `variant_order`: each variant appears once.
All inputs are finite; a program needn't handle non-finite values. No bound on the sum of `free_flags` on one device may be relied on, other than what follows from the above.
Results may differ from the reference program's by a relative error of at most 0.0015.
Values may be sent and summed in bfloat16 or wider, within the bound.
No kernel may reach another device: no remote copies, remote signals or barrier semaphores. Data moves between devices by JAX's collectives and lax.ppermute only.
A program may use at most 64 MiB of HBM per device.

```python
import math
import jax
import jax.numpy as jnp
import numpy as np
from jax import lax

PAN_DEV = 64
CONTROL = 2048
LOADS = 64
STATIONS = 128
VERT_DEV = 32
PANELS = 512
VERTS = 256
VARIANTS = 2
STATIONS_ALL = 1024
CAPACITY = 20
N_PANELS = 4
N_COLS = 2


def draw_connectivity(key, part):
    local_rows = jax.random.randint(key, (3, PANELS), 0, VERT_DEV, dtype=jnp.int32)
    block_start = jnp.arange(PANELS, dtype=jnp.int32) // PAN_DEV * VERT_DEV
    return (local_rows + block_start[None, :]).astype(jnp.int32)


def plant(array, own_key, low, largest):
    spot = [jax.random.randint(jax.random.fold_in(own_key, axis), (), 0, length) for axis, length in enumerate(array.shape)]
    longest = array.shape.index(max(array.shape))
    beside = spot[:longest] + [(spot[longest] + 1) % array.shape[longest]] + spot[longest + 1:]
    return array.at[tuple(spot)].set(low).at[tuple(beside)].set(largest)


def levels(rng, extent, split, least, largest):
    factor_of, own = 1.0, jax.random.fold_in(rng, 6)
    for axis_at, shards_of in split:
        steps = jnp.exp(jax.random.uniform(jax.random.fold_in(own, axis_at), (shards_of,), jnp.float32, least / len(split), largest / len(split)))
        factor_of = factor_of * jnp.repeat(steps, extent[axis_at] // shards_of).reshape([-1 if axis == axis_at else 1 for axis in range(len(extent))])
    return factor_of


def routed_block(own_key, own, number, rows, number_of, top, reach, skew):
    ranking = jax.random.permutation(own_key, number_of)
    crowded, common = shares(number_of, rows * top, reach, skew, True), shares(number_of, rows * top, reach, skew, False)
    places = jnp.arange(number_of)

    def named(sizes, rotation):
        used = int((sizes > 0).sum())
        fixed = max(1, used // 4)
        shifted = fixed + (places - fixed + rotation * (used - fixed)) % max(1, number_of - fixed)
        return jnp.zeros((number_of,), jnp.int32).at[ranking[jnp.where(places < fixed, places, shifted)]].set(jnp.asarray(sizes, jnp.int32))

    sizes = jnp.where(number % 4 == 0, named(crowded, number // 4), named(common, number - number // 4 - 1))
    mixed = jax.random.permutation(jax.random.fold_in(own, 3), number_of)
    source_of, taker = mixed[0:number_of // 2 * 2:2], mixed[1:number_of // 2 * 2:2]
    margin = jnp.minimum(sizes[source_of] - 1, reach - sizes[taker]) // 2
    margin = jnp.where((source_of == ranking[0]) | (taker == ranking[0]) | (sizes[taker] == 0), 0, jnp.maximum(margin, 0))
    shifted = jax.random.randint(jax.random.fold_in(own, 4), (number_of // 2,), 0, 1 << 20) % (margin + 1)
    sizes = sizes.at[source_of].add(-shifted).at[taker].add(shifted)
    members = jnp.searchsorted(jnp.cumsum(sizes), jnp.arange(rows * top), side="right").astype(jnp.int32)
    grid = members.reshape(top, rows).T
    grid = grid[jax.random.permutation(jax.random.fold_in(own, 1), rows)]
    rotation = jax.random.randint(jax.random.fold_in(own, 2), (rows, 1), 0, top)
    return jnp.take_along_axis(grid, (jnp.arange(top)[None, :] + rotation) % top, axis=1)


def shares(count, total, bound, slope, full):
    weights = [(1 << 20) // math.isqrt(rank ** slope) + 1 for rank in range(1, count + 1)]
    largest = bound if full else min(bound, max(-(-total // count), total * weights[0] // sum(weights)))
    least = 1 if total - largest >= count - 1 else 0
    given, rest = [largest] + [least] * (count - 1), total - largest - least * (count - 1)
    while rest > 0:
        movable = [i for i in range(1, count) if given[i] < largest] or [i for i in range(1, count) if given[i] < bound]
        whole, budget = sum([weights[i] for i in movable]), rest
        for i in movable:
            more = min(bound - given[i], max(1, budget * weights[i] // whole), rest)
            given[i] = given[i] + more
            rest = rest - more
    return np.array(given)


def noise(stream_key, dims, spread, limit, shards=(), kind=jnp.bfloat16):
    factor_of = levels(stream_key, dims, shards, -0.22, 0.18) if shards else 1.0
    values = jax.random.normal(stream_key, dims, jnp.float32) * spread * factor_of
    return jnp.minimum(jnp.maximum(values, -limit), limit).astype(kind)


def setup_inputs(seed: int = 0, part: int = 0) -> dict:
    streams_of = jax.random.split(jax.random.key(seed), 9)
    part_keys = jax.random.split(jax.random.fold_in(streams_of[8], part), 9)
    base_points = noise(part_keys[0], (3, VERTS), 1.0, 6.0, ((1, 8),), jnp.float32)
    control_points = noise(streams_of[1], (3, CONTROL), 1.0, 6.0, (), jnp.float32)
    morph_weights = noise(part_keys[2], (VARIANTS, 3, CONTROL), 0.025, 0.15, (), jnp.float32)
    connectivity = draw_connectivity(jax.random.fold_in(jax.random.fold_in(streams_of[8], part), 71), part)
    free_flags = plant((jax.random.randint(part_keys[4], (PANELS,), 0, 4) < 1).astype(jnp.int32), jax.random.fold_in(part_keys[4], 1), 0, 1)
    station_owner_keys = jax.random.split(jax.random.fold_in(part_keys[5], 1), PANELS // PAN_DEV)
    station_owner_turns = jax.random.permutation(jax.random.fold_in(part_keys[5], 3), PANELS // PAN_DEV)
    station_owner = jax.vmap(lambda own, number: routed_block(jax.random.fold_in(part_keys[5], 2), own, number, PAN_DEV, N_PANELS * N_COLS, 1, CAPACITY, 2))(station_owner_keys, station_owner_turns).reshape((PANELS, 1))
    variant_order = jax.random.permutation(part_keys[6], VARIANTS).astype(jnp.int32)
    load_velocity = noise(streams_of[7], (LOADS, 3), 1.0, 5.0, (), jnp.float32)
    return dict(base_points=base_points, control_points=control_points, morph_weights=morph_weights, connectivity=connectivity, free_flags=free_flags, station_owner=station_owner, variant_order=variant_order, load_velocity=load_velocity)


HIGH = lax.Precision.HIGHEST
CORE_SQUARE = 0.0025
SKIN_SQUARE = 0.01

def panel_shape(moved_points, corner_rows):
    first_corner = jnp.take(moved_points, corner_rows[0], axis=2)
    second_corner = jnp.take(moved_points, corner_rows[1], axis=2)
    third_corner = jnp.take(moved_points, corner_rows[2], axis=2)
    centroid = (first_corner + second_corner + third_corner) / 3.0
    edge_one = second_corner - first_corner
    edge_two = third_corner - first_corner
    cross_x = edge_one[:, 1] * edge_two[:, 2] - edge_one[:, 2] * edge_two[:, 1]
    cross_y = edge_one[:, 2] * edge_two[:, 0] - edge_one[:, 0] * edge_two[:, 2]
    cross_z = edge_one[:, 0] * edge_two[:, 1] - edge_one[:, 1] * edge_two[:, 0]
    area = 0.5 * jnp.stack([cross_x, cross_y, cross_z], axis=1)
    weight = jnp.sqrt(lax.optimization_barrier(jnp.sum(area * area, axis=1)) + SKIN_SQUARE)
    return (centroid, area, weight)

def apply_influence(centroid, weight, strengths, kernel_scale):

    def per_variant(operands):
        centres, weights, values = operands
        values_wide = values.astype(jnp.float32)
        row_blocks = centres.reshape(3, -1, PAN_DEV).transpose(1, 0, 2)

        def per_block(targets):
            distance = (targets[0][:, None] - centres[0][None, :]) ** 2 + (targets[1][:, None] - centres[1][None, :]) ** 2 + (targets[2][:, None] - centres[2][None, :]) ** 2
            influence = (weights[None, :] * kernel_scale * lax.rsqrt(distance + CORE_SQUARE)).astype(jnp.bfloat16)
            return jnp.dot(values_wide, influence.astype(jnp.float32).T, precision=HIGH)
        result = lax.map(per_block, row_blocks)
        return result.transpose(1, 0, 2).reshape(values.shape[0], -1)
    return lax.map(per_variant, (centroid, weight, strengths))

def reference(base_points, control_points, morph_weights, connectivity, free_flags, station_owner, variant_order, load_velocity):
    chosen = morph_weights[variant_order]
    vertex_blocks = base_points.reshape(3, -1, VERT_DEV).transpose(1, 0, 2)

    def move_block(block_points):
        distance = (control_points[0][:, None] - block_points[0][None, :]) ** 2 + (control_points[1][:, None] - block_points[1][None, :]) ** 2 + (control_points[2][:, None] - block_points[2][None, :]) ** 2
        basis_values = lax.rsqrt(1.0 + distance)
        return block_points[None] + jnp.einsum('mac,cn->man', chosen, basis_values, precision=HIGH)
    moved_blocks = lax.map(move_block, vertex_blocks)
    moved_points = moved_blocks.transpose(1, 2, 0, 3).reshape(VARIANTS, 3, VERTS)
    centroid, area, weight = panel_shape(moved_points, connectivity)
    hull_mask = (1 - free_flags).astype(jnp.float32)
    boundary = jnp.einsum('ka,man->mkn', load_velocity, area, precision=HIGH) * hull_mask[None, None, :]
    first_strengths = boundary.astype(jnp.bfloat16)
    kernel_scale = 1.0 / (4.0 * math.pi * math.sqrt(PANELS))
    induced = apply_influence(centroid, weight, first_strengths, kernel_scale)
    second_strengths = (first_strengths.astype(jnp.float32) + (boundary - induced)).astype(jnp.bfloat16)
    pressure = apply_influence(centroid, weight, second_strengths, kernel_scale)
    panel_force = pressure * (area[:, 2, :] * hull_mask[None, :])[:, None, :]
    station_index = station_owner[:, 0] * STATIONS + jnp.arange(PANELS, dtype=jnp.int32) % STATIONS
    station_loads = jax.ops.segment_sum(panel_force.reshape(-1, PANELS).T, station_index, num_segments=STATIONS_ALL)
    station_place = jnp.arange(STATIONS_ALL, dtype=jnp.float32)[:, None] / STATIONS_ALL
    running = jnp.cumsum(station_loads, axis=0)
    earlier = running - station_loads
    placed_loads = station_loads * station_place
    moment_arm = jnp.cumsum(placed_loads, axis=0) - placed_loads
    inv_root = 1.0 / math.sqrt(PANELS)
    shear = (running * inv_root).T.reshape(VARIANTS, LOADS, STATIONS_ALL)
    moment = ((station_place * earlier - moment_arm) * inv_root).T.reshape(VARIANTS, LOADS, STATIONS_ALL)
    return (shear, moment)
```

```python
import functools
import math

import jax
import jax.numpy as jnp
from jax import lax
from jax.experimental import pallas as pl
from jax.experimental.pallas import tpu as pltpu
from jax.sharding import PartitionSpec as P

STATIONS = 128
LANES = 128
PANELS_ON_ONE = 1024


HIGH = lax.Precision.HIGHEST
CORE_SQUARE = 0.0025
SKIN_SQUARE = 0.01


def prefix(shard, axis, combine, identity):
    length, index = (lax.axis_size(axis), lax.axis_index(axis))
    everything = jax.tree.map(lambda part: lax.all_gather(part, axis), shard)
    start = jax.tree.map(
        lambda part, zero: jnp.broadcast_to(jnp.asarray(zero, part.dtype), part.shape),
        shard,
        identity,
    )

    def step(k, before):
        reached = k < index
        new = combine(before, jax.tree.map(lambda part: part[k], everything))
        return jax.tree.map(lambda a, b: jnp.where(reached, a, b), new, before)

    return lax.fori_loop(0, length, step, start)


def panel_shape(moved_points, corner_rows):
    first_corner = jnp.take(moved_points, corner_rows[0], axis=2)
    second_corner = jnp.take(moved_points, corner_rows[1], axis=2)
    third_corner = jnp.take(moved_points, corner_rows[2], axis=2)
    centroid = (first_corner + second_corner + third_corner) / 3.0
    edge_one = second_corner - first_corner
    edge_two = third_corner - first_corner
    cross_x = edge_one[:, 1] * edge_two[:, 2] - edge_one[:, 2] * edge_two[:, 1]
    cross_y = edge_one[:, 2] * edge_two[:, 0] - edge_one[:, 0] * edge_two[:, 2]
    cross_z = edge_one[:, 0] * edge_two[:, 1] - edge_one[:, 1] * edge_two[:, 0]
    area = 0.5 * jnp.stack([cross_x, cross_y, cross_z], axis=1)
    weight = jnp.sqrt(jnp.sum(area * area, axis=1) + SKIN_SQUARE)
    return (centroid, area, weight)


def tile_block(targets, sources, strengths, kernel_scale):
    distance = (
        (targets[:, 0, :, None] - sources[:, 0, None, :]) ** 2
        + (targets[:, 1, :, None] - sources[:, 1, None, :]) ** 2
        + (targets[:, 2, :, None] - sources[:, 2, None, :]) ** 2
    )
    influence = (sources[:, 3, None, :] * kernel_scale * lax.rsqrt(distance + CORE_SQUARE)).astype(
        jnp.bfloat16
    )
    return jnp.einsum("mrn,mkn->mkr", influence, strengths, preferred_element_type=jnp.float32)


def tile_product(carry_sum, targets, sources, strengths, kernel_scale):
    columns = strengths.shape[2]
    block_width = columns
    for candidate in (2048, 1024, 512):
        if columns > candidate and columns % candidate == 0:
            block_width = candidate
            break
    if block_width == columns:
        return carry_sum + tile_block(targets, sources, strengths, kernel_scale)

    def block_step(step_index, running_sum):
        column_start = step_index * block_width
        part_sources = lax.dynamic_slice_in_dim(sources, column_start, block_width, 2)
        part_strengths = lax.dynamic_slice_in_dim(strengths, column_start, block_width, 2)
        return running_sum + tile_block(targets, part_sources, part_strengths, kernel_scale)

    return lax.fori_loop(0, columns // block_width, block_step, carry_sum)


def add_pairs(earlier, later):
    return (earlier[0] + later[0], earlier[1] + later[1])


def shards_split(
    base_points,
    control_points,
    morph_weights,
    connectivity,
    free_flags,
    station_owner,
    variant_order,
    load_velocity,
):
    owners = lax.axis_size(("panels", "cols"))
    owner_index = lax.axis_index(("panels", "cols"))
    phase_index = lax.axis_index("phase")
    variant_dev = variant_order.shape[0] // lax.axis_size("phase")
    vert_dev = base_points.shape[1]
    pan_dev = connectivity.shape[1]
    load_count = load_velocity.shape[0]
    panels_total = pan_dev * owners
    own_variants = lax.dynamic_slice_in_dim(
        variant_order, phase_index * variant_dev, variant_dev, 0
    )
    picker = (
        own_variants[:, None] == jnp.arange(variant_order.shape[0], dtype=jnp.int32)[None, :]
    ).astype(jnp.float32)
    chosen = jnp.einsum("mv,vac->mac", picker, morph_weights, precision=HIGH)
    distance = (
        (control_points[0][:, None] - base_points[0][None, :]) ** 2
        + (control_points[1][:, None] - base_points[1][None, :]) ** 2
        + (control_points[2][:, None] - base_points[2][None, :]) ** 2
    )
    basis_values = lax.rsqrt(1.0 + distance)
    moved_points = base_points[None] + jnp.einsum(
        "mac,cn->man", chosen, basis_values, precision=HIGH
    )
    local_corners = connectivity - owner_index * vert_dev
    centroid, area, weight = panel_shape(moved_points, local_corners)
    hull_mask = (1 - free_flags).astype(jnp.float32)
    boundary = (
        jnp.einsum("ka,man->mkn", load_velocity, area, precision=HIGH) * hull_mask[None, None, :]
    )
    first_strengths = boundary.astype(jnp.bfloat16)
    kernel_scale = 1.0 / (4.0 * math.pi * math.sqrt(panels_total))
    own_geometry = jnp.concatenate([centroid, weight[:, None, :]], axis=1)
    sources = lax.all_gather(own_geometry, "panels", axis=2, tiled=True)
    row_targets = lax.all_gather(centroid, "cols", axis=2, tiled=True)

    def apply_influence(strengths):
        empty_sum = jnp.zeros((variant_dev, load_count, row_targets.shape[2]), jnp.float32)
        partial_sums = tile_product(
            empty_sum,
            row_targets,
            sources,
            lax.all_gather(strengths, "panels", axis=2, tiled=True),
            kernel_scale,
        )
        return lax.psum_scatter(partial_sums, "cols", scatter_dimension=2, tiled=True)

    induced = apply_influence(first_strengths)
    second_strengths = (first_strengths.astype(jnp.float32) + (boundary - induced)).astype(
        jnp.bfloat16
    )
    pressure = apply_influence(second_strengths)
    panel_force = pressure * (area[:, 2, :] * hull_mask[None, :])[:, None, :]
    force_rows = panel_force.reshape(-1, pan_dev)
    capacity = max(2, 5 * pan_dev // (2 * owners))
    target_owner = station_owner[:, 0]
    panel_order = jnp.arange(pan_dev, dtype=jnp.int32)
    ahead = (target_owner[:, None] == target_owner[None, :]) & (
        panel_order[None, :] < panel_order[:, None]
    )
    slot_rank = jnp.sum(ahead.astype(jnp.int32), axis=1)
    slot_index = target_owner * capacity + slot_rank
    all_slots = jnp.arange(owners * capacity, dtype=jnp.int32)
    placed = slot_index[:, None] == all_slots[None, :]
    send_values = jnp.dot(force_rows, placed.astype(jnp.float32), precision=HIGH)
    station_bins = (owner_index * pan_dev + panel_order) % STATIONS
    send_bins = jnp.max(jnp.where(placed, station_bins[:, None], -1), axis=0)[None, :]
    recv_values, recv_bins = (
        lax.all_to_all(send_values, ("panels", "cols"), split_axis=1, concat_axis=1, tiled=True),
        lax.all_to_all(send_bins, ("panels", "cols"), split_axis=1, concat_axis=1, tiled=True),
    )
    matches = (recv_bins[0][:, None] == jnp.arange(STATIONS, dtype=jnp.int32)[None, :]).astype(
        jnp.float32
    )
    station_loads = jnp.dot(recv_values, matches, precision=HIGH)
    station_place = (owner_index * STATIONS + jnp.arange(STATIONS, dtype=jnp.int32)).astype(
        jnp.float32
    ) / (STATIONS * owners)
    placed_loads = station_loads * station_place[None, :]
    own_total = jnp.sum(station_loads, axis=1)
    own_arm = jnp.sum(placed_loads, axis=1)
    zero_row = jnp.zeros_like(own_total)
    prior_total, prior_arm = prefix(
        (own_total, own_arm), ("panels", "cols"), add_pairs, (zero_row, zero_row)
    )
    station_rank = jnp.arange(STATIONS, dtype=jnp.int32)
    inclusive = (station_rank[:, None] <= station_rank[None, :]).astype(jnp.float32)
    strict = (station_rank[:, None] < station_rank[None, :]).astype(jnp.float32)
    running = prior_total[:, None] + jnp.dot(station_loads, inclusive, precision=HIGH)
    earlier = prior_total[:, None] + jnp.dot(station_loads, strict, precision=HIGH)
    moment_arm = prior_arm[:, None] + jnp.dot(placed_loads, strict, precision=HIGH)
    inv_root = 1.0 / math.sqrt(panels_total)
    shear = (running * inv_root).reshape(variant_dev, load_count, STATIONS)
    moment = ((station_place[None, :] * earlier - moment_arm) * inv_root).reshape(
        variant_dev, load_count, STATIONS
    )
    return (shear, moment)


def geometry_kernel(
    vert_dev,
    order_ref,
    base_ref,
    control_ref,
    weights_ref,
    corner_ref,
    flags_ref,
    owner_ref,
    out_ref,
):
    variant = order_ref[lax.axis_index("phase")]
    pan_dev = corner_ref.shape[1]
    diagonal = lax.broadcasted_iota(jnp.int32, (vert_dev, vert_dev), 0) == lax.broadcasted_iota(
        jnp.int32, (vert_dev, vert_dev), 1
    )
    base = [
        jnp.sum(jnp.where(diagonal, base_ref[a : a + 1, :], 0.0), axis=1, keepdims=True)
        for a in range(3)
    ]
    totals = [jnp.zeros((vert_dev, LANES), jnp.float32) for _ in range(3)]
    for start in range(0, control_ref.shape[1], LANES):
        part = pl.ds(start, LANES)
        distance = (
            (control_ref[0:1, part] - base[0]) ** 2
            + (control_ref[1:2, part] - base[1]) ** 2
            + (control_ref[2:3, part] - base[2]) ** 2
        )
        basis = lax.rsqrt(1.0 + distance)
        totals = [totals[a] + weights_ref[variant, a : a + 1, part] * basis for a in range(3)]
    moved = [base[a] + jnp.sum(totals[a], axis=1, keepdims=True) for a in range(3)]
    vertex = lax.broadcasted_iota(jnp.int32, (vert_dev, pan_dev), 0)
    corners = []
    for k in range(3):
        chosen = vertex == lax.rem(corner_ref[k : k + 1, :], vert_dev)
        corners.append(
            [jnp.sum(jnp.where(chosen, moved[a], 0.0), axis=0, keepdims=True) for a in range(3)]
        )
    first, second, third = corners
    centroid = [(first[a] + second[a] + third[a]) * (1.0 / 3.0) for a in range(3)]
    one = [second[a] - first[a] for a in range(3)]
    two = [third[a] - first[a] for a in range(3)]
    area = [
        0.5 * (one[1] * two[2] - one[2] * two[1]),
        0.5 * (one[2] * two[0] - one[0] * two[2]),
        0.5 * (one[0] * two[1] - one[1] * two[0]),
    ]
    hull = (1 - flags_ref[...]).astype(jnp.float32)
    owner = owner_ref[...].astype(jnp.float32)
    rows = jnp.concatenate(centroid + area + [hull, owner], axis=0)
    rows = jnp.concatenate([rows] * (LANES // pan_dev), axis=1)
    last = lax.broadcasted_iota(jnp.int32, rows.shape, 0) == rows.shape[0] - 1
    for target in range(out_ref.shape[0]):
        out_ref[target] = jnp.where(last, rows - float(target), rows)


def loads_kernel(pan_dev, kernel_scale, rows_ref, velocity_ref, shear_ref, moment_ref, influence):
    owners = rows_ref.shape[0]
    shared = LANES // pan_dev
    tiles = owners // shared
    panels_total = owners * pan_dev
    load_count = velocity_ref.shape[0]
    lane = lax.broadcasted_iota(jnp.int32, (8, LANES), 1)
    panels, columns = [], []
    for q in range(tiles):
        tile = rows_ref[q * shared]
        for h in range(1, shared):
            tile = jnp.where(lane >= h * pan_dev, rows_ref[q * shared + h], tile)
        panels.append(tile)
        area = [tile[3 + a : 4 + a, :] for a in range(3)]
        weight = jnp.sqrt(area[0] * area[0] + area[1] * area[1] + area[2] * area[2] + SKIN_SQUARE)
        columns.append(
            jnp.concatenate([tile[0:3, :], weight * kernel_scale, tile[4:8, :]], axis=0).T
        )
    for source in range(tiles):
        column = columns[source]
        centre = [column[:, a : a + 1] for a in range(3)]
        weight = column[:, 3:4]
        for target in range(tiles):
            tile = panels[target]
            distance = (
                (tile[0:1, :] - centre[0]) ** 2
                + (tile[1:2, :] - centre[1]) ** 2
                + (tile[2:3, :] - centre[2]) ** 2
            )
            influence[pl.ds(source * LANES, LANES), pl.ds(target * LANES, LANES)] = (
                weight * lax.rsqrt(distance + CORE_SQUARE)
            ).astype(jnp.bfloat16)
    velocity = [velocity_ref[:, a : a + 1] for a in range(3)]
    boundary = jnp.concatenate(
        [
            (velocity[0] * tile[3:4, :] + velocity[1] * tile[4:5, :] + velocity[2] * tile[5:6, :])
            * tile[6:7, :]
            for tile in panels
        ],
        axis=1,
    )
    first = boundary.astype(jnp.bfloat16)
    induced = jnp.dot(first, influence[...], preferred_element_type=jnp.float32)
    second = (first.astype(jnp.float32) + (boundary - induced)).astype(jnp.bfloat16)
    pressure = jnp.dot(second, influence[...], preferred_element_type=jnp.float32)

    stations_all = STATIONS * owners
    own_loads = jnp.zeros((load_count, LANES), jnp.float32)
    prior_loads = jnp.zeros((load_count, LANES), jnp.float32)
    prior_arms = jnp.zeros((load_count, LANES), jnp.float32)
    rank = lax.broadcasted_iota(jnp.int32, (1, LANES), 1).astype(jnp.float32)
    for q, tile in enumerate(panels):
        force = pressure[:, q * LANES : (q + 1) * LANES] * (tile[5:6, :] * tile[6:7, :])
        owner = tile[7:8, :]
        prior = owner < 0.0
        place = (owner * STATIONS + rank) * (1.0 / stations_all)
        own_loads = own_loads + jnp.where(owner == 0.0, force, 0.0)
        prior_loads = prior_loads + jnp.where(prior, force, 0.0)
        prior_arms = prior_arms + force * jnp.where(prior, place, 0.0)
    prior_total = jnp.sum(prior_loads, axis=1, keepdims=True)
    prior_arm = jnp.sum(prior_arms, axis=1, keepdims=True)
    station = lax.broadcasted_iota(jnp.int32, (STATIONS, 2 * STATIONS), 0)
    place = lax.broadcasted_iota(jnp.int32, (STATIONS, 2 * STATIONS), 1)
    arm = place - STATIONS - station
    steps = jnp.where(
        place < STATIONS, (station <= place).astype(jnp.int32), jnp.maximum(arm, 0)
    ).astype(jnp.float32).astype(jnp.bfloat16)
    high = own_loads.astype(jnp.bfloat16)
    rest = own_loads - high.astype(jnp.float32)
    middle = rest.astype(jnp.bfloat16)
    low = (rest - middle.astype(jnp.float32)).astype(jnp.bfloat16)
    sums = jnp.dot(
        jnp.concatenate([high, middle, low], axis=0), steps, preferred_element_type=jnp.float32
    )
    sums = sums[:load_count] + (sums[load_count : 2 * load_count] + sums[2 * load_count :])
    inv_root = 1.0 / math.sqrt(panels_total)
    shear_ref[0] = (prior_total + sums[:, :STATIONS]) * inv_root
    moment_ref[0] = (
        (rank * (1.0 / stations_all)) * prior_total
        - prior_arm
        + sums[:, STATIONS:] * (1.0 / stations_all)
    ) * inv_root


def shards_whole(
    base_points,
    control_points,
    morph_weights,
    connectivity,
    free_flags,
    station_owner,
    variant_order,
    load_velocity,
):
    owners = lax.axis_size(("panels", "cols"))
    vert_dev = base_points.shape[1]
    pan_dev = connectivity.shape[1]
    load_count = load_velocity.shape[0]
    panels_total = pan_dev * owners
    vmem = pl.BlockSpec(memory_space=pltpu.VMEM)
    rows = pl.pallas_call(
        functools.partial(geometry_kernel, vert_dev),
        out_shape=jax.ShapeDtypeStruct((owners, 8, LANES), jnp.float32),
        in_specs=[pl.BlockSpec(memory_space=pltpu.SMEM)] + [vmem] * 6,
        out_specs=vmem,
        name="geometry",
    )(
        variant_order,
        base_points,
        control_points,
        morph_weights,
        connectivity,
        free_flags.reshape(1, pan_dev),
        station_owner.reshape(1, pan_dev),
    )
    rows = lax.all_to_all(rows, ("panels", "cols"), split_axis=0, concat_axis=0)
    kernel_scale = 1.0 / (4.0 * math.pi * math.sqrt(panels_total))
    out = jax.ShapeDtypeStruct((1, load_count, STATIONS), jnp.float32)
    return pl.pallas_call(
        functools.partial(loads_kernel, pan_dev, kernel_scale),
        out_shape=(out, out),
        in_specs=[vmem] * 2,
        out_specs=(vmem, vmem),
        scratch_shapes=[pltpu.VMEM((panels_total, panels_total), jnp.bfloat16)],
        compiler_params=pltpu.CompilerParams(vmem_limit_bytes=32 * 1024 * 1024),
        name="loads",
    )(rows, load_velocity)


def shards(
    base_points,
    control_points,
    morph_weights,
    connectivity,
    free_flags,
    station_owner,
    variant_order,
    load_velocity,
):
    owners = lax.axis_size(("panels", "cols"))
    pan_dev = connectivity.shape[1]
    panels_total = owners * pan_dev
    whole = (
        panels_total <= PANELS_ON_ONE
        and panels_total % LANES == 0
        and LANES % pan_dev == 0
        and STATIONS == LANES
        and variant_order.shape[0] == lax.axis_size("phase")
        and control_points.shape[1] % LANES == 0
        and load_velocity.shape[0] % 16 == 0
    )
    return (shards_whole if whole else shards_split)(
        base_points,
        control_points,
        morph_weights,
        connectivity,
        free_flags,
        station_owner,
        variant_order,
        load_velocity,
    )


def solution(mesh):
    return jax.shard_map(
        shards,
        mesh=mesh,
        in_specs=(
            P(None, ("groups", "panels", "cols")),
            P(),
            P("groups", None, None),
            P(None, ("groups", "panels", "cols")),
            P(("groups", "panels", "cols")),
            P(("groups", "panels", "cols"), None),
            P("groups"),
            P(),
        ),
        out_specs=(
            P(("groups", "phase"), None, ("panels", "cols")),
            P(("groups", "phase"), None, ("panels", "cols")),
        ),
        check_vma=False,
    )
```

```python
import functools
import math

import jax
import jax.numpy as jnp
from jax import lax
from jax.experimental import pallas as pl
from jax.experimental.pallas import tpu as pltpu
from jax.sharding import PartitionSpec as P

STATIONS = 128
LANES = 128
PANELS_ON_ONE = 1024


HIGH = lax.Precision.HIGHEST
CORE_SQUARE = 0.0025
SKIN_SQUARE = 0.01


def prefix(shard, axis, combine, identity):
    length, index = (lax.axis_size(axis), lax.axis_index(axis))
    everything = jax.tree.map(lambda part: lax.all_gather(part, axis), shard)
    start = jax.tree.map(
        lambda part, zero: jnp.broadcast_to(jnp.asarray(zero, part.dtype), part.shape),
        shard,
        identity,
    )

    def step(k, before):
        reached = k < index
        new = combine(before, jax.tree.map(lambda part: part[k], everything))
        return jax.tree.map(lambda a, b: jnp.where(reached, a, b), new, before)

    return lax.fori_loop(0, length, step, start)


def panel_shape(moved_points, corner_rows):
    first_corner = jnp.take(moved_points, corner_rows[0], axis=2)
    second_corner = jnp.take(moved_points, corner_rows[1], axis=2)
    third_corner = jnp.take(moved_points, corner_rows[2], axis=2)
    centroid = (first_corner + second_corner + third_corner) / 3.0
    edge_one = second_corner - first_corner
    edge_two = third_corner - first_corner
    cross_x = edge_one[:, 1] * edge_two[:, 2] - edge_one[:, 2] * edge_two[:, 1]
    cross_y = edge_one[:, 2] * edge_two[:, 0] - edge_one[:, 0] * edge_two[:, 2]
    cross_z = edge_one[:, 0] * edge_two[:, 1] - edge_one[:, 1] * edge_two[:, 0]
    area = 0.5 * jnp.stack([cross_x, cross_y, cross_z], axis=1)
    weight = jnp.sqrt(jnp.sum(area * area, axis=1) + SKIN_SQUARE)
    return (centroid, area, weight)


def tile_block(targets, sources, strengths, kernel_scale):
    distance = (
        (targets[:, 0, :, None] - sources[:, 0, None, :]) ** 2
        + (targets[:, 1, :, None] - sources[:, 1, None, :]) ** 2
        + (targets[:, 2, :, None] - sources[:, 2, None, :]) ** 2
    )
    influence = (sources[:, 3, None, :] * kernel_scale * lax.rsqrt(distance + CORE_SQUARE)).astype(
        jnp.bfloat16
    )
    return jnp.einsum("mrn,mkn->mkr", influence, strengths, preferred_element_type=jnp.float32)


def tile_product(carry_sum, targets, sources, strengths, kernel_scale):
    columns = strengths.shape[2]
    block_width = columns
    for candidate in (2048, 1024, 512):
        if columns > candidate and columns % candidate == 0:
            block_width = candidate
            break
    if block_width == columns:
        return carry_sum + tile_block(targets, sources, strengths, kernel_scale)

    def block_step(step_index, running_sum):
        column_start = step_index * block_width
        part_sources = lax.dynamic_slice_in_dim(sources, column_start, block_width, 2)
        part_strengths = lax.dynamic_slice_in_dim(strengths, column_start, block_width, 2)
        return running_sum + tile_block(targets, part_sources, part_strengths, kernel_scale)

    return lax.fori_loop(0, columns // block_width, block_step, carry_sum)


def add_pairs(earlier, later):
    return (earlier[0] + later[0], earlier[1] + later[1])


def shards_split(
    base_points,
    control_points,
    morph_weights,
    connectivity,
    free_flags,
    station_owner,
    variant_order,
    load_velocity,
):
    owners = lax.axis_size(("panels", "cols"))
    owner_index = lax.axis_index(("panels", "cols"))
    phase_index = lax.axis_index("phase")
    variant_dev = variant_order.shape[0] // lax.axis_size("phase")
    vert_dev = base_points.shape[1]
    pan_dev = connectivity.shape[1]
    load_count = load_velocity.shape[0]
    panels_total = pan_dev * owners
    own_variants = lax.dynamic_slice_in_dim(
        variant_order, phase_index * variant_dev, variant_dev, 0
    )
    picker = (
        own_variants[:, None] == jnp.arange(variant_order.shape[0], dtype=jnp.int32)[None, :]
    ).astype(jnp.float32)
    chosen = jnp.einsum("mv,vac->mac", picker, morph_weights, precision=HIGH)
    distance = (
        (control_points[0][:, None] - base_points[0][None, :]) ** 2
        + (control_points[1][:, None] - base_points[1][None, :]) ** 2
        + (control_points[2][:, None] - base_points[2][None, :]) ** 2
    )
    basis_values = lax.rsqrt(1.0 + distance)
    moved_points = base_points[None] + jnp.einsum(
        "mac,cn->man", chosen, basis_values, precision=HIGH
    )
    local_corners = connectivity - owner_index * vert_dev
    centroid, area, weight = panel_shape(moved_points, local_corners)
    hull_mask = (1 - free_flags).astype(jnp.float32)
    boundary = (
        jnp.einsum("ka,man->mkn", load_velocity, area, precision=HIGH) * hull_mask[None, None, :]
    )
    first_strengths = boundary.astype(jnp.bfloat16)
    kernel_scale = 1.0 / (4.0 * math.pi * math.sqrt(panels_total))
    own_geometry = jnp.concatenate([centroid, weight[:, None, :]], axis=1)
    sources = lax.all_gather(own_geometry, "panels", axis=2, tiled=True)
    row_targets = lax.all_gather(centroid, "cols", axis=2, tiled=True)

    def apply_influence(strengths):
        empty_sum = jnp.zeros((variant_dev, load_count, row_targets.shape[2]), jnp.float32)
        partial_sums = tile_product(
            empty_sum,
            row_targets,
            sources,
            lax.all_gather(strengths, "panels", axis=2, tiled=True),
            kernel_scale,
        )
        return lax.psum_scatter(partial_sums, "cols", scatter_dimension=2, tiled=True)

    induced = apply_influence(first_strengths)
    second_strengths = (first_strengths.astype(jnp.float32) + (boundary - induced)).astype(
        jnp.bfloat16
    )
    pressure = apply_influence(second_strengths)
    panel_force = pressure * (area[:, 2, :] * hull_mask[None, :])[:, None, :]
    force_rows = panel_force.reshape(-1, pan_dev)
    capacity = max(2, 5 * pan_dev // (2 * owners))
    target_owner = station_owner[:, 0]
    panel_order = jnp.arange(pan_dev, dtype=jnp.int32)
    ahead = (target_owner[:, None] == target_owner[None, :]) & (
        panel_order[None, :] < panel_order[:, None]
    )
    slot_rank = jnp.sum(ahead.astype(jnp.int32), axis=1)
    slot_index = target_owner * capacity + slot_rank
    all_slots = jnp.arange(owners * capacity, dtype=jnp.int32)
    placed = slot_index[:, None] == all_slots[None, :]
    send_values = jnp.dot(force_rows, placed.astype(jnp.float32), precision=HIGH)
    station_bins = (owner_index * pan_dev + panel_order) % STATIONS
    send_bins = jnp.max(jnp.where(placed, station_bins[:, None], -1), axis=0)[None, :]
    recv_values, recv_bins = (
        lax.all_to_all(send_values, ("panels", "cols"), split_axis=1, concat_axis=1, tiled=True),
        lax.all_to_all(send_bins, ("panels", "cols"), split_axis=1, concat_axis=1, tiled=True),
    )
    matches = (recv_bins[0][:, None] == jnp.arange(STATIONS, dtype=jnp.int32)[None, :]).astype(
        jnp.float32
    )
    station_loads = jnp.dot(recv_values, matches, precision=HIGH)
    station_place = (owner_index * STATIONS + jnp.arange(STATIONS, dtype=jnp.int32)).astype(
        jnp.float32
    ) / (STATIONS * owners)
    placed_loads = station_loads * station_place[None, :]
    own_total = jnp.sum(station_loads, axis=1)
    own_arm = jnp.sum(placed_loads, axis=1)
    zero_row = jnp.zeros_like(own_total)
    prior_total, prior_arm = prefix(
        (own_total, own_arm), ("panels", "cols"), add_pairs, (zero_row, zero_row)
    )
    station_rank = jnp.arange(STATIONS, dtype=jnp.int32)
    inclusive = (station_rank[:, None] <= station_rank[None, :]).astype(jnp.float32)
    strict = (station_rank[:, None] < station_rank[None, :]).astype(jnp.float32)
    running = prior_total[:, None] + jnp.dot(station_loads, inclusive, precision=HIGH)
    earlier = prior_total[:, None] + jnp.dot(station_loads, strict, precision=HIGH)
    moment_arm = prior_arm[:, None] + jnp.dot(placed_loads, strict, precision=HIGH)
    inv_root = 1.0 / math.sqrt(panels_total)
    shear = (running * inv_root).reshape(variant_dev, load_count, STATIONS)
    moment = ((station_place[None, :] * earlier - moment_arm) * inv_root).reshape(
        variant_dev, load_count, STATIONS
    )
    return (shear, moment)


def geometry_kernel(
    vert_dev,
    order_ref,
    base_ref,
    control_ref,
    weights_ref,
    corner_ref,
    flags_ref,
    owner_ref,
    out_ref,
):
    variant = order_ref[lax.axis_index("phase")]
    pan_dev = corner_ref.shape[1]
    diagonal = lax.broadcasted_iota(jnp.int32, (vert_dev, vert_dev), 0) == lax.broadcasted_iota(
        jnp.int32, (vert_dev, vert_dev), 1
    )
    base = [
        jnp.sum(jnp.where(diagonal, base_ref[a : a + 1, :], 0.0), axis=1, keepdims=True)
        for a in range(3)
    ]
    totals = [jnp.zeros((vert_dev, LANES), jnp.float32) for _ in range(3)]
    for start in range(0, control_ref.shape[1], LANES):
        part = pl.ds(start, LANES)
        distance = (
            (control_ref[0:1, part] - base[0]) ** 2
            + (control_ref[1:2, part] - base[1]) ** 2
            + (control_ref[2:3, part] - base[2]) ** 2
        )
        basis = lax.rsqrt(1.0 + distance)
        for a in range(3):
            weights = weights_ref[a, 0:1, part]
            for v in range(1, weights_ref.shape[1]):
                weights = jnp.where(variant == v, weights_ref[a, v : v + 1, part], weights)
            totals[a] = totals[a] + weights * basis
    moved = [base[a] + jnp.sum(totals[a], axis=1, keepdims=True) for a in range(3)]
    vertex = lax.broadcasted_iota(jnp.int32, (vert_dev, pan_dev), 0)
    corners = []
    for k in range(3):
        chosen = vertex == lax.rem(corner_ref[k : k + 1, :], vert_dev)
        corners.append(
            [jnp.sum(jnp.where(chosen, moved[a], 0.0), axis=0, keepdims=True) for a in range(3)]
        )
    first, second, third = corners
    centroid = [(first[a] + second[a] + third[a]) * (1.0 / 3.0) for a in range(3)]
    one = [second[a] - first[a] for a in range(3)]
    two = [third[a] - first[a] for a in range(3)]
    area = [
        0.5 * (one[1] * two[2] - one[2] * two[1]),
        0.5 * (one[2] * two[0] - one[0] * two[2]),
        0.5 * (one[0] * two[1] - one[1] * two[0]),
    ]
    hull = (1 - flags_ref[...]).astype(jnp.float32)
    owner = owner_ref[...].astype(jnp.float32)
    rows = jnp.concatenate(centroid + area + [hull, owner], axis=0)
    rows = jnp.concatenate([rows] * (LANES // pan_dev), axis=1)
    last = lax.broadcasted_iota(jnp.int32, rows.shape, 0) == rows.shape[0] - 1
    for target in range(out_ref.shape[0]):
        out_ref[out_ref.shape[0] - 1 - target] = jnp.where(last, rows - float(target), rows)


def loads_kernel(pan_dev, kernel_scale, rows_ref, velocity_ref, shear_ref, moment_ref, influence):
    owners = rows_ref.shape[0]
    shared = LANES // pan_dev
    tiles = owners // shared
    panels_total = owners * pan_dev
    load_count = velocity_ref.shape[0]
    lane = lax.broadcasted_iota(jnp.int32, (8, LANES), 1)
    panels, columns = [], []
    for q in range(tiles):
        tile = rows_ref[owners - 1 - q * shared]
        for h in range(1, shared):
            tile = jnp.where(lane >= h * pan_dev, rows_ref[owners - 1 - q * shared - h], tile)
        panels.append(tile)
        area = [tile[3 + a : 4 + a, :] for a in range(3)]
        weight = jnp.sqrt(area[0] * area[0] + area[1] * area[1] + area[2] * area[2] + SKIN_SQUARE)
        columns.append(
            jnp.concatenate([tile[0:3, :], weight * kernel_scale, tile[4:8, :]], axis=0).T
        )
    for source in range(tiles):
        column = columns[source]
        centre = [column[:, a : a + 1] for a in range(3)]
        weight = column[:, 3:4]
        for target in range(tiles):
            tile = panels[target]
            distance = (
                (tile[0:1, :] - centre[0]) ** 2
                + (tile[1:2, :] - centre[1]) ** 2
                + (tile[2:3, :] - centre[2]) ** 2
            )
            influence[pl.ds(source * LANES, LANES), pl.ds(target * LANES, LANES)] = (
                weight * lax.rsqrt(distance + CORE_SQUARE)
            ).astype(jnp.bfloat16)
    velocity = [velocity_ref[:, a : a + 1] for a in range(3)]
    boundary = jnp.concatenate(
        [
            (velocity[0] * tile[3:4, :] + velocity[1] * tile[4:5, :] + velocity[2] * tile[5:6, :])
            * tile[6:7, :]
            for tile in panels
        ],
        axis=1,
    )
    first = boundary.astype(jnp.bfloat16)
    induced = jnp.dot(first, influence[...], preferred_element_type=jnp.float32)
    second = (first.astype(jnp.float32) + (boundary - induced)).astype(jnp.bfloat16)
    pressure = jnp.dot(second, influence[...], preferred_element_type=jnp.float32)

    stations_all = STATIONS * owners
    own_loads = jnp.zeros((load_count, LANES), jnp.float32)
    prior_loads = jnp.zeros((load_count, LANES), jnp.float32)
    prior_arms = jnp.zeros((load_count, LANES), jnp.float32)
    rank = lax.broadcasted_iota(jnp.int32, (1, LANES), 1).astype(jnp.float32)
    for q, tile in enumerate(panels):
        force = pressure[:, q * LANES : (q + 1) * LANES] * (tile[5:6, :] * tile[6:7, :])
        owner = tile[7:8, :]
        prior = owner < 0.0
        place = (owner * STATIONS + rank) * (1.0 / stations_all)
        own_loads = own_loads + jnp.where(owner == 0.0, force, 0.0)
        prior_loads = prior_loads + jnp.where(prior, force, 0.0)
        prior_arms = prior_arms + force * jnp.where(prior, place, 0.0)
    prior_total = jnp.sum(prior_loads, axis=1, keepdims=True)
    prior_arm = jnp.sum(prior_arms, axis=1, keepdims=True)
    station = lax.broadcasted_iota(jnp.int32, (STATIONS, 2 * STATIONS), 0)
    place = lax.broadcasted_iota(jnp.int32, (STATIONS, 2 * STATIONS), 1)
    arm = place - STATIONS - station
    steps = jnp.where(
        place < STATIONS, (station <= place).astype(jnp.int32), jnp.maximum(arm, 0)
    ).astype(jnp.float32).astype(jnp.bfloat16)
    high = own_loads.astype(jnp.bfloat16)
    rest = own_loads - high.astype(jnp.float32)
    middle = rest.astype(jnp.bfloat16)
    low = (rest - middle.astype(jnp.float32)).astype(jnp.bfloat16)
    sums = jnp.dot(
        jnp.concatenate([high, middle, low], axis=0), steps, preferred_element_type=jnp.float32
    )
    sums = sums[:load_count] + (sums[load_count : 2 * load_count] + sums[2 * load_count :])
    inv_root = 1.0 / math.sqrt(panels_total)
    shear_ref[0] = (prior_total + sums[:, :STATIONS]) * inv_root
    moment_ref[0] = (
        (rank * (1.0 / stations_all)) * prior_total
        - prior_arm
        + sums[:, STATIONS:] * (1.0 / stations_all)
    ) * inv_root


def shards_whole(
    base_points,
    control_points,
    morph_weights,
    connectivity,
    free_flags,
    station_owner,
    variant_order,
    load_velocity,
):
    owners = lax.axis_size(("panels", "cols"))
    vert_dev = base_points.shape[1]
    pan_dev = connectivity.shape[1]
    load_count = load_velocity.shape[0]
    panels_total = pan_dev * owners
    vmem = pl.BlockSpec(memory_space=pltpu.VMEM)
    rows = pl.pallas_call(
        functools.partial(geometry_kernel, vert_dev),
        out_shape=jax.ShapeDtypeStruct((owners, 8, LANES), jnp.float32),
        in_specs=[pl.BlockSpec(memory_space=pltpu.SMEM)] + [vmem] * 6,
        out_specs=vmem,
        name="geometry",
    )(
        variant_order,
        base_points,
        control_points,
        morph_weights.transpose(1, 0, 2),
        connectivity,
        free_flags.reshape(1, pan_dev),
        station_owner.reshape(1, pan_dev),
    )
    order = list(range(owners))[::-1]
    rows = lax.all_to_all(
        rows, ("panels", "cols"), split_axis=0, concat_axis=0, axis_index_groups=[order]
    )
    kernel_scale = 1.0 / (4.0 * math.pi * math.sqrt(panels_total))
    out = jax.ShapeDtypeStruct((1, load_count, STATIONS), jnp.float32)
    return pl.pallas_call(
        functools.partial(loads_kernel, pan_dev, kernel_scale),
        out_shape=(out, out),
        in_specs=[vmem] * 2,
        out_specs=(vmem, vmem),
        scratch_shapes=[pltpu.VMEM((panels_total, panels_total), jnp.bfloat16)],
        compiler_params=pltpu.CompilerParams(vmem_limit_bytes=32 * 1024 * 1024),
        name="loads",
    )(rows, load_velocity)


def shards(
    base_points,
    control_points,
    morph_weights,
    connectivity,
    free_flags,
    station_owner,
    variant_order,
    load_velocity,
):
    owners = lax.axis_size(("panels", "cols"))
    pan_dev = connectivity.shape[1]
    panels_total = owners * pan_dev
    whole = (
        panels_total <= PANELS_ON_ONE
        and panels_total % LANES == 0
        and LANES % pan_dev == 0
        and STATIONS == LANES
        and variant_order.shape[0] == lax.axis_size("phase")
        and control_points.shape[1] % LANES == 0
        and load_velocity.shape[0] % 16 == 0
    )
    return (shards_whole if whole else shards_split)(
        base_points,
        control_points,
        morph_weights,
        connectivity,
        free_flags,
        station_owner,
        variant_order,
        load_velocity,
    )


def solution(mesh):
    return jax.shard_map(
        shards,
        mesh=mesh,
        in_specs=(
            P(None, ("groups", "panels", "cols")),
            P(),
            P("groups", None, None),
            P(None, ("groups", "panels", "cols")),
            P(("groups", "panels", "cols")),
            P(("groups", "panels", "cols"), None),
            P("groups"),
            P(),
        ),
        out_specs=(
            P(("groups", "phase"), None, ("panels", "cols")),
            P(("groups", "phase"), None, ("panels", "cols")),
        ),
        check_vma=False,
    )
```

```python
import functools
import math

import jax
import jax.numpy as jnp
from jax import lax
from jax.experimental import pallas as pl
from jax.experimental.pallas import tpu as pltpu
from jax.sharding import PartitionSpec as P

STATIONS = 128
LANES = 128
PANELS_ON_ONE = 1024


HIGH = lax.Precision.HIGHEST
CORE_SQUARE = 0.0025
SKIN_SQUARE = 0.01


def prefix(shard, axis, combine, identity):
    length, index = (lax.axis_size(axis), lax.axis_index(axis))
    everything = jax.tree.map(lambda part: lax.all_gather(part, axis), shard)
    start = jax.tree.map(
        lambda part, zero: jnp.broadcast_to(jnp.asarray(zero, part.dtype), part.shape),
        shard,
        identity,
    )

    def step(k, before):
        reached = k < index
        new = combine(before, jax.tree.map(lambda part: part[k], everything))
        return jax.tree.map(lambda a, b: jnp.where(reached, a, b), new, before)

    return lax.fori_loop(0, length, step, start)


def panel_shape(moved_points, corner_rows):
    first_corner = jnp.take(moved_points, corner_rows[0], axis=2)
    second_corner = jnp.take(moved_points, corner_rows[1], axis=2)
    third_corner = jnp.take(moved_points, corner_rows[2], axis=2)
    centroid = (first_corner + second_corner + third_corner) / 3.0
    edge_one = second_corner - first_corner
    edge_two = third_corner - first_corner
    cross_x = edge_one[:, 1] * edge_two[:, 2] - edge_one[:, 2] * edge_two[:, 1]
    cross_y = edge_one[:, 2] * edge_two[:, 0] - edge_one[:, 0] * edge_two[:, 2]
    cross_z = edge_one[:, 0] * edge_two[:, 1] - edge_one[:, 1] * edge_two[:, 0]
    area = 0.5 * jnp.stack([cross_x, cross_y, cross_z], axis=1)
    weight = jnp.sqrt(jnp.sum(area * area, axis=1) + SKIN_SQUARE)
    return (centroid, area, weight)


def tile_block(targets, sources, strengths, kernel_scale):
    distance = (
        (targets[:, 0, :, None] - sources[:, 0, None, :]) ** 2
        + (targets[:, 1, :, None] - sources[:, 1, None, :]) ** 2
        + (targets[:, 2, :, None] - sources[:, 2, None, :]) ** 2
    )
    influence = (sources[:, 3, None, :] * kernel_scale * lax.rsqrt(distance + CORE_SQUARE)).astype(
        jnp.bfloat16
    )
    return jnp.einsum("mrn,mkn->mkr", influence, strengths, preferred_element_type=jnp.float32)


def tile_product(carry_sum, targets, sources, strengths, kernel_scale):
    columns = strengths.shape[2]
    block_width = columns
    for candidate in (2048, 1024, 512):
        if columns > candidate and columns % candidate == 0:
            block_width = candidate
            break
    if block_width == columns:
        return carry_sum + tile_block(targets, sources, strengths, kernel_scale)

    def block_step(step_index, running_sum):
        column_start = step_index * block_width
        part_sources = lax.dynamic_slice_in_dim(sources, column_start, block_width, 2)
        part_strengths = lax.dynamic_slice_in_dim(strengths, column_start, block_width, 2)
        return running_sum + tile_block(targets, part_sources, part_strengths, kernel_scale)

    return lax.fori_loop(0, columns // block_width, block_step, carry_sum)


def add_pairs(earlier, later):
    return (earlier[0] + later[0], earlier[1] + later[1])


def shards_split(
    base_points,
    control_points,
    morph_weights,
    connectivity,
    free_flags,
    station_owner,
    variant_order,
    load_velocity,
):
    owners = lax.axis_size(("panels", "cols"))
    owner_index = lax.axis_index(("panels", "cols"))
    phase_index = lax.axis_index("phase")
    variant_dev = variant_order.shape[0] // lax.axis_size("phase")
    vert_dev = base_points.shape[1]
    pan_dev = connectivity.shape[1]
    load_count = load_velocity.shape[0]
    panels_total = pan_dev * owners
    own_variants = lax.dynamic_slice_in_dim(
        variant_order, phase_index * variant_dev, variant_dev, 0
    )
    picker = (
        own_variants[:, None] == jnp.arange(variant_order.shape[0], dtype=jnp.int32)[None, :]
    ).astype(jnp.float32)
    chosen = jnp.einsum("mv,vac->mac", picker, morph_weights, precision=HIGH)
    distance = (
        (control_points[0][:, None] - base_points[0][None, :]) ** 2
        + (control_points[1][:, None] - base_points[1][None, :]) ** 2
        + (control_points[2][:, None] - base_points[2][None, :]) ** 2
    )
    basis_values = lax.rsqrt(1.0 + distance)
    moved_points = base_points[None] + jnp.einsum(
        "mac,cn->man", chosen, basis_values, precision=HIGH
    )
    local_corners = connectivity - owner_index * vert_dev
    centroid, area, weight = panel_shape(moved_points, local_corners)
    hull_mask = (1 - free_flags).astype(jnp.float32)
    boundary = (
        jnp.einsum("ka,man->mkn", load_velocity, area, precision=HIGH) * hull_mask[None, None, :]
    )
    first_strengths = boundary.astype(jnp.bfloat16)
    kernel_scale = 1.0 / (4.0 * math.pi * math.sqrt(panels_total))
    own_geometry = jnp.concatenate([centroid, weight[:, None, :]], axis=1)
    sources = lax.all_gather(own_geometry, "panels", axis=2, tiled=True)
    row_targets = lax.all_gather(centroid, "cols", axis=2, tiled=True)

    def apply_influence(strengths):
        empty_sum = jnp.zeros((variant_dev, load_count, row_targets.shape[2]), jnp.float32)
        partial_sums = tile_product(
            empty_sum,
            row_targets,
            sources,
            lax.all_gather(strengths, "panels", axis=2, tiled=True),
            kernel_scale,
        )
        return lax.psum_scatter(partial_sums, "cols", scatter_dimension=2, tiled=True)

    induced = apply_influence(first_strengths)
    second_strengths = (first_strengths.astype(jnp.float32) + (boundary - induced)).astype(
        jnp.bfloat16
    )
    pressure = apply_influence(second_strengths)
    panel_force = pressure * (area[:, 2, :] * hull_mask[None, :])[:, None, :]
    force_rows = panel_force.reshape(-1, pan_dev)
    capacity = max(2, 5 * pan_dev // (2 * owners))
    target_owner = station_owner[:, 0]
    panel_order = jnp.arange(pan_dev, dtype=jnp.int32)
    ahead = (target_owner[:, None] == target_owner[None, :]) & (
        panel_order[None, :] < panel_order[:, None]
    )
    slot_rank = jnp.sum(ahead.astype(jnp.int32), axis=1)
    slot_index = target_owner * capacity + slot_rank
    all_slots = jnp.arange(owners * capacity, dtype=jnp.int32)
    placed = slot_index[:, None] == all_slots[None, :]
    send_values = jnp.dot(force_rows, placed.astype(jnp.float32), precision=HIGH)
    station_bins = (owner_index * pan_dev + panel_order) % STATIONS
    send_bins = jnp.max(jnp.where(placed, station_bins[:, None], -1), axis=0)[None, :]
    recv_values, recv_bins = (
        lax.all_to_all(send_values, ("panels", "cols"), split_axis=1, concat_axis=1, tiled=True),
        lax.all_to_all(send_bins, ("panels", "cols"), split_axis=1, concat_axis=1, tiled=True),
    )
    matches = (recv_bins[0][:, None] == jnp.arange(STATIONS, dtype=jnp.int32)[None, :]).astype(
        jnp.float32
    )
    station_loads = jnp.dot(recv_values, matches, precision=HIGH)
    station_place = (owner_index * STATIONS + jnp.arange(STATIONS, dtype=jnp.int32)).astype(
        jnp.float32
    ) / (STATIONS * owners)
    placed_loads = station_loads * station_place[None, :]
    own_total = jnp.sum(station_loads, axis=1)
    own_arm = jnp.sum(placed_loads, axis=1)
    zero_row = jnp.zeros_like(own_total)
    prior_total, prior_arm = prefix(
        (own_total, own_arm), ("panels", "cols"), add_pairs, (zero_row, zero_row)
    )
    station_rank = jnp.arange(STATIONS, dtype=jnp.int32)
    inclusive = (station_rank[:, None] <= station_rank[None, :]).astype(jnp.float32)
    strict = (station_rank[:, None] < station_rank[None, :]).astype(jnp.float32)
    running = prior_total[:, None] + jnp.dot(station_loads, inclusive, precision=HIGH)
    earlier = prior_total[:, None] + jnp.dot(station_loads, strict, precision=HIGH)
    moment_arm = prior_arm[:, None] + jnp.dot(placed_loads, strict, precision=HIGH)
    inv_root = 1.0 / math.sqrt(panels_total)
    shear = (running * inv_root).reshape(variant_dev, load_count, STATIONS)
    moment = ((station_place[None, :] * earlier - moment_arm) * inv_root).reshape(
        variant_dev, load_count, STATIONS
    )
    return (shear, moment)


def geometry_kernel(
    vert_dev,
    phases,
    order_hbm,
    base_hbm,
    control_hbm,
    weights_hbm,
    corner_hbm,
    flags_hbm,
    owner_hbm,
    out_hbm,
    order_ref,
    base_ref,
    control_ref,
    weights_ref,
    corner_ref,
    flags_ref,
    owner_ref,
    out_ref,
    arrived,
):
    @pl.when(lax.axis_index("phase") == 0)
    def _():
        sources = (
            base_hbm,
            control_hbm,
            weights_hbm,
            order_hbm,
            corner_hbm,
            flags_hbm,
            owner_hbm,
        )
        places = (
            base_ref,
            control_ref,
            weights_ref,
            order_ref,
            corner_ref,
            flags_ref,
            owner_ref,
        )
        copies = [
            pltpu.make_async_copy(source, place, arrived.at[k])
            for k, (source, place) in enumerate(zip(sources, places))
        ]
        for copy in copies:
            copy.start()
        for copy in copies:
            copy.wait()
        panel_rows(
            vert_dev,
            phases,
            order_ref,
            base_ref,
            control_ref,
            weights_ref,
            corner_ref,
            flags_ref,
            owner_ref,
            out_ref,
        )
        copy = pltpu.make_async_copy(out_ref, out_hbm, arrived.at[0])
        copy.start()
        copy.wait()


def panel_rows(
    vert_dev,
    phases,
    order_ref,
    base_ref,
    control_ref,
    weights_ref,
    corner_ref,
    flags_ref,
    owner_ref,
    out_ref,
):
    pan_dev = corner_ref.shape[1]
    diagonal = lax.broadcasted_iota(jnp.int32, (vert_dev, vert_dev), 0) == lax.broadcasted_iota(
        jnp.int32, (vert_dev, vert_dev), 1
    )
    base = [
        jnp.sum(jnp.where(diagonal, base_ref[a : a + 1, :], 0.0), axis=1, keepdims=True)
        for a in range(3)
    ]
    totals = [
        [jnp.zeros((vert_dev, LANES), jnp.float32) for _ in range(3)] for _ in range(phases)
    ]
    for start in range(0, control_ref.shape[1], LANES):
        part = pl.ds(start, LANES)
        distance = (
            (control_ref[0:1, part] - base[0]) ** 2
            + (control_ref[1:2, part] - base[1]) ** 2
            + (control_ref[2:3, part] - base[2]) ** 2
        )
        basis = lax.rsqrt(1.0 + distance)
        for slot in range(phases):
            for a in range(3):
                weights = weights_ref[a, 0:1, part]
                for v in range(1, weights_ref.shape[1]):
                    weights = jnp.where(
                        order_ref[slot] == v, weights_ref[a, v : v + 1, part], weights
                    )
                totals[slot][a] = totals[slot][a] + weights * basis
    vertex = lax.broadcasted_iota(jnp.int32, (vert_dev, pan_dev), 0)
    chosen = [vertex == lax.rem(corner_ref[k : k + 1, :], vert_dev) for k in range(3)]
    hull = (1 - flags_ref[...]).astype(jnp.float32)
    owner = owner_ref[...].astype(jnp.float32)
    targets = out_ref.shape[0]
    for slot in range(phases):
        moved = [base[a] + jnp.sum(totals[slot][a], axis=1, keepdims=True) for a in range(3)]
        first, second, third = [
            [
                jnp.sum(jnp.where(chosen[k], moved[a], 0.0), axis=0, keepdims=True)
                for a in range(3)
            ]
            for k in range(3)
        ]
        centroid = [(first[a] + second[a] + third[a]) * (1.0 / 3.0) for a in range(3)]
        one = [second[a] - first[a] for a in range(3)]
        two = [third[a] - first[a] for a in range(3)]
        area = [
            0.5 * (one[1] * two[2] - one[2] * two[1]),
            0.5 * (one[2] * two[0] - one[0] * two[2]),
            0.5 * (one[0] * two[1] - one[1] * two[0]),
        ]
        rows = jnp.concatenate(centroid + area + [hull, owner], axis=0)
        rows = jnp.concatenate([rows] * (LANES // pan_dev), axis=1)
        last = lax.broadcasted_iota(jnp.int32, rows.shape, 0) == rows.shape[0] - 1
        for target in range(targets // phases):
            out_ref[targets - 1 - target * phases - slot] = jnp.where(
                last, rows - float(target), rows
            )


def loads_kernel(
    pan_dev, phases, kernel_scale, rows_ref, velocity_ref, shear_ref, moment_ref, influence
):
    members = rows_ref.shape[0]
    owners = members // phases
    shared = LANES // pan_dev
    tiles = owners // shared
    panels_total = owners * pan_dev
    load_count = velocity_ref.shape[0]
    lane = lax.broadcasted_iota(jnp.int32, (8, LANES), 1)
    panels, columns = [], []
    for q in range(tiles):
        tile = rows_ref[members - 1 - q * shared * phases]
        for h in range(1, shared):
            tile = jnp.where(lane >= h * pan_dev, rows_ref[members - 1 - (q * shared + h) * phases], tile)
        panels.append(tile)
        area = [tile[3 + a : 4 + a, :] for a in range(3)]
        weight = jnp.sqrt(area[0] * area[0] + area[1] * area[1] + area[2] * area[2] + SKIN_SQUARE)
        columns.append(
            jnp.concatenate([tile[0:3, :], weight * kernel_scale, tile[4:8, :]], axis=0).T
        )
    for source in range(tiles):
        column = columns[source]
        centre = [column[:, a : a + 1] for a in range(3)]
        weight = column[:, 3:4]
        for target in range(tiles):
            tile = panels[target]
            distance = (
                (tile[0:1, :] - centre[0]) ** 2
                + (tile[1:2, :] - centre[1]) ** 2
                + (tile[2:3, :] - centre[2]) ** 2
            )
            influence[pl.ds(source * LANES, LANES), pl.ds(target * LANES, LANES)] = (
                weight * lax.rsqrt(distance + CORE_SQUARE)
            ).astype(jnp.bfloat16)
    velocity = [velocity_ref[:, a : a + 1] for a in range(3)]
    boundary = jnp.concatenate(
        [
            (velocity[0] * tile[3:4, :] + velocity[1] * tile[4:5, :] + velocity[2] * tile[5:6, :])
            * tile[6:7, :]
            for tile in panels
        ],
        axis=1,
    )
    first = boundary.astype(jnp.bfloat16)
    induced = jnp.dot(first, influence[...], preferred_element_type=jnp.float32)
    second = (first.astype(jnp.float32) + (boundary - induced)).astype(jnp.bfloat16)
    pressure = jnp.dot(second, influence[...], preferred_element_type=jnp.float32)

    stations_all = STATIONS * owners
    own_loads = jnp.zeros((load_count, LANES), jnp.float32)
    prior_loads = jnp.zeros((load_count, LANES), jnp.float32)
    prior_arms = jnp.zeros((load_count, LANES), jnp.float32)
    rank = lax.broadcasted_iota(jnp.int32, (1, LANES), 1).astype(jnp.float32)
    for q, tile in enumerate(panels):
        force = pressure[:, q * LANES : (q + 1) * LANES] * (tile[5:6, :] * tile[6:7, :])
        owner = tile[7:8, :]
        prior = owner < 0.0
        place = (owner * STATIONS + rank) * (1.0 / stations_all)
        own_loads = own_loads + jnp.where(owner == 0.0, force, 0.0)
        prior_loads = prior_loads + jnp.where(prior, force, 0.0)
        prior_arms = prior_arms + force * jnp.where(prior, place, 0.0)
    prior_total = jnp.sum(prior_loads, axis=1, keepdims=True)
    prior_arm = jnp.sum(prior_arms, axis=1, keepdims=True)
    station = lax.broadcasted_iota(jnp.int32, (STATIONS, 2 * STATIONS), 0)
    place = lax.broadcasted_iota(jnp.int32, (STATIONS, 2 * STATIONS), 1)
    arm = place - STATIONS - station
    steps = jnp.where(
        place < STATIONS, (station <= place).astype(jnp.int32), jnp.maximum(arm, 0)
    ).astype(jnp.float32).astype(jnp.bfloat16)
    high = own_loads.astype(jnp.bfloat16)
    rest = own_loads - high.astype(jnp.float32)
    middle = rest.astype(jnp.bfloat16)
    low = (rest - middle.astype(jnp.float32)).astype(jnp.bfloat16)
    sums = jnp.dot(
        jnp.concatenate([high, middle, low], axis=0), steps, preferred_element_type=jnp.float32
    )
    sums = sums[:load_count] + (sums[load_count : 2 * load_count] + sums[2 * load_count :])
    inv_root = 1.0 / math.sqrt(panels_total)
    shear_ref[0] = (prior_total + sums[:, :STATIONS]) * inv_root
    moment_ref[0] = (
        (rank * (1.0 / stations_all)) * prior_total
        - prior_arm
        + sums[:, STATIONS:] * (1.0 / stations_all)
    ) * inv_root


def shards_whole(
    base_points,
    control_points,
    morph_weights,
    connectivity,
    free_flags,
    station_owner,
    variant_order,
    load_velocity,
):
    owners = lax.axis_size(("panels", "cols"))
    vert_dev = base_points.shape[1]
    pan_dev = connectivity.shape[1]
    load_count = load_velocity.shape[0]
    panels_total = pan_dev * owners
    phases = lax.axis_size("phase")
    members = owners * phases
    variants = morph_weights.shape[0]
    control = control_points.shape[1]
    vmem = pl.BlockSpec(memory_space=pltpu.VMEM)
    anywhere = pl.BlockSpec(memory_space=pl.ANY)
    rows = pl.pallas_call(
        functools.partial(geometry_kernel, vert_dev, phases),
        out_shape=jax.ShapeDtypeStruct((members, 8, LANES), jnp.float32),
        in_specs=[anywhere] * 7,
        out_specs=anywhere,
        scratch_shapes=[
            pltpu.SMEM((variants,), jnp.int32),
            pltpu.VMEM((3, vert_dev), jnp.float32),
            pltpu.VMEM((3, control), jnp.float32),
            pltpu.VMEM((3, variants, control), jnp.float32),
            pltpu.VMEM((3, pan_dev), jnp.int32),
            pltpu.VMEM((1, pan_dev), jnp.int32),
            pltpu.VMEM((1, pan_dev), jnp.int32),
            pltpu.VMEM((members, 8, LANES), jnp.float32),
            pltpu.SemaphoreType.DMA((7,)),
        ],
        name="geometry",
    )(
        variant_order,
        base_points,
        control_points,
        morph_weights.transpose(1, 0, 2),
        connectivity,
        free_flags.reshape(1, pan_dev),
        station_owner.reshape(1, pan_dev),
    )
    order = list(range(members))[::-1]
    rows = lax.all_to_all(
        rows, ("panels", "cols", "phase"), split_axis=0, concat_axis=0, axis_index_groups=[order]
    )
    kernel_scale = 1.0 / (4.0 * math.pi * math.sqrt(panels_total))
    out = jax.ShapeDtypeStruct((1, load_count, STATIONS), jnp.float32)
    return pl.pallas_call(
        functools.partial(loads_kernel, pan_dev, phases, kernel_scale),
        out_shape=(out, out),
        in_specs=[vmem] * 2,
        out_specs=(vmem, vmem),
        scratch_shapes=[pltpu.VMEM((panels_total, panels_total), jnp.bfloat16)],
        compiler_params=pltpu.CompilerParams(vmem_limit_bytes=32 * 1024 * 1024),
        name="loads",
    )(rows, load_velocity)


def shards(
    base_points,
    control_points,
    morph_weights,
    connectivity,
    free_flags,
    station_owner,
    variant_order,
    load_velocity,
):
    owners = lax.axis_size(("panels", "cols"))
    pan_dev = connectivity.shape[1]
    panels_total = owners * pan_dev
    whole = (
        panels_total <= PANELS_ON_ONE
        and panels_total % LANES == 0
        and LANES % pan_dev == 0
        and STATIONS == LANES
        and variant_order.shape[0] == lax.axis_size("phase")
        and control_points.shape[1] % LANES == 0
        and load_velocity.shape[0] % 16 == 0
    )
    return (shards_whole if whole else shards_split)(
        base_points,
        control_points,
        morph_weights,
        connectivity,
        free_flags,
        station_owner,
        variant_order,
        load_velocity,
    )


def solution(mesh):
    return jax.shard_map(
        shards,
        mesh=mesh,
        in_specs=(
            P(None, ("groups", "panels", "cols")),
            P(),
            P("groups", None, None),
            P(None, ("groups", "panels", "cols")),
            P(("groups", "panels", "cols")),
            P(("groups", "panels", "cols"), None),
            P("groups"),
            P(),
        ),
        out_specs=(
            P(("groups", "phase"), None, ("panels", "cols")),
            P(("groups", "phase"), None, ("panels", "cols")),
        ),
        check_vma=False,
    )
```

```python
import functools
import math

import jax
import jax.numpy as jnp
from jax import lax
from jax.experimental import pallas as pl
from jax.experimental.pallas import tpu as pltpu
from jax.sharding import PartitionSpec as P

STATIONS = 128
LANES = 128
PANELS_ON_ONE = 1024


HIGH = lax.Precision.HIGHEST
CORE_SQUARE = 0.0025
SKIN_SQUARE = 0.01


def prefix(shard, axis, combine, identity):
    length, index = (lax.axis_size(axis), lax.axis_index(axis))
    everything = jax.tree.map(lambda part: lax.all_gather(part, axis), shard)
    start = jax.tree.map(
        lambda part, zero: jnp.broadcast_to(jnp.asarray(zero, part.dtype), part.shape),
        shard,
        identity,
    )

    def step(k, before):
        reached = k < index
        new = combine(before, jax.tree.map(lambda part: part[k], everything))
        return jax.tree.map(lambda a, b: jnp.where(reached, a, b), new, before)

    return lax.fori_loop(0, length, step, start)


def panel_shape(moved_points, corner_rows):
    first_corner = jnp.take(moved_points, corner_rows[0], axis=2)
    second_corner = jnp.take(moved_points, corner_rows[1], axis=2)
    third_corner = jnp.take(moved_points, corner_rows[2], axis=2)
    centroid = (first_corner + second_corner + third_corner) / 3.0
    edge_one = second_corner - first_corner
    edge_two = third_corner - first_corner
    cross_x = edge_one[:, 1] * edge_two[:, 2] - edge_one[:, 2] * edge_two[:, 1]
    cross_y = edge_one[:, 2] * edge_two[:, 0] - edge_one[:, 0] * edge_two[:, 2]
    cross_z = edge_one[:, 0] * edge_two[:, 1] - edge_one[:, 1] * edge_two[:, 0]
    area = 0.5 * jnp.stack([cross_x, cross_y, cross_z], axis=1)
    weight = jnp.sqrt(jnp.sum(area * area, axis=1) + SKIN_SQUARE)
    return (centroid, area, weight)


def tile_block(targets, sources, strengths, kernel_scale):
    distance = (
        (targets[:, 0, :, None] - sources[:, 0, None, :]) ** 2
        + (targets[:, 1, :, None] - sources[:, 1, None, :]) ** 2
        + (targets[:, 2, :, None] - sources[:, 2, None, :]) ** 2
    )
    influence = (sources[:, 3, None, :] * kernel_scale * lax.rsqrt(distance + CORE_SQUARE)).astype(
        jnp.bfloat16
    )
    return jnp.einsum("mrn,mkn->mkr", influence, strengths, preferred_element_type=jnp.float32)


def tile_product(carry_sum, targets, sources, strengths, kernel_scale):
    columns = strengths.shape[2]
    block_width = columns
    for candidate in (2048, 1024, 512):
        if columns > candidate and columns % candidate == 0:
            block_width = candidate
            break
    if block_width == columns:
        return carry_sum + tile_block(targets, sources, strengths, kernel_scale)

    def block_step(step_index, running_sum):
        column_start = step_index * block_width
        part_sources = lax.dynamic_slice_in_dim(sources, column_start, block_width, 2)
        part_strengths = lax.dynamic_slice_in_dim(strengths, column_start, block_width, 2)
        return running_sum + tile_block(targets, part_sources, part_strengths, kernel_scale)

    return lax.fori_loop(0, columns // block_width, block_step, carry_sum)


def add_pairs(earlier, later):
    return (earlier[0] + later[0], earlier[1] + later[1])


def shards_split(
    base_points,
    control_points,
    morph_weights,
    connectivity,
    free_flags,
    station_owner,
    variant_order,
    load_velocity,
):
    owners = lax.axis_size(("panels", "cols"))
    owner_index = lax.axis_index(("panels", "cols"))
    phase_index = lax.axis_index("phase")
    variant_dev = variant_order.shape[0] // lax.axis_size("phase")
    vert_dev = base_points.shape[1]
    pan_dev = connectivity.shape[1]
    load_count = load_velocity.shape[0]
    panels_total = pan_dev * owners
    own_variants = lax.dynamic_slice_in_dim(
        variant_order, phase_index * variant_dev, variant_dev, 0
    )
    picker = (
        own_variants[:, None] == jnp.arange(variant_order.shape[0], dtype=jnp.int32)[None, :]
    ).astype(jnp.float32)
    chosen = jnp.einsum("mv,vac->mac", picker, morph_weights, precision=HIGH)
    distance = (
        (control_points[0][:, None] - base_points[0][None, :]) ** 2
        + (control_points[1][:, None] - base_points[1][None, :]) ** 2
        + (control_points[2][:, None] - base_points[2][None, :]) ** 2
    )
    basis_values = lax.rsqrt(1.0 + distance)
    moved_points = base_points[None] + jnp.einsum(
        "mac,cn->man", chosen, basis_values, precision=HIGH
    )
    local_corners = connectivity - owner_index * vert_dev
    centroid, area, weight = panel_shape(moved_points, local_corners)
    hull_mask = (1 - free_flags).astype(jnp.float32)
    boundary = (
        jnp.einsum("ka,man->mkn", load_velocity, area, precision=HIGH) * hull_mask[None, None, :]
    )
    first_strengths = boundary.astype(jnp.bfloat16)
    kernel_scale = 1.0 / (4.0 * math.pi * math.sqrt(panels_total))
    own_geometry = jnp.concatenate([centroid, weight[:, None, :]], axis=1)
    sources = lax.all_gather(own_geometry, "panels", axis=2, tiled=True)
    row_targets = lax.all_gather(centroid, "cols", axis=2, tiled=True)

    def apply_influence(strengths):
        empty_sum = jnp.zeros((variant_dev, load_count, row_targets.shape[2]), jnp.float32)
        partial_sums = tile_product(
            empty_sum,
            row_targets,
            sources,
            lax.all_gather(strengths, "panels", axis=2, tiled=True),
            kernel_scale,
        )
        return lax.psum_scatter(partial_sums, "cols", scatter_dimension=2, tiled=True)

    induced = apply_influence(first_strengths)
    second_strengths = (first_strengths.astype(jnp.float32) + (boundary - induced)).astype(
        jnp.bfloat16
    )
    pressure = apply_influence(second_strengths)
    panel_force = pressure * (area[:, 2, :] * hull_mask[None, :])[:, None, :]
    force_rows = panel_force.reshape(-1, pan_dev)
    capacity = max(2, 5 * pan_dev // (2 * owners))
    target_owner = station_owner[:, 0]
    panel_order = jnp.arange(pan_dev, dtype=jnp.int32)
    ahead = (target_owner[:, None] == target_owner[None, :]) & (
        panel_order[None, :] < panel_order[:, None]
    )
    slot_rank = jnp.sum(ahead.astype(jnp.int32), axis=1)
    slot_index = target_owner * capacity + slot_rank
    all_slots = jnp.arange(owners * capacity, dtype=jnp.int32)
    placed = slot_index[:, None] == all_slots[None, :]
    send_values = jnp.dot(force_rows, placed.astype(jnp.float32), precision=HIGH)
    station_bins = (owner_index * pan_dev + panel_order) % STATIONS
    send_bins = jnp.max(jnp.where(placed, station_bins[:, None], -1), axis=0)[None, :]
    recv_values, recv_bins = (
        lax.all_to_all(send_values, ("panels", "cols"), split_axis=1, concat_axis=1, tiled=True),
        lax.all_to_all(send_bins, ("panels", "cols"), split_axis=1, concat_axis=1, tiled=True),
    )
    matches = (recv_bins[0][:, None] == jnp.arange(STATIONS, dtype=jnp.int32)[None, :]).astype(
        jnp.float32
    )
    station_loads = jnp.dot(recv_values, matches, precision=HIGH)
    station_place = (owner_index * STATIONS + jnp.arange(STATIONS, dtype=jnp.int32)).astype(
        jnp.float32
    ) / (STATIONS * owners)
    placed_loads = station_loads * station_place[None, :]
    own_total = jnp.sum(station_loads, axis=1)
    own_arm = jnp.sum(placed_loads, axis=1)
    zero_row = jnp.zeros_like(own_total)
    prior_total, prior_arm = prefix(
        (own_total, own_arm), ("panels", "cols"), add_pairs, (zero_row, zero_row)
    )
    station_rank = jnp.arange(STATIONS, dtype=jnp.int32)
    inclusive = (station_rank[:, None] <= station_rank[None, :]).astype(jnp.float32)
    strict = (station_rank[:, None] < station_rank[None, :]).astype(jnp.float32)
    running = prior_total[:, None] + jnp.dot(station_loads, inclusive, precision=HIGH)
    earlier = prior_total[:, None] + jnp.dot(station_loads, strict, precision=HIGH)
    moment_arm = prior_arm[:, None] + jnp.dot(placed_loads, strict, precision=HIGH)
    inv_root = 1.0 / math.sqrt(panels_total)
    shear = (running * inv_root).reshape(variant_dev, load_count, STATIONS)
    moment = ((station_place[None, :] * earlier - moment_arm) * inv_root).reshape(
        variant_dev, load_count, STATIONS
    )
    return (shear, moment)


def geometry_kernel(
    vert_dev,
    phases,
    order_hbm,
    base_hbm,
    control_hbm,
    weights_hbm,
    corner_hbm,
    flags_hbm,
    owner_hbm,
    out_hbm,
    order_ref,
    base_ref,
    control_ref,
    weights_ref,
    corner_ref,
    flags_ref,
    owner_ref,
    out_ref,
    arrived,
):
    @pl.when(lax.axis_index("phase") == phases - 1)
    def _():
        sources = (
            base_hbm,
            control_hbm,
            weights_hbm,
            order_hbm,
            corner_hbm,
            flags_hbm,
            owner_hbm,
        )
        places = (
            base_ref,
            control_ref,
            weights_ref,
            order_ref,
            corner_ref,
            flags_ref,
            owner_ref,
        )
        copies = [
            pltpu.make_async_copy(source, place, arrived.at[k])
            for k, (source, place) in enumerate(zip(sources, places))
        ]
        for copy in copies:
            copy.start()
        for copy in copies:
            copy.wait()
        panel_rows(
            vert_dev,
            phases,
            order_ref,
            base_ref,
            control_ref,
            weights_ref,
            corner_ref,
            flags_ref,
            owner_ref,
            out_ref,
        )
        copy = pltpu.make_async_copy(out_ref, out_hbm, arrived.at[0])
        copy.start()
        copy.wait()


def panel_rows(
    vert_dev,
    phases,
    order_ref,
    base_ref,
    control_ref,
    weights_ref,
    corner_ref,
    flags_ref,
    owner_ref,
    out_ref,
):
    pan_dev = corner_ref.shape[1]
    diagonal = lax.broadcasted_iota(jnp.int32, (vert_dev, vert_dev), 0) == lax.broadcasted_iota(
        jnp.int32, (vert_dev, vert_dev), 1
    )
    base = [
        jnp.sum(jnp.where(diagonal, base_ref[a : a + 1, :], 0.0), axis=1, keepdims=True)
        for a in range(3)
    ]
    totals = [
        [jnp.zeros((vert_dev, LANES), jnp.float32) for _ in range(3)] for _ in range(phases)
    ]
    for start in range(0, control_ref.shape[1], LANES):
        part = pl.ds(start, LANES)
        distance = (
            (control_ref[0:1, part] - base[0]) ** 2
            + (control_ref[1:2, part] - base[1]) ** 2
            + (control_ref[2:3, part] - base[2]) ** 2
        )
        basis = lax.rsqrt(1.0 + distance)
        for slot in range(phases):
            for a in range(3):
                weights = weights_ref[a, 0:1, part]
                for v in range(1, weights_ref.shape[1]):
                    weights = jnp.where(
                        order_ref[slot] == v, weights_ref[a, v : v + 1, part], weights
                    )
                totals[slot][a] = totals[slot][a] + weights * basis
    vertex = lax.broadcasted_iota(jnp.int32, (vert_dev, pan_dev), 0)
    chosen = [vertex == lax.rem(corner_ref[k : k + 1, :], vert_dev) for k in range(3)]
    hull = (1 - flags_ref[...]).astype(jnp.float32)
    owner = owner_ref[...].astype(jnp.float32)
    targets = out_ref.shape[0]
    for slot in range(phases):
        moved = [base[a] + jnp.sum(totals[slot][a], axis=1, keepdims=True) for a in range(3)]
        first, second, third = [
            [
                jnp.sum(jnp.where(chosen[k], moved[a], 0.0), axis=0, keepdims=True)
                for a in range(3)
            ]
            for k in range(3)
        ]
        centroid = [(first[a] + second[a] + third[a]) * (1.0 / 3.0) for a in range(3)]
        one = [second[a] - first[a] for a in range(3)]
        two = [third[a] - first[a] for a in range(3)]
        area = [
            0.5 * (one[1] * two[2] - one[2] * two[1]),
            0.5 * (one[2] * two[0] - one[0] * two[2]),
            0.5 * (one[0] * two[1] - one[1] * two[0]),
        ]
        rows = centroid + area + [hull, owner]
        height = out_ref.shape[1]
        rows = jnp.concatenate(
            [jnp.concatenate(rows[k : k + height], axis=0) for k in range(0, len(rows), height)],
            axis=1,
        )
        last = (lax.broadcasted_iota(jnp.int32, rows.shape, 0) == height - 1) & (
            lax.broadcasted_iota(jnp.int32, rows.shape, 1) >= LANES - pan_dev
        )
        for target in range(targets // phases):
            out_ref[targets - (target + 1) * phases + slot] = jnp.where(
                last, rows - float(target), rows
            )


def loads_kernel(
    pan_dev, phases, kernel_scale, rows_ref, velocity_ref, shear_ref, moment_ref, influence
):
    members = rows_ref.shape[0]
    owners = members // phases
    shared = LANES // pan_dev
    tiles = owners // shared
    panels_total = owners * pan_dev
    load_count = velocity_ref.shape[0]
    height = rows_ref.shape[1]
    lane = lax.broadcasted_iota(jnp.int32, (height, LANES), 1)
    panels, columns = [], []
    for q in range(tiles):
        blocks = [rows_ref[members - 1 - (q * shared + h) * phases] for h in range(shared)]
        pieces = []
        for k in range(shared):
            piece = None
            for h, block in enumerate(blocks):
                moved = block if h == k else pltpu.roll(block, (h - k) % shared * pan_dev, 1)
                piece = moved if h == 0 else jnp.where(lane >= h * pan_dev, moved, piece)
            pieces.append(piece)
        tile = jnp.concatenate(pieces, axis=0)
        panels.append(tile)
        area = [tile[3 + a : 4 + a, :] for a in range(3)]
        weight = jnp.sqrt(area[0] * area[0] + area[1] * area[1] + area[2] * area[2] + SKIN_SQUARE)
        columns.append(
            jnp.concatenate([tile[0:3, :], weight * kernel_scale, tile[4:8, :]], axis=0).T
        )
    for source in range(tiles):
        column = columns[source]
        centre = [column[:, a : a + 1] for a in range(3)]
        weight = column[:, 3:4]
        for target in range(tiles):
            tile = panels[target]
            distance = (
                (tile[0:1, :] - centre[0]) ** 2
                + (tile[1:2, :] - centre[1]) ** 2
                + (tile[2:3, :] - centre[2]) ** 2
            )
            influence[pl.ds(source * LANES, LANES), pl.ds(target * LANES, LANES)] = (
                weight * lax.rsqrt(distance + CORE_SQUARE)
            ).astype(jnp.bfloat16)
    velocity = [velocity_ref[:, a : a + 1] for a in range(3)]
    boundary = jnp.concatenate(
        [
            (velocity[0] * tile[3:4, :] + velocity[1] * tile[4:5, :] + velocity[2] * tile[5:6, :])
            * tile[6:7, :]
            for tile in panels
        ],
        axis=1,
    )
    first = boundary.astype(jnp.bfloat16)
    induced = jnp.dot(first, influence[...], preferred_element_type=jnp.float32)
    second = (first.astype(jnp.float32) + (boundary - induced)).astype(jnp.bfloat16)
    pressure = jnp.dot(second, influence[...], preferred_element_type=jnp.float32)

    stations_all = STATIONS * owners
    own_loads = jnp.zeros((load_count, LANES), jnp.float32)
    prior_loads = jnp.zeros((load_count, LANES), jnp.float32)
    prior_arms = jnp.zeros((load_count, LANES), jnp.float32)
    rank = lax.broadcasted_iota(jnp.int32, (1, LANES), 1).astype(jnp.float32)
    for q, tile in enumerate(panels):
        force = pressure[:, q * LANES : (q + 1) * LANES] * (tile[5:6, :] * tile[6:7, :])
        owner = tile[7:8, :]
        prior = owner < 0.0
        place = (owner * STATIONS + rank) * (1.0 / stations_all)
        own_loads = own_loads + jnp.where(owner == 0.0, force, 0.0)
        prior_loads = prior_loads + jnp.where(prior, force, 0.0)
        prior_arms = prior_arms + force * jnp.where(prior, place, 0.0)
    prior_total = jnp.sum(prior_loads, axis=1, keepdims=True)
    prior_arm = jnp.sum(prior_arms, axis=1, keepdims=True)
    station = lax.broadcasted_iota(jnp.int32, (STATIONS, 2 * STATIONS), 0)
    place = lax.broadcasted_iota(jnp.int32, (STATIONS, 2 * STATIONS), 1)
    arm = place - STATIONS - station
    steps = jnp.where(
        place < STATIONS, (station <= place).astype(jnp.int32), jnp.maximum(arm, 0)
    ).astype(jnp.float32).astype(jnp.bfloat16)
    high = own_loads.astype(jnp.bfloat16)
    rest = own_loads - high.astype(jnp.float32)
    middle = rest.astype(jnp.bfloat16)
    low = (rest - middle.astype(jnp.float32)).astype(jnp.bfloat16)
    sums = jnp.dot(
        jnp.concatenate([high, middle, low], axis=0), steps, preferred_element_type=jnp.float32
    )
    sums = sums[:load_count] + (sums[load_count : 2 * load_count] + sums[2 * load_count :])
    inv_root = 1.0 / math.sqrt(panels_total)
    shear_ref[0] = (prior_total + sums[:, :STATIONS]) * inv_root
    moment_ref[0] = (
        (rank * (1.0 / stations_all)) * prior_total
        - prior_arm
        + sums[:, STATIONS:] * (1.0 / stations_all)
    ) * inv_root


def shards_whole(
    base_points,
    control_points,
    morph_weights,
    connectivity,
    free_flags,
    station_owner,
    variant_order,
    load_velocity,
):
    owners = lax.axis_size(("panels", "cols"))
    vert_dev = base_points.shape[1]
    pan_dev = connectivity.shape[1]
    load_count = load_velocity.shape[0]
    panels_total = pan_dev * owners
    phases = lax.axis_size("phase")
    members = owners * phases
    variants = morph_weights.shape[0]
    control = control_points.shape[1]
    height = 8 * pan_dev // LANES
    vmem = pl.BlockSpec(memory_space=pltpu.VMEM)
    anywhere = pl.BlockSpec(memory_space=pl.ANY)
    rows = pl.pallas_call(
        functools.partial(geometry_kernel, vert_dev, phases),
        out_shape=jax.ShapeDtypeStruct((members, height, LANES), jnp.float32),
        in_specs=[anywhere] * 7,
        out_specs=anywhere,
        scratch_shapes=[
            pltpu.SMEM((variants,), jnp.int32),
            pltpu.VMEM((3, vert_dev), jnp.float32),
            pltpu.VMEM((3, control), jnp.float32),
            pltpu.VMEM((3, variants, control), jnp.float32),
            pltpu.VMEM((3, pan_dev), jnp.int32),
            pltpu.VMEM((1, pan_dev), jnp.int32),
            pltpu.VMEM((1, pan_dev), jnp.int32),
            pltpu.VMEM((members, height, LANES), jnp.float32),
            pltpu.SemaphoreType.DMA((7,)),
        ],
        name="geometry",
    )(
        variant_order,
        base_points,
        control_points,
        morph_weights.transpose(1, 0, 2),
        connectivity,
        free_flags.reshape(1, pan_dev),
        station_owner.reshape(1, pan_dev),
    )
    order = [owner * phases + k for owner in range(owners)[::-1] for k in range(phases)]
    rows = lax.all_to_all(
        rows, ("panels", "cols", "phase"), split_axis=0, concat_axis=0, axis_index_groups=[order]
    )
    kernel_scale = 1.0 / (4.0 * math.pi * math.sqrt(panels_total))
    out = jax.ShapeDtypeStruct((1, load_count, STATIONS), jnp.float32)
    return pl.pallas_call(
        functools.partial(loads_kernel, pan_dev, phases, kernel_scale),
        out_shape=(out, out),
        in_specs=[vmem] * 2,
        out_specs=(vmem, vmem),
        scratch_shapes=[pltpu.VMEM((panels_total, panels_total), jnp.bfloat16)],
        compiler_params=pltpu.CompilerParams(vmem_limit_bytes=32 * 1024 * 1024),
        name="loads",
    )(rows, load_velocity)


def shards(
    base_points,
    control_points,
    morph_weights,
    connectivity,
    free_flags,
    station_owner,
    variant_order,
    load_velocity,
):
    owners = lax.axis_size(("panels", "cols"))
    pan_dev = connectivity.shape[1]
    panels_total = owners * pan_dev
    whole = (
        panels_total <= PANELS_ON_ONE
        and panels_total % LANES == 0
        and LANES % pan_dev == 0
        and 8 * pan_dev % LANES == 0
        and STATIONS == LANES
        and variant_order.shape[0] == lax.axis_size("phase")
        and control_points.shape[1] % LANES == 0
        and load_velocity.shape[0] % 16 == 0
    )
    return (shards_whole if whole else shards_split)(
        base_points,
        control_points,
        morph_weights,
        connectivity,
        free_flags,
        station_owner,
        variant_order,
        load_velocity,
    )


def solution(mesh):
    return jax.shard_map(
        shards,
        mesh=mesh,
        in_specs=(
            P(None, ("groups", "panels", "cols")),
            P(),
            P("groups", None, None),
            P(None, ("groups", "panels", "cols")),
            P(("groups", "panels", "cols")),
            P(("groups", "panels", "cols"), None),
            P("groups"),
            P(),
        ),
        out_specs=(
            P(("groups", "phase"), None, ("panels", "cols")),
            P(("groups", "phase"), None, ("panels", "cols")),
        ),
        check_vma=False,
    )
```

```python
import functools
import math

import jax
import jax.numpy as jnp
from jax import lax
from jax.experimental import pallas as pl
from jax.experimental.pallas import tpu as pltpu
from jax.sharding import PartitionSpec as P

STATIONS = 128
LANES = 128
PANELS_ON_ONE = 1024


HIGH = lax.Precision.HIGHEST
CORE_SQUARE = 0.0025
SKIN_SQUARE = 0.01


def prefix(shard, axis, combine, identity):
    length, index = (lax.axis_size(axis), lax.axis_index(axis))
    everything = jax.tree.map(lambda part: lax.all_gather(part, axis), shard)
    start = jax.tree.map(
        lambda part, zero: jnp.broadcast_to(jnp.asarray(zero, part.dtype), part.shape),
        shard,
        identity,
    )

    def step(k, before):
        reached = k < index
        new = combine(before, jax.tree.map(lambda part: part[k], everything))
        return jax.tree.map(lambda a, b: jnp.where(reached, a, b), new, before)

    return lax.fori_loop(0, length, step, start)


def panel_shape(moved_points, corner_rows):
    first_corner = jnp.take(moved_points, corner_rows[0], axis=2)
    second_corner = jnp.take(moved_points, corner_rows[1], axis=2)
    third_corner = jnp.take(moved_points, corner_rows[2], axis=2)
    centroid = (first_corner + second_corner + third_corner) / 3.0
    edge_one = second_corner - first_corner
    edge_two = third_corner - first_corner
    cross_x = edge_one[:, 1] * edge_two[:, 2] - edge_one[:, 2] * edge_two[:, 1]
    cross_y = edge_one[:, 2] * edge_two[:, 0] - edge_one[:, 0] * edge_two[:, 2]
    cross_z = edge_one[:, 0] * edge_two[:, 1] - edge_one[:, 1] * edge_two[:, 0]
    area = 0.5 * jnp.stack([cross_x, cross_y, cross_z], axis=1)
    weight = jnp.sqrt(jnp.sum(area * area, axis=1) + SKIN_SQUARE)
    return (centroid, area, weight)


def tile_block(targets, sources, strengths, kernel_scale):
    distance = (
        (targets[:, 0, :, None] - sources[:, 0, None, :]) ** 2
        + (targets[:, 1, :, None] - sources[:, 1, None, :]) ** 2
        + (targets[:, 2, :, None] - sources[:, 2, None, :]) ** 2
    )
    influence = (sources[:, 3, None, :] * kernel_scale * lax.rsqrt(distance + CORE_SQUARE)).astype(
        jnp.bfloat16
    )
    return jnp.einsum("mrn,mkn->mkr", influence, strengths, preferred_element_type=jnp.float32)


def tile_product(carry_sum, targets, sources, strengths, kernel_scale):
    columns = strengths.shape[2]
    block_width = columns
    for candidate in (2048, 1024, 512):
        if columns > candidate and columns % candidate == 0:
            block_width = candidate
            break
    if block_width == columns:
        return carry_sum + tile_block(targets, sources, strengths, kernel_scale)

    def block_step(step_index, running_sum):
        column_start = step_index * block_width
        part_sources = lax.dynamic_slice_in_dim(sources, column_start, block_width, 2)
        part_strengths = lax.dynamic_slice_in_dim(strengths, column_start, block_width, 2)
        return running_sum + tile_block(targets, part_sources, part_strengths, kernel_scale)

    return lax.fori_loop(0, columns // block_width, block_step, carry_sum)


def add_pairs(earlier, later):
    return (earlier[0] + later[0], earlier[1] + later[1])


def shards_split(
    base_points,
    control_points,
    morph_weights,
    connectivity,
    free_flags,
    station_owner,
    variant_order,
    load_velocity,
):
    owners = lax.axis_size(("panels", "cols"))
    owner_index = lax.axis_index(("panels", "cols"))
    phase_index = lax.axis_index("phase")
    variant_dev = variant_order.shape[0] // lax.axis_size("phase")
    vert_dev = base_points.shape[1]
    pan_dev = connectivity.shape[1]
    load_count = load_velocity.shape[0]
    panels_total = pan_dev * owners
    own_variants = lax.dynamic_slice_in_dim(
        variant_order, phase_index * variant_dev, variant_dev, 0
    )
    picker = (
        own_variants[:, None] == jnp.arange(variant_order.shape[0], dtype=jnp.int32)[None, :]
    ).astype(jnp.float32)
    chosen = jnp.einsum("mv,vac->mac", picker, morph_weights, precision=HIGH)
    distance = (
        (control_points[0][:, None] - base_points[0][None, :]) ** 2
        + (control_points[1][:, None] - base_points[1][None, :]) ** 2
        + (control_points[2][:, None] - base_points[2][None, :]) ** 2
    )
    basis_values = lax.rsqrt(1.0 + distance)
    moved_points = base_points[None] + jnp.einsum(
        "mac,cn->man", chosen, basis_values, precision=HIGH
    )
    local_corners = connectivity - owner_index * vert_dev
    centroid, area, weight = panel_shape(moved_points, local_corners)
    hull_mask = (1 - free_flags).astype(jnp.float32)
    boundary = (
        jnp.einsum("ka,man->mkn", load_velocity, area, precision=HIGH) * hull_mask[None, None, :]
    )
    first_strengths = boundary.astype(jnp.bfloat16)
    kernel_scale = 1.0 / (4.0 * math.pi * math.sqrt(panels_total))
    own_geometry = jnp.concatenate([centroid, weight[:, None, :]], axis=1)
    sources = lax.all_gather(own_geometry, "panels", axis=2, tiled=True)
    row_targets = lax.all_gather(centroid, "cols", axis=2, tiled=True)

    def apply_influence(strengths):
        empty_sum = jnp.zeros((variant_dev, load_count, row_targets.shape[2]), jnp.float32)
        partial_sums = tile_product(
            empty_sum,
            row_targets,
            sources,
            lax.all_gather(strengths, "panels", axis=2, tiled=True),
            kernel_scale,
        )
        return lax.psum_scatter(partial_sums, "cols", scatter_dimension=2, tiled=True)

    induced = apply_influence(first_strengths)
    second_strengths = (first_strengths.astype(jnp.float32) + (boundary - induced)).astype(
        jnp.bfloat16
    )
    pressure = apply_influence(second_strengths)
    panel_force = pressure * (area[:, 2, :] * hull_mask[None, :])[:, None, :]
    force_rows = panel_force.reshape(-1, pan_dev)
    capacity = max(2, 5 * pan_dev // (2 * owners))
    target_owner = station_owner[:, 0]
    panel_order = jnp.arange(pan_dev, dtype=jnp.int32)
    ahead = (target_owner[:, None] == target_owner[None, :]) & (
        panel_order[None, :] < panel_order[:, None]
    )
    slot_rank = jnp.sum(ahead.astype(jnp.int32), axis=1)
    slot_index = target_owner * capacity + slot_rank
    all_slots = jnp.arange(owners * capacity, dtype=jnp.int32)
    placed = slot_index[:, None] == all_slots[None, :]
    send_values = jnp.dot(force_rows, placed.astype(jnp.float32), precision=HIGH)
    station_bins = (owner_index * pan_dev + panel_order) % STATIONS
    send_bins = jnp.max(jnp.where(placed, station_bins[:, None], -1), axis=0)[None, :]
    recv_values, recv_bins = (
        lax.all_to_all(send_values, ("panels", "cols"), split_axis=1, concat_axis=1, tiled=True),
        lax.all_to_all(send_bins, ("panels", "cols"), split_axis=1, concat_axis=1, tiled=True),
    )
    matches = (recv_bins[0][:, None] == jnp.arange(STATIONS, dtype=jnp.int32)[None, :]).astype(
        jnp.float32
    )
    station_loads = jnp.dot(recv_values, matches, precision=HIGH)
    station_place = (owner_index * STATIONS + jnp.arange(STATIONS, dtype=jnp.int32)).astype(
        jnp.float32
    ) / (STATIONS * owners)
    placed_loads = station_loads * station_place[None, :]
    own_total = jnp.sum(station_loads, axis=1)
    own_arm = jnp.sum(placed_loads, axis=1)
    zero_row = jnp.zeros_like(own_total)
    prior_total, prior_arm = prefix(
        (own_total, own_arm), ("panels", "cols"), add_pairs, (zero_row, zero_row)
    )
    station_rank = jnp.arange(STATIONS, dtype=jnp.int32)
    inclusive = (station_rank[:, None] <= station_rank[None, :]).astype(jnp.float32)
    strict = (station_rank[:, None] < station_rank[None, :]).astype(jnp.float32)
    running = prior_total[:, None] + jnp.dot(station_loads, inclusive, precision=HIGH)
    earlier = prior_total[:, None] + jnp.dot(station_loads, strict, precision=HIGH)
    moment_arm = prior_arm[:, None] + jnp.dot(placed_loads, strict, precision=HIGH)
    inv_root = 1.0 / math.sqrt(panels_total)
    shear = (running * inv_root).reshape(variant_dev, load_count, STATIONS)
    moment = ((station_place[None, :] * earlier - moment_arm) * inv_root).reshape(
        variant_dev, load_count, STATIONS
    )
    return (shear, moment)


def geometry_kernel(
    vert_dev,
    phases,
    order_hbm,
    base_hbm,
    control_hbm,
    weights_hbm,
    corner_hbm,
    flags_hbm,
    owner_hbm,
    out_ref,
    order_ref,
    base_ref,
    control_ref,
    weights_ref,
    corner_ref,
    flags_ref,
    owner_ref,
    arrived,
):
    @pl.when(lax.axis_index("phase") == phases - 1)
    def _():
        sources = (
            base_hbm,
            control_hbm,
            weights_hbm,
            order_hbm,
            corner_hbm,
            flags_hbm,
            owner_hbm,
        )
        places = (
            base_ref,
            control_ref,
            weights_ref,
            order_ref,
            corner_ref,
            flags_ref,
            owner_ref,
        )
        copies = [
            pltpu.make_async_copy(source, place, arrived.at[k])
            for k, (source, place) in enumerate(zip(sources, places))
        ]
        for copy in copies:
            copy.start()
        for copy in copies:
            copy.wait()
        panel_rows(
            vert_dev,
            phases,
            order_ref,
            base_ref,
            control_ref,
            weights_ref,
            corner_ref,
            flags_ref,
            owner_ref,
            out_ref,
        )


def panel_rows(
    vert_dev,
    phases,
    order_ref,
    base_ref,
    control_ref,
    weights_ref,
    corner_ref,
    flags_ref,
    owner_ref,
    out_ref,
):
    pan_dev = corner_ref.shape[1]
    diagonal = lax.broadcasted_iota(jnp.int32, (vert_dev, vert_dev), 0) == lax.broadcasted_iota(
        jnp.int32, (vert_dev, vert_dev), 1
    )
    base = [
        jnp.sum(jnp.where(diagonal, base_ref[a : a + 1, :], 0.0), axis=1, keepdims=True)
        for a in range(3)
    ]
    totals = [
        [jnp.zeros((vert_dev, LANES), jnp.float32) for _ in range(3)] for _ in range(phases)
    ]
    for start in range(0, control_ref.shape[1], LANES):
        part = pl.ds(start, LANES)
        distance = (
            (control_ref[0:1, part] - base[0]) ** 2
            + (control_ref[1:2, part] - base[1]) ** 2
            + (control_ref[2:3, part] - base[2]) ** 2
        )
        basis = lax.rsqrt(1.0 + distance)
        for slot in range(phases):
            for a in range(3):
                weights = weights_ref[a, 0:1, part]
                for v in range(1, weights_ref.shape[1]):
                    weights = jnp.where(
                        order_ref[slot] == v, weights_ref[a, v : v + 1, part], weights
                    )
                totals[slot][a] = totals[slot][a] + weights * basis
    vertex = lax.broadcasted_iota(jnp.int32, (vert_dev, pan_dev), 0)
    chosen = [vertex == lax.rem(corner_ref[k : k + 1, :], vert_dev) for k in range(3)]
    hull = (1 - flags_ref[...]).astype(jnp.float32)
    owner = owner_ref[...].astype(jnp.float32)
    targets = out_ref.shape[0]
    for slot in range(phases):
        moved = [base[a] + jnp.sum(totals[slot][a], axis=1, keepdims=True) for a in range(3)]
        first, second, third = [
            [
                jnp.sum(jnp.where(chosen[k], moved[a], 0.0), axis=0, keepdims=True)
                for a in range(3)
            ]
            for k in range(3)
        ]
        centroid = [(first[a] + second[a] + third[a]) * (1.0 / 3.0) for a in range(3)]
        one = [second[a] - first[a] for a in range(3)]
        two = [third[a] - first[a] for a in range(3)]
        area = [
            0.5 * (one[1] * two[2] - one[2] * two[1]),
            0.5 * (one[2] * two[0] - one[0] * two[2]),
            0.5 * (one[0] * two[1] - one[1] * two[0]),
        ]
        rows = centroid + area + [hull, owner]
        height = out_ref.shape[1]
        rows = jnp.concatenate(
            [jnp.concatenate(rows[k : k + height], axis=0) for k in range(0, len(rows), height)],
            axis=1,
        )
        last = (lax.broadcasted_iota(jnp.int32, rows.shape, 0) == height - 1) & (
            lax.broadcasted_iota(jnp.int32, rows.shape, 1) >= LANES - pan_dev
        )
        for target in range(targets // phases):
            out_ref[targets - (target + 1) * phases + slot] = jnp.where(
                last, rows - float(target), rows
            )


def loads_kernel(
    pan_dev, phases, kernel_scale, rows_ref, velocity_ref, shear_ref, moment_ref, influence
):
    members = rows_ref.shape[0]
    owners = members // phases
    shared = LANES // pan_dev
    tiles = owners // shared
    panels_total = owners * pan_dev
    load_count = velocity_ref.shape[1]
    height = rows_ref.shape[1]
    lane = lax.broadcasted_iota(jnp.int32, (height, LANES), 1)
    panels, columns = [], []
    for q in range(tiles):
        blocks = [rows_ref[members - 1 - (q * shared + h) * phases] for h in range(shared)]
        pieces = []
        for k in range(shared):
            piece = None
            for h, block in enumerate(blocks):
                moved = block if h == k else pltpu.roll(block, (h - k) % shared * pan_dev, 1)
                piece = moved if h == 0 else jnp.where(lane >= h * pan_dev, moved, piece)
            pieces.append(piece)
        tile = jnp.concatenate(pieces, axis=0)
        panels.append(tile)
        area = [tile[3 + a : 4 + a, :] for a in range(3)]
        weight = jnp.sqrt(area[0] * area[0] + area[1] * area[1] + area[2] * area[2] + SKIN_SQUARE)
        columns.append(
            jnp.concatenate([tile[0:3, :], weight * kernel_scale, tile[4:8, :]], axis=0).T
        )
    for source in range(tiles):
        column = columns[source]
        centre = [column[:, a : a + 1] for a in range(3)]
        weight = column[:, 3:4]
        for target in range(tiles):
            tile = panels[target]
            distance = (
                (tile[0:1, :] - centre[0]) ** 2
                + (tile[1:2, :] - centre[1]) ** 2
                + (tile[2:3, :] - centre[2]) ** 2
            )
            influence[pl.ds(source * LANES, LANES), pl.ds(target * LANES, LANES)] = (
                weight * lax.rsqrt(distance + CORE_SQUARE)
            ).astype(jnp.bfloat16)
    velocity = jnp.concatenate(
        [velocity_ref[...], jnp.zeros((8 - velocity_ref.shape[0], load_count), jnp.float32)], axis=0
    ).T
    velocity = [velocity[:, a : a + 1] for a in range(3)]
    boundary = jnp.concatenate(
        [
            (velocity[0] * tile[3:4, :] + velocity[1] * tile[4:5, :] + velocity[2] * tile[5:6, :])
            * tile[6:7, :]
            for tile in panels
        ],
        axis=1,
    )
    first = boundary.astype(jnp.bfloat16)
    induced = jnp.dot(first, influence[...], preferred_element_type=jnp.float32)
    second = (first.astype(jnp.float32) + (boundary - induced)).astype(jnp.bfloat16)
    pressure = jnp.dot(second, influence[...], preferred_element_type=jnp.float32)

    stations_all = STATIONS * owners
    own_loads = jnp.zeros((load_count, LANES), jnp.float32)
    prior_loads = jnp.zeros((load_count, LANES), jnp.float32)
    prior_arms = jnp.zeros((load_count, LANES), jnp.float32)
    rank = lax.broadcasted_iota(jnp.int32, (1, LANES), 1).astype(jnp.float32)
    for q, tile in enumerate(panels):
        force = pressure[:, q * LANES : (q + 1) * LANES] * (tile[5:6, :] * tile[6:7, :])
        owner = tile[7:8, :]
        prior = owner < 0.0
        place = (owner * STATIONS + rank) * (1.0 / stations_all)
        own_loads = own_loads + jnp.where(owner == 0.0, force, 0.0)
        prior_loads = prior_loads + jnp.where(prior, force, 0.0)
        prior_arms = prior_arms + force * jnp.where(prior, place, 0.0)
    prior_total = jnp.sum(prior_loads, axis=1, keepdims=True)
    prior_arm = jnp.sum(prior_arms, axis=1, keepdims=True)
    station = lax.broadcasted_iota(jnp.int32, (STATIONS, 2 * STATIONS), 0)
    place = lax.broadcasted_iota(jnp.int32, (STATIONS, 2 * STATIONS), 1)
    arm = place - STATIONS - station
    steps = jnp.where(
        place < STATIONS, (station <= place).astype(jnp.int32), jnp.maximum(arm, 0)
    ).astype(jnp.float32).astype(jnp.bfloat16)
    high = own_loads.astype(jnp.bfloat16)
    rest = own_loads - high.astype(jnp.float32)
    middle = rest.astype(jnp.bfloat16)
    low = (rest - middle.astype(jnp.float32)).astype(jnp.bfloat16)
    sums = jnp.dot(
        jnp.concatenate([high, middle, low], axis=0), steps, preferred_element_type=jnp.float32
    )
    sums = sums[:load_count] + (sums[load_count : 2 * load_count] + sums[2 * load_count :])
    inv_root = 1.0 / math.sqrt(panels_total)
    shear_ref[0] = (prior_total + sums[:, :STATIONS]) * inv_root
    moment_ref[0] = (
        (rank * (1.0 / stations_all)) * prior_total
        - prior_arm
        + sums[:, STATIONS:] * (1.0 / stations_all)
    ) * inv_root


def shards_whole(
    base_points,
    control_points,
    morph_weights,
    connectivity,
    free_flags,
    station_owner,
    variant_order,
    load_velocity,
):
    owners = lax.axis_size(("panels", "cols"))
    vert_dev = base_points.shape[1]
    pan_dev = connectivity.shape[1]
    load_count = load_velocity.shape[0]
    panels_total = pan_dev * owners
    phases = lax.axis_size("phase")
    members = owners * phases
    variants = morph_weights.shape[0]
    control = control_points.shape[1]
    height = 8 * pan_dev // LANES
    vmem = pl.BlockSpec(memory_space=pltpu.VMEM)
    anywhere = pl.BlockSpec(memory_space=pl.ANY)
    rows = pl.pallas_call(
        functools.partial(geometry_kernel, vert_dev, phases),
        out_shape=pltpu.VMEM((members, height, LANES), jnp.float32),
        in_specs=[anywhere] * 7,
        out_specs=vmem,
        scratch_shapes=[
            pltpu.SMEM((variants,), jnp.int32),
            pltpu.VMEM((3, vert_dev), jnp.float32),
            pltpu.VMEM((3, control), jnp.float32),
            pltpu.VMEM((3, variants, control), jnp.float32),
            pltpu.VMEM((3, pan_dev), jnp.int32),
            pltpu.VMEM((1, pan_dev), jnp.int32),
            pltpu.VMEM((1, pan_dev), jnp.int32),
            pltpu.SemaphoreType.DMA((7,)),
        ],
        name="geometry",
    )(
        variant_order,
        base_points,
        control_points,
        morph_weights.transpose(1, 0, 2),
        connectivity,
        free_flags.reshape(1, pan_dev),
        station_owner.reshape(1, pan_dev),
    )
    order = [owner * phases + k for owner in range(owners)[::-1] for k in range(phases)]
    rows = lax.all_to_all(
        rows, ("panels", "cols", "phase"), split_axis=0, concat_axis=0, axis_index_groups=[order]
    )
    kernel_scale = 1.0 / (4.0 * math.pi * math.sqrt(panels_total))
    out = jax.ShapeDtypeStruct((1, load_count, STATIONS), jnp.float32)
    return pl.pallas_call(
        functools.partial(loads_kernel, pan_dev, phases, kernel_scale),
        out_shape=(out, out),
        in_specs=[vmem] * 2,
        out_specs=(vmem, vmem),
        scratch_shapes=[pltpu.VMEM((panels_total, panels_total), jnp.bfloat16)],
        compiler_params=pltpu.CompilerParams(vmem_limit_bytes=32 * 1024 * 1024),
        name="loads",
    )(rows, load_velocity.T)


def shards(
    base_points,
    control_points,
    morph_weights,
    connectivity,
    free_flags,
    station_owner,
    variant_order,
    load_velocity,
):
    owners = lax.axis_size(("panels", "cols"))
    pan_dev = connectivity.shape[1]
    panels_total = owners * pan_dev
    whole = (
        panels_total <= PANELS_ON_ONE
        and panels_total % LANES == 0
        and LANES % pan_dev == 0
        and 8 * pan_dev % LANES == 0
        and STATIONS == LANES
        and variant_order.shape[0] == lax.axis_size("phase")
        and control_points.shape[1] % LANES == 0
        and load_velocity.shape[0] % 16 == 0
    )
    return (shards_whole if whole else shards_split)(
        base_points,
        control_points,
        morph_weights,
        connectivity,
        free_flags,
        station_owner,
        variant_order,
        load_velocity,
    )


def solution(mesh):
    return jax.shard_map(
        shards,
        mesh=mesh,
        in_specs=(
            P(None, ("groups", "panels", "cols")),
            P(),
            P("groups", None, None),
            P(None, ("groups", "panels", "cols")),
            P(("groups", "panels", "cols")),
            P(("groups", "panels", "cols"), None),
            P("groups"),
            P(),
        ),
        out_specs=(
            P(("groups", "phase"), None, ("panels", "cols")),
            P(("groups", "phase"), None, ("panels", "cols")),
        ),
        check_vma=False,
    )
```

```python
import functools
import math

import jax
import jax.numpy as jnp
import numpy as np
from jax import lax
from jax.experimental import pallas as pl
from jax.experimental.pallas import tpu as pltpu
from jax.sharding import PartitionSpec as P

STATIONS = 128
LANES = 128
PANELS_ON_ONE = 1024


HIGH = lax.Precision.HIGHEST
CORE_SQUARE = 0.0025
SKIN_SQUARE = 0.01


def prefix(shard, axis, combine, identity):
    length, index = (lax.axis_size(axis), lax.axis_index(axis))
    everything = jax.tree.map(lambda part: lax.all_gather(part, axis), shard)
    start = jax.tree.map(
        lambda part, zero: jnp.broadcast_to(jnp.asarray(zero, part.dtype), part.shape),
        shard,
        identity,
    )

    def step(k, before):
        reached = k < index
        new = combine(before, jax.tree.map(lambda part: part[k], everything))
        return jax.tree.map(lambda a, b: jnp.where(reached, a, b), new, before)

    return lax.fori_loop(0, length, step, start)


def panel_shape(moved_points, corner_rows):
    first_corner = jnp.take(moved_points, corner_rows[0], axis=2)
    second_corner = jnp.take(moved_points, corner_rows[1], axis=2)
    third_corner = jnp.take(moved_points, corner_rows[2], axis=2)
    centroid = (first_corner + second_corner + third_corner) / 3.0
    edge_one = second_corner - first_corner
    edge_two = third_corner - first_corner
    cross_x = edge_one[:, 1] * edge_two[:, 2] - edge_one[:, 2] * edge_two[:, 1]
    cross_y = edge_one[:, 2] * edge_two[:, 0] - edge_one[:, 0] * edge_two[:, 2]
    cross_z = edge_one[:, 0] * edge_two[:, 1] - edge_one[:, 1] * edge_two[:, 0]
    area = 0.5 * jnp.stack([cross_x, cross_y, cross_z], axis=1)
    weight = jnp.sqrt(jnp.sum(area * area, axis=1) + SKIN_SQUARE)
    return (centroid, area, weight)


def tile_block(targets, sources, strengths, kernel_scale):
    distance = (
        (targets[:, 0, :, None] - sources[:, 0, None, :]) ** 2
        + (targets[:, 1, :, None] - sources[:, 1, None, :]) ** 2
        + (targets[:, 2, :, None] - sources[:, 2, None, :]) ** 2
    )
    influence = (sources[:, 3, None, :] * kernel_scale * lax.rsqrt(distance + CORE_SQUARE)).astype(
        jnp.bfloat16
    )
    return jnp.einsum("mrn,mkn->mkr", influence, strengths, preferred_element_type=jnp.float32)


def tile_product(carry_sum, targets, sources, strengths, kernel_scale):
    columns = strengths.shape[2]
    block_width = columns
    for candidate in (2048, 1024, 512):
        if columns > candidate and columns % candidate == 0:
            block_width = candidate
            break
    if block_width == columns:
        return carry_sum + tile_block(targets, sources, strengths, kernel_scale)

    def block_step(step_index, running_sum):
        column_start = step_index * block_width
        part_sources = lax.dynamic_slice_in_dim(sources, column_start, block_width, 2)
        part_strengths = lax.dynamic_slice_in_dim(strengths, column_start, block_width, 2)
        return running_sum + tile_block(targets, part_sources, part_strengths, kernel_scale)

    return lax.fori_loop(0, columns // block_width, block_step, carry_sum)


def add_pairs(earlier, later):
    return (earlier[0] + later[0], earlier[1] + later[1])


def shards_split(
    base_points,
    control_points,
    morph_weights,
    connectivity,
    free_flags,
    station_owner,
    variant_order,
    load_velocity,
):
    owners = lax.axis_size(("panels", "cols"))
    owner_index = lax.axis_index(("panels", "cols"))
    phase_index = lax.axis_index("phase")
    variant_dev = variant_order.shape[0] // lax.axis_size("phase")
    vert_dev = base_points.shape[1]
    pan_dev = connectivity.shape[1]
    load_count = load_velocity.shape[0]
    panels_total = pan_dev * owners
    own_variants = lax.dynamic_slice_in_dim(
        variant_order, phase_index * variant_dev, variant_dev, 0
    )
    picker = (
        own_variants[:, None] == jnp.arange(variant_order.shape[0], dtype=jnp.int32)[None, :]
    ).astype(jnp.float32)
    chosen = jnp.einsum("mv,vac->mac", picker, morph_weights, precision=HIGH)
    distance = (
        (control_points[0][:, None] - base_points[0][None, :]) ** 2
        + (control_points[1][:, None] - base_points[1][None, :]) ** 2
        + (control_points[2][:, None] - base_points[2][None, :]) ** 2
    )
    basis_values = lax.rsqrt(1.0 + distance)
    moved_points = base_points[None] + jnp.einsum(
        "mac,cn->man", chosen, basis_values, precision=HIGH
    )
    local_corners = connectivity - owner_index * vert_dev
    centroid, area, weight = panel_shape(moved_points, local_corners)
    hull_mask = (1 - free_flags).astype(jnp.float32)
    boundary = (
        jnp.einsum("ka,man->mkn", load_velocity, area, precision=HIGH) * hull_mask[None, None, :]
    )
    first_strengths = boundary.astype(jnp.bfloat16)
    kernel_scale = 1.0 / (4.0 * math.pi * math.sqrt(panels_total))
    own_geometry = jnp.concatenate([centroid, weight[:, None, :]], axis=1)
    sources = lax.all_gather(own_geometry, "panels", axis=2, tiled=True)
    row_targets = lax.all_gather(centroid, "cols", axis=2, tiled=True)

    def apply_influence(strengths):
        empty_sum = jnp.zeros((variant_dev, load_count, row_targets.shape[2]), jnp.float32)
        partial_sums = tile_product(
            empty_sum,
            row_targets,
            sources,
            lax.all_gather(strengths, "panels", axis=2, tiled=True),
            kernel_scale,
        )
        return lax.psum_scatter(partial_sums, "cols", scatter_dimension=2, tiled=True)

    induced = apply_influence(first_strengths)
    second_strengths = (first_strengths.astype(jnp.float32) + (boundary - induced)).astype(
        jnp.bfloat16
    )
    pressure = apply_influence(second_strengths)
    panel_force = pressure * (area[:, 2, :] * hull_mask[None, :])[:, None, :]
    force_rows = panel_force.reshape(-1, pan_dev)
    capacity = max(2, 5 * pan_dev // (2 * owners))
    target_owner = station_owner[:, 0]
    panel_order = jnp.arange(pan_dev, dtype=jnp.int32)
    ahead = (target_owner[:, None] == target_owner[None, :]) & (
        panel_order[None, :] < panel_order[:, None]
    )
    slot_rank = jnp.sum(ahead.astype(jnp.int32), axis=1)
    slot_index = target_owner * capacity + slot_rank
    all_slots = jnp.arange(owners * capacity, dtype=jnp.int32)
    placed = slot_index[:, None] == all_slots[None, :]
    send_values = jnp.dot(force_rows, placed.astype(jnp.float32), precision=HIGH)
    station_bins = (owner_index * pan_dev + panel_order) % STATIONS
    send_bins = jnp.max(jnp.where(placed, station_bins[:, None], -1), axis=0)[None, :]
    recv_values, recv_bins = (
        lax.all_to_all(send_values, ("panels", "cols"), split_axis=1, concat_axis=1, tiled=True),
        lax.all_to_all(send_bins, ("panels", "cols"), split_axis=1, concat_axis=1, tiled=True),
    )
    matches = (recv_bins[0][:, None] == jnp.arange(STATIONS, dtype=jnp.int32)[None, :]).astype(
        jnp.float32
    )
    station_loads = jnp.dot(recv_values, matches, precision=HIGH)
    station_place = (owner_index * STATIONS + jnp.arange(STATIONS, dtype=jnp.int32)).astype(
        jnp.float32
    ) / (STATIONS * owners)
    placed_loads = station_loads * station_place[None, :]
    own_total = jnp.sum(station_loads, axis=1)
    own_arm = jnp.sum(placed_loads, axis=1)
    zero_row = jnp.zeros_like(own_total)
    prior_total, prior_arm = prefix(
        (own_total, own_arm), ("panels", "cols"), add_pairs, (zero_row, zero_row)
    )
    station_rank = jnp.arange(STATIONS, dtype=jnp.int32)
    inclusive = (station_rank[:, None] <= station_rank[None, :]).astype(jnp.float32)
    strict = (station_rank[:, None] < station_rank[None, :]).astype(jnp.float32)
    running = prior_total[:, None] + jnp.dot(station_loads, inclusive, precision=HIGH)
    earlier = prior_total[:, None] + jnp.dot(station_loads, strict, precision=HIGH)
    moment_arm = prior_arm[:, None] + jnp.dot(placed_loads, strict, precision=HIGH)
    inv_root = 1.0 / math.sqrt(panels_total)
    shear = (running * inv_root).reshape(variant_dev, load_count, STATIONS)
    moment = ((station_place[None, :] * earlier - moment_arm) * inv_root).reshape(
        variant_dev, load_count, STATIONS
    )
    return (shear, moment)


def geometry_kernel(
    vert_dev,
    phases,
    order,
    order_hbm,
    base_hbm,
    control_hbm,
    weights_hbm,
    corner_hbm,
    flags_hbm,
    owner_hbm,
    out_ref,
    order_ref,
    base_ref,
    control_ref,
    weights_ref,
    corner_ref,
    flags_ref,
    owner_ref,
    arrived,
):
    @pl.when(lax.axis_index("phase") == phases - 1)
    def _():
        sources = (
            weights_hbm,
            control_hbm,
            base_hbm,
            corner_hbm,
            flags_hbm,
            owner_hbm,
            order_hbm,
        )
        places = (
            weights_ref,
            control_ref,
            base_ref,
            corner_ref,
            flags_ref,
            owner_ref,
            order_ref,
        )
        copies = [
            pltpu.make_async_copy(source, place, arrived.at[k])
            for k, (source, place) in enumerate(zip(sources, places))
        ]
        for copy in copies:
            copy.start()
        for copy in copies:
            copy.wait()
        panel_rows(
            vert_dev,
            phases,
            order,
            order_ref,
            base_ref,
            control_ref,
            weights_ref,
            corner_ref,
            flags_ref,
            owner_ref,
            out_ref,
        )


def panel_rows(
    vert_dev,
    phases,
    order,
    order_ref,
    base_ref,
    control_ref,
    weights_ref,
    corner_ref,
    flags_ref,
    owner_ref,
    out_ref,
):
    pan_dev = corner_ref.shape[1]
    variants = weights_ref.shape[1]
    diagonal = lax.broadcasted_iota(jnp.int32, (vert_dev, vert_dev), 0) == lax.broadcasted_iota(
        jnp.int32, (vert_dev, vert_dev), 1
    )
    base = [
        jnp.sum(jnp.where(diagonal, base_ref[a : a + 1, :], 0.0), axis=1, keepdims=True)
        for a in range(3)
    ]
    totals = [[None] * 3 for _ in range(variants)]
    for start in range(0, control_ref.shape[1], LANES):
        part = pl.ds(start, LANES)
        distance = (
            (control_ref[0:1, part] - base[0]) ** 2
            + (control_ref[1:2, part] - base[1]) ** 2
            + (control_ref[2:3, part] - base[2]) ** 2
        )
        basis = lax.rsqrt(1.0 + distance)
        for v in range(variants):
            for a in range(3):
                term = weights_ref[a, v : v + 1, part] * basis
                totals[v][a] = term if start == 0 else totals[v][a] + term
    lane = lax.broadcasted_iota(jnp.int32, (vert_dev, LANES), 1)
    moved = []
    for a in range(3):
        shift = jnp.sum(totals[0][a], axis=1, keepdims=True)
        for v in range(1, variants):
            own = jnp.sum(totals[v][a], axis=1, keepdims=True)
            shift = jnp.where(lane >= v * pan_dev, own, shift)
        moved.append(base[a] + shift)

    def repeated(row):
        return jnp.concatenate([row] * variants, axis=1)

    vertex = lax.broadcasted_iota(jnp.int32, (vert_dev, LANES), 0)
    corners = []
    for k in range(3):
        chosen = vertex == lax.rem(repeated(corner_ref[k : k + 1, :]), vert_dev)
        corners.append(
            [jnp.sum(jnp.where(chosen, moved[a], 0.0), axis=0, keepdims=True) for a in range(3)]
        )
    first, second, third = corners
    centroid = [(first[a] + second[a] + third[a]) * (1.0 / 3.0) for a in range(3)]
    one = [second[a] - first[a] for a in range(3)]
    two = [third[a] - first[a] for a in range(3)]
    area = [
        0.5 * (one[1] * two[2] - one[2] * two[1]),
        0.5 * (one[2] * two[0] - one[0] * two[2]),
        0.5 * (one[0] * two[1] - one[1] * two[0]),
    ]
    hull = (1 - repeated(flags_ref[...])).astype(jnp.float32)
    owner = repeated(owner_ref[...]).astype(jnp.float32)
    rows = centroid + area + [hull, owner]
    height = out_ref.shape[1]
    shared = LANES // pan_dev
    pieces = [jnp.concatenate(rows[k : k + height], axis=0) for k in range(0, len(rows), height)]
    lane = lax.broadcasted_iota(jnp.int32, (height, LANES), 1)
    last = (lax.broadcasted_iota(jnp.int32, (height, LANES), 0) == height - 1) & (
        lane >= LANES - pan_dev
    )
    blocks = []
    for v in range(variants):
        block = None
        for k, piece in enumerate(pieces):
            piece = piece if k == v else pltpu.roll(piece, (k - v) % shared * pan_dev, 1)
            block = piece if k == 0 else jnp.where(lane >= k * pan_dev, piece, block)
        blocks.append(block)
    for slot in range(phases):
        block = blocks[0]
        for v in range(1, variants):
            block = jnp.where(order_ref[slot] == v, blocks[v], block)
        for place, member in enumerate(order):
            if member % phases == slot:
                out_ref[place] = jnp.where(last, block - float(member // phases), block)


def in_parts(values):
    high = values.astype(jnp.bfloat16).astype(jnp.float32)
    rest = values - high
    middle = rest.astype(jnp.bfloat16).astype(jnp.float32)
    return high, middle, rest - middle


def dot_rows(left, right):
    return lax.dot_general(
        left.astype(jnp.bfloat16),
        right.astype(jnp.bfloat16),
        (((0,), (0,)), ((), ())),
        preferred_element_type=jnp.float32,
    )


def spread_matrix():
    spread = np.zeros((16, 4 * LANES), np.float32)
    for row in range(12):
        spread[row, row % 4 * LANES : (row % 4 + 1) * LANES] = 1.0
    return spread


def loads_kernel(
    pan_dev,
    places,
    kernel_scale,
    rows_ref,
    velocity_ref,
    spread_ref,
    shear_ref,
    moment_ref,
    influence,
):
    owners = len(places)
    shared = LANES // pan_dev
    tiles = owners // shared
    panels_total = owners * pan_dev
    load_count = velocity_ref.shape[1]
    height = rows_ref.shape[1]
    lane = lax.broadcasted_iota(jnp.int32, (height, LANES), 1)
    panels = []
    for q in range(tiles):
        blocks = [rows_ref[places[q * shared + h]] for h in range(shared)]
        pieces = []
        for k in range(shared):
            piece = None
            for h, block in enumerate(blocks):
                moved = block if h == k else pltpu.roll(block, (h - k) % shared * pan_dev, 1)
                piece = moved if h == 0 else jnp.where(lane >= h * pan_dev, moved, piece)
            pieces.append(piece)
        panels.append(jnp.concatenate(pieces, axis=0))
    rows = jnp.concatenate(panels, axis=1)
    centre = rows[0:3, :]
    area = rows[3:6, :]
    hull = rows[6:7, :]
    owner = rows[7:8, :]
    weight = (
        jnp.sqrt(
            area[0:1, :] * area[0:1, :]
            + area[1:2, :] * area[1:2, :]
            + area[2:3, :] * area[2:3, :]
            + SKIN_SQUARE
        )
        * kernel_scale
    )
    high, middle, low = in_parts(jnp.concatenate([centre, weight], axis=0))
    columns = dot_rows(
        jnp.concatenate([high, middle, low, jnp.zeros_like(low)], axis=0), spread_ref[...]
    )
    blank = jnp.zeros((1, panels_total), jnp.float32)
    area_parts = in_parts(jnp.concatenate([area, blank], axis=0))
    velocity_parts = in_parts(
        jnp.concatenate([velocity_ref[...], jnp.zeros((1, load_count), jnp.float32)], axis=0)
    )
    pairs = ((0, 0), (0, 1), (1, 0), (1, 1), (0, 2), (2, 0), (1, 2), (2, 1))
    boundary = (
        dot_rows(
            jnp.concatenate([velocity_parts[k] for k, _ in pairs], axis=0),
            jnp.concatenate([area_parts[k] for _, k in pairs], axis=0),
        )
        * hull
    )
    first = boundary.astype(jnp.bfloat16)
    for source in range(tiles):
        for target in range(source, tiles):
            tile = panels[target]
            column = columns[source * LANES : (source + 1) * LANES, :]
            column = [column[:, a * LANES : (a + 1) * LANES] for a in range(4)]
            inverse = lax.rsqrt(
                (tile[0:1, :] - column[0]) ** 2
                + (tile[1:2, :] - column[1]) ** 2
                + (tile[2:3, :] - column[2]) ** 2
                + CORE_SQUARE
            )
            here, there = pl.ds(source * LANES, LANES), pl.ds(target * LANES, LANES)
            influence[here, there] = (column[3] * inverse).astype(jnp.bfloat16)
            if target != source:
                other = columns[target * LANES : (target + 1) * LANES, 3 * LANES :]
                influence[there, here] = (other * inverse.T).astype(jnp.bfloat16)
    induced = jnp.dot(first, influence[...], preferred_element_type=jnp.float32)
    second = (first.astype(jnp.float32) + (boundary - induced)).astype(jnp.bfloat16)
    pressure = jnp.dot(second, influence[...], preferred_element_type=jnp.float32)
    stations_all = STATIONS * owners
    own_loads = jnp.zeros((load_count, LANES), jnp.float32)
    prior_loads = jnp.zeros((load_count, LANES), jnp.float32)
    prior_arms = jnp.zeros((load_count, LANES), jnp.float32)
    rank = lax.broadcasted_iota(jnp.int32, (1, LANES), 1).astype(jnp.float32)
    for q, tile in enumerate(panels):
        force = pressure[:, q * LANES : (q + 1) * LANES] * (tile[5:6, :] * tile[6:7, :])
        owner = tile[7:8, :]
        prior = owner < 0.0
        place = (owner * STATIONS + rank) * (1.0 / stations_all)
        own_loads = own_loads + jnp.where(owner == 0.0, force, 0.0)
        prior_loads = prior_loads + jnp.where(prior, force, 0.0)
        prior_arms = prior_arms + force * jnp.where(prior, place, 0.0)
    prior_total = jnp.sum(prior_loads, axis=1, keepdims=True)
    prior_arm = jnp.sum(prior_arms, axis=1, keepdims=True)
    station = lax.broadcasted_iota(jnp.int32, (STATIONS, 2 * STATIONS), 0)
    place = lax.broadcasted_iota(jnp.int32, (STATIONS, 2 * STATIONS), 1)
    arm = place - STATIONS - station
    steps = jnp.where(
        place < STATIONS, (station <= place).astype(jnp.int32), jnp.maximum(arm, 0)
    ).astype(jnp.float32).astype(jnp.bfloat16)
    high = own_loads.astype(jnp.bfloat16)
    rest = own_loads - high.astype(jnp.float32)
    middle = rest.astype(jnp.bfloat16)
    low = (rest - middle.astype(jnp.float32)).astype(jnp.bfloat16)
    sums = jnp.dot(
        jnp.concatenate([high, middle, low], axis=0), steps, preferred_element_type=jnp.float32
    )
    sums = sums[:load_count] + (sums[load_count : 2 * load_count] + sums[2 * load_count :])
    inv_root = 1.0 / math.sqrt(panels_total)
    shear_ref[0] = (prior_total + sums[:, :STATIONS]) * inv_root
    moment_ref[0] = (
        (rank * (1.0 / stations_all)) * prior_total
        - prior_arm
        + sums[:, STATIONS:] * (1.0 / stations_all)
    ) * inv_root


def shards_whole(
    base_points,
    control_points,
    morph_weights,
    connectivity,
    free_flags,
    station_owner,
    variant_order,
    load_velocity,
):
    owners = lax.axis_size(("panels", "cols"))
    vert_dev = base_points.shape[1]
    pan_dev = connectivity.shape[1]
    load_count = load_velocity.shape[0]
    panels_total = pan_dev * owners
    phases = lax.axis_size("phase")
    members = owners * phases
    variants = morph_weights.shape[0]
    control = control_points.shape[1]
    height = 8 * pan_dev // LANES
    order = [owner * phases + k for owner in range(owners)[::-1] for k in range(phases)]
    vmem = pl.BlockSpec(memory_space=pltpu.VMEM)
    anywhere = pl.BlockSpec(memory_space=pl.ANY)
    rows = pl.pallas_call(
        functools.partial(geometry_kernel, vert_dev, phases, order),
        out_shape=pltpu.VMEM((members, height, LANES), jnp.float32),
        in_specs=[anywhere] * 7,
        out_specs=vmem,
        scratch_shapes=[
            pltpu.SMEM((variants,), jnp.int32),
            pltpu.VMEM((3, vert_dev), jnp.float32),
            pltpu.VMEM((3, control), jnp.float32),
            pltpu.VMEM((3, variants, control), jnp.float32),
            pltpu.VMEM((3, pan_dev), jnp.int32),
            pltpu.VMEM((1, pan_dev), jnp.int32),
            pltpu.VMEM((1, pan_dev), jnp.int32),
            pltpu.SemaphoreType.DMA((7,)),
        ],
        name="geometry",
    )(
        variant_order,
        base_points,
        control_points,
        morph_weights.transpose(1, 0, 2),
        connectivity,
        free_flags.reshape(1, pan_dev),
        station_owner.reshape(1, pan_dev),
    )
    rows = lax.all_to_all(
        rows, ("panels", "cols", "phase"), split_axis=0, concat_axis=0, axis_index_groups=[order]
    )
    places = [order.index(owner * phases + phases - 1) for owner in range(owners)]
    kernel_scale = 1.0 / (4.0 * math.pi * math.sqrt(panels_total))
    out = jax.ShapeDtypeStruct((1, load_count, STATIONS), jnp.float32)
    return pl.pallas_call(
        functools.partial(loads_kernel, pan_dev, places, kernel_scale),
        out_shape=(out, out),
        in_specs=[vmem] * 3,
        out_specs=(vmem, vmem),
        scratch_shapes=[pltpu.VMEM((panels_total, panels_total), jnp.bfloat16)],
        compiler_params=pltpu.CompilerParams(vmem_limit_bytes=32 * 1024 * 1024),
        name="loads",
    )(
        rows,
        load_velocity.T,
        jnp.asarray(spread_matrix(), jnp.bfloat16),
    )


def shards(
    base_points,
    control_points,
    morph_weights,
    connectivity,
    free_flags,
    station_owner,
    variant_order,
    load_velocity,
):
    owners = lax.axis_size(("panels", "cols"))
    pan_dev = connectivity.shape[1]
    panels_total = owners * pan_dev
    whole = (
        panels_total <= PANELS_ON_ONE
        and panels_total % LANES == 0
        and LANES % pan_dev == 0
        and 8 * pan_dev % LANES == 0
        and STATIONS == LANES
        and variant_order.shape[0] == lax.axis_size("phase")
        and morph_weights.shape[0] * pan_dev == LANES
        and control_points.shape[1] % LANES == 0
        and load_velocity.shape[0] % 16 == 0
    )
    return (shards_whole if whole else shards_split)(
        base_points,
        control_points,
        morph_weights,
        connectivity,
        free_flags,
        station_owner,
        variant_order,
        load_velocity,
    )


def solution(mesh):
    return jax.shard_map(
        shards,
        mesh=mesh,
        in_specs=(
            P(None, ("groups", "panels", "cols")),
            P(),
            P("groups", None, None),
            P(None, ("groups", "panels", "cols")),
            P(("groups", "panels", "cols")),
            P(("groups", "panels", "cols"), None),
            P("groups"),
            P(),
        ),
        out_specs=(
            P(("groups", "phase"), None, ("panels", "cols")),
            P(("groups", "phase"), None, ("panels", "cols")),
        ),
        check_vma=False,
    )
```

```python
import functools
import math

import jax
import jax.numpy as jnp
import numpy as np
from jax import lax
from jax.experimental import pallas as pl
from jax.experimental.pallas import tpu as pltpu
from jax.sharding import PartitionSpec as P

STATIONS = 128
LANES = 128
PANELS_ON_ONE = 1024


HIGH = lax.Precision.HIGHEST
CORE_SQUARE = 0.0025
SKIN_SQUARE = 0.01


def prefix(shard, axis, combine, identity):
    length, index = (lax.axis_size(axis), lax.axis_index(axis))
    everything = jax.tree.map(lambda part: lax.all_gather(part, axis), shard)
    start = jax.tree.map(
        lambda part, zero: jnp.broadcast_to(jnp.asarray(zero, part.dtype), part.shape),
        shard,
        identity,
    )

    def step(k, before):
        reached = k < index
        new = combine(before, jax.tree.map(lambda part: part[k], everything))
        return jax.tree.map(lambda a, b: jnp.where(reached, a, b), new, before)

    return lax.fori_loop(0, length, step, start)


def panel_shape(moved_points, corner_rows):
    first_corner = jnp.take(moved_points, corner_rows[0], axis=2)
    second_corner = jnp.take(moved_points, corner_rows[1], axis=2)
    third_corner = jnp.take(moved_points, corner_rows[2], axis=2)
    centroid = (first_corner + second_corner + third_corner) / 3.0
    edge_one = second_corner - first_corner
    edge_two = third_corner - first_corner
    cross_x = edge_one[:, 1] * edge_two[:, 2] - edge_one[:, 2] * edge_two[:, 1]
    cross_y = edge_one[:, 2] * edge_two[:, 0] - edge_one[:, 0] * edge_two[:, 2]
    cross_z = edge_one[:, 0] * edge_two[:, 1] - edge_one[:, 1] * edge_two[:, 0]
    area = 0.5 * jnp.stack([cross_x, cross_y, cross_z], axis=1)
    weight = jnp.sqrt(jnp.sum(area * area, axis=1) + SKIN_SQUARE)
    return (centroid, area, weight)


def tile_block(targets, sources, strengths, kernel_scale):
    distance = (
        (targets[:, 0, :, None] - sources[:, 0, None, :]) ** 2
        + (targets[:, 1, :, None] - sources[:, 1, None, :]) ** 2
        + (targets[:, 2, :, None] - sources[:, 2, None, :]) ** 2
    )
    influence = (sources[:, 3, None, :] * kernel_scale * lax.rsqrt(distance + CORE_SQUARE)).astype(
        jnp.bfloat16
    )
    return jnp.einsum("mrn,mkn->mkr", influence, strengths, preferred_element_type=jnp.float32)


def tile_product(carry_sum, targets, sources, strengths, kernel_scale):
    columns = strengths.shape[2]
    block_width = columns
    for candidate in (2048, 1024, 512):
        if columns > candidate and columns % candidate == 0:
            block_width = candidate
            break
    if block_width == columns:
        return carry_sum + tile_block(targets, sources, strengths, kernel_scale)

    def block_step(step_index, running_sum):
        column_start = step_index * block_width
        part_sources = lax.dynamic_slice_in_dim(sources, column_start, block_width, 2)
        part_strengths = lax.dynamic_slice_in_dim(strengths, column_start, block_width, 2)
        return running_sum + tile_block(targets, part_sources, part_strengths, kernel_scale)

    return lax.fori_loop(0, columns // block_width, block_step, carry_sum)


def add_pairs(earlier, later):
    return (earlier[0] + later[0], earlier[1] + later[1])


def shards_split(
    base_points,
    control_points,
    morph_weights,
    connectivity,
    free_flags,
    station_owner,
    variant_order,
    load_velocity,
):
    owners = lax.axis_size(("panels", "cols"))
    owner_index = lax.axis_index(("panels", "cols"))
    phase_index = lax.axis_index("phase")
    variant_dev = variant_order.shape[0] // lax.axis_size("phase")
    vert_dev = base_points.shape[1]
    pan_dev = connectivity.shape[1]
    load_count = load_velocity.shape[0]
    panels_total = pan_dev * owners
    own_variants = lax.dynamic_slice_in_dim(
        variant_order, phase_index * variant_dev, variant_dev, 0
    )
    picker = (
        own_variants[:, None] == jnp.arange(variant_order.shape[0], dtype=jnp.int32)[None, :]
    ).astype(jnp.float32)
    chosen = jnp.einsum("mv,vac->mac", picker, morph_weights, precision=HIGH)
    distance = (
        (control_points[0][:, None] - base_points[0][None, :]) ** 2
        + (control_points[1][:, None] - base_points[1][None, :]) ** 2
        + (control_points[2][:, None] - base_points[2][None, :]) ** 2
    )
    basis_values = lax.rsqrt(1.0 + distance)
    moved_points = base_points[None] + jnp.einsum(
        "mac,cn->man", chosen, basis_values, precision=HIGH
    )
    local_corners = connectivity - owner_index * vert_dev
    centroid, area, weight = panel_shape(moved_points, local_corners)
    hull_mask = (1 - free_flags).astype(jnp.float32)
    boundary = (
        jnp.einsum("ka,man->mkn", load_velocity, area, precision=HIGH) * hull_mask[None, None, :]
    )
    first_strengths = boundary.astype(jnp.bfloat16)
    kernel_scale = 1.0 / (4.0 * math.pi * math.sqrt(panels_total))
    own_geometry = jnp.concatenate([centroid, weight[:, None, :]], axis=1)
    sources = lax.all_gather(own_geometry, "panels", axis=2, tiled=True)
    row_targets = lax.all_gather(centroid, "cols", axis=2, tiled=True)

    def apply_influence(strengths):
        empty_sum = jnp.zeros((variant_dev, load_count, row_targets.shape[2]), jnp.float32)
        partial_sums = tile_product(
            empty_sum,
            row_targets,
            sources,
            lax.all_gather(strengths, "panels", axis=2, tiled=True),
            kernel_scale,
        )
        return lax.psum_scatter(partial_sums, "cols", scatter_dimension=2, tiled=True)

    induced = apply_influence(first_strengths)
    second_strengths = (first_strengths.astype(jnp.float32) + (boundary - induced)).astype(
        jnp.bfloat16
    )
    pressure = apply_influence(second_strengths)
    panel_force = pressure * (area[:, 2, :] * hull_mask[None, :])[:, None, :]
    force_rows = panel_force.reshape(-1, pan_dev)
    capacity = max(2, 5 * pan_dev // (2 * owners))
    target_owner = station_owner[:, 0]
    panel_order = jnp.arange(pan_dev, dtype=jnp.int32)
    ahead = (target_owner[:, None] == target_owner[None, :]) & (
        panel_order[None, :] < panel_order[:, None]
    )
    slot_rank = jnp.sum(ahead.astype(jnp.int32), axis=1)
    slot_index = target_owner * capacity + slot_rank
    all_slots = jnp.arange(owners * capacity, dtype=jnp.int32)
    placed = slot_index[:, None] == all_slots[None, :]
    send_values = jnp.dot(force_rows, placed.astype(jnp.float32), precision=HIGH)
    station_bins = (owner_index * pan_dev + panel_order) % STATIONS
    send_bins = jnp.max(jnp.where(placed, station_bins[:, None], -1), axis=0)[None, :]
    recv_values, recv_bins = (
        lax.all_to_all(send_values, ("panels", "cols"), split_axis=1, concat_axis=1, tiled=True),
        lax.all_to_all(send_bins, ("panels", "cols"), split_axis=1, concat_axis=1, tiled=True),
    )
    matches = (recv_bins[0][:, None] == jnp.arange(STATIONS, dtype=jnp.int32)[None, :]).astype(
        jnp.float32
    )
    station_loads = jnp.dot(recv_values, matches, precision=HIGH)
    station_place = (owner_index * STATIONS + jnp.arange(STATIONS, dtype=jnp.int32)).astype(
        jnp.float32
    ) / (STATIONS * owners)
    placed_loads = station_loads * station_place[None, :]
    own_total = jnp.sum(station_loads, axis=1)
    own_arm = jnp.sum(placed_loads, axis=1)
    zero_row = jnp.zeros_like(own_total)
    prior_total, prior_arm = prefix(
        (own_total, own_arm), ("panels", "cols"), add_pairs, (zero_row, zero_row)
    )
    station_rank = jnp.arange(STATIONS, dtype=jnp.int32)
    inclusive = (station_rank[:, None] <= station_rank[None, :]).astype(jnp.float32)
    strict = (station_rank[:, None] < station_rank[None, :]).astype(jnp.float32)
    running = prior_total[:, None] + jnp.dot(station_loads, inclusive, precision=HIGH)
    earlier = prior_total[:, None] + jnp.dot(station_loads, strict, precision=HIGH)
    moment_arm = prior_arm[:, None] + jnp.dot(placed_loads, strict, precision=HIGH)
    inv_root = 1.0 / math.sqrt(panels_total)
    shear = (running * inv_root).reshape(variant_dev, load_count, STATIONS)
    moment = ((station_place[None, :] * earlier - moment_arm) * inv_root).reshape(
        variant_dev, load_count, STATIONS
    )
    return (shear, moment)


def geometry_kernel(
    vert_dev,
    phases,
    order,
    kernel_scale,
    order_hbm,
    base_hbm,
    control_hbm,
    weights_hbm,
    corner_hbm,
    flags_hbm,
    owner_hbm,
    out_ref,
    order_ref,
    base_ref,
    control_ref,
    weights_ref,
    corner_ref,
    flags_ref,
    owner_ref,
    arrived,
):
    @pl.when(lax.axis_index("phase") == phases - 1)
    def _():
        sources = (
            weights_hbm,
            control_hbm,
            base_hbm,
            corner_hbm,
            flags_hbm,
            owner_hbm,
            order_hbm,
        )
        places = (
            weights_ref,
            control_ref,
            base_ref,
            corner_ref,
            flags_ref,
            owner_ref,
            order_ref,
        )
        copies = [
            pltpu.make_async_copy(source, place, arrived.at[k])
            for k, (source, place) in enumerate(zip(sources, places))
        ]
        for copy in copies:
            copy.start()
        for copy in copies:
            copy.wait()
        panel_rows(
            vert_dev,
            phases,
            order,
            kernel_scale,
            order_ref,
            base_ref,
            control_ref,
            weights_ref,
            corner_ref,
            flags_ref,
            owner_ref,
            out_ref,
        )


def panel_rows(
    vert_dev,
    phases,
    order,
    kernel_scale,
    order_ref,
    base_ref,
    control_ref,
    weights_ref,
    corner_ref,
    flags_ref,
    owner_ref,
    out_ref,
):
    pan_dev = corner_ref.shape[1]
    variants = weights_ref.shape[1]
    diagonal = lax.broadcasted_iota(jnp.int32, (vert_dev, vert_dev), 0) == lax.broadcasted_iota(
        jnp.int32, (vert_dev, vert_dev), 1
    )
    base = [
        jnp.sum(jnp.where(diagonal, base_ref[a : a + 1, :], 0.0), axis=1, keepdims=True)
        for a in range(3)
    ]
    totals = [[None] * 3 for _ in range(variants)]
    for start in range(0, control_ref.shape[1], LANES):
        part = pl.ds(start, LANES)
        distance = (
            (control_ref[0:1, part] - base[0]) ** 2
            + (control_ref[1:2, part] - base[1]) ** 2
            + (control_ref[2:3, part] - base[2]) ** 2
        )
        basis = lax.rsqrt(1.0 + distance)
        for v in range(variants):
            for a in range(3):
                term = weights_ref[a, v : v + 1, part] * basis
                totals[v][a] = term if start == 0 else totals[v][a] + term
    lane = lax.broadcasted_iota(jnp.int32, (vert_dev, LANES), 1)
    moved = []
    for a in range(3):
        shift = jnp.sum(totals[0][a], axis=1, keepdims=True)
        for v in range(1, variants):
            own = jnp.sum(totals[v][a], axis=1, keepdims=True)
            shift = jnp.where(lane >= v * pan_dev, own, shift)
        moved.append(base[a] + shift)

    def repeated(row):
        return jnp.concatenate([row] * variants, axis=1)

    vertex = lax.broadcasted_iota(jnp.int32, (vert_dev, LANES), 0)
    corners = []
    for k in range(3):
        chosen = vertex == lax.rem(repeated(corner_ref[k : k + 1, :]), vert_dev)
        corners.append(
            [jnp.sum(jnp.where(chosen, moved[a], 0.0), axis=0, keepdims=True) for a in range(3)]
        )
    first, second, third = corners
    centroid = [(first[a] + second[a] + third[a]) * (1.0 / 3.0) for a in range(3)]
    one = [second[a] - first[a] for a in range(3)]
    two = [third[a] - first[a] for a in range(3)]
    area = [
        0.5 * (one[1] * two[2] - one[2] * two[1]),
        0.5 * (one[2] * two[0] - one[0] * two[2]),
        0.5 * (one[0] * two[1] - one[1] * two[0]),
    ]
    weight = (
        jnp.sqrt(area[0] * area[0] + area[1] * area[1] + area[2] * area[2] + SKIN_SQUARE)
        * kernel_scale
    )
    hull = (1 - repeated(flags_ref[...])).astype(jnp.float32)
    owner = repeated(owner_ref[...]).astype(jnp.float32)
    rows = centroid + [weight] + [hull * area[a] for a in range(3)] + [owner]
    height = out_ref.shape[1]
    shared = LANES // pan_dev
    pieces = [jnp.concatenate(rows[k : k + height], axis=0) for k in range(0, len(rows), height)]
    turned = [
        [pltpu.roll(piece, t * pan_dev, 1) if t else piece for t in range(shared)]
        for piece in pieces
    ]
    lane = lax.broadcasted_iota(jnp.int32, (height, LANES), 1)
    row = lax.broadcasted_iota(jnp.int32, (height, LANES), 0)
    cols = lax.axis_size("cols")
    place_here = (lax.axis_index("panels") * cols + lax.axis_index("cols")) % shared
    begin = (place_here + shared - 1) % shared * pan_dev
    last = (row == height - 1) & (lane >= begin) & (lane < begin + pan_dev)
    blocks = [None] * variants
    for h in range(shared):
        slots = [(k + h) % shared for k in range(shared)]
        for v in range(variants):
            block = turned[slots.index(0)][-v % shared]
            for slot in range(1, shared):
                piece = turned[slots.index(slot)][(slot - v) % shared]
                block = jnp.where(lane >= slot * pan_dev, piece, block)
            blocks[v] = block if h == 0 else jnp.where(place_here == h, block, blocks[v])
    for slot in range(phases):
        block = blocks[0]
        for v in range(1, variants):
            block = jnp.where(order_ref[slot] == v, blocks[v], block)
        for place, member in enumerate(order):
            if member % phases == slot:
                out_ref[place] = jnp.where(last, block - float(member // phases), block)


def in_parts(values):
    high = values.astype(jnp.bfloat16).astype(jnp.float32)
    rest = values - high
    middle = rest.astype(jnp.bfloat16).astype(jnp.float32)
    return high, middle, rest - middle


def dot_rows(left, right):
    return lax.dot_general(
        left.astype(jnp.bfloat16),
        right.astype(jnp.bfloat16),
        (((0,), (0,)), ((), ())),
        preferred_element_type=jnp.float32,
    )


def spread_matrix():
    spread = np.zeros((16, 4 * LANES), np.float32)
    for row in range(12):
        spread[row, row % 4 * LANES : (row % 4 + 1) * LANES] = 1.0
    return spread


def loads_kernel(
    pan_dev,
    places,
    rows_ref,
    velocity_ref,
    spread_ref,
    shear_ref,
    moment_ref,
):
    owners = len(places)
    shared = LANES // pan_dev
    tiles = owners // shared
    panels_total = owners * pan_dev
    load_count = velocity_ref.shape[1]
    height = rows_ref.shape[1]
    lane = lax.broadcasted_iota(jnp.int32, (height, LANES), 1)
    panels = []
    for q in range(tiles):
        blocks = [rows_ref[places[q * shared + h]] for h in range(shared)]
        pieces = []
        for k in range(shared):
            piece = blocks[-k % shared]
            for slot in range(1, shared):
                piece = jnp.where(lane >= slot * pan_dev, blocks[(slot - k) % shared], piece)
            pieces.append(pltpu.roll(piece, LANES - k * pan_dev, 1) if k else piece)
        panels.append(pieces)

    def tile_rows(q, begin, end):
        if height < end - begin:
            return jnp.concatenate(panels[q][begin // height : end // height], axis=0)
        return panels[q][begin // height][begin % height : begin % height + end - begin, :]

    centres = [tile_rows(q, 0, 4) for q in range(tiles)]
    areas = [tile_rows(q, 4, 8) for q in range(tiles)]
    high, middle, low = in_parts(jnp.concatenate(centres, axis=1))
    columns = dot_rows(
        jnp.concatenate([high, middle, low, jnp.zeros_like(low)], axis=0), spread_ref[...]
    )
    influences = {}
    for source in range(tiles):
        for target in range(source, tiles):
            tile = centres[target]
            column = columns[source * LANES : (source + 1) * LANES, :]
            column = [column[:, a * LANES : (a + 1) * LANES] for a in range(4)]
            inverse = lax.rsqrt(
                (tile[0:1, :] - column[0]) ** 2
                + (tile[1:2, :] - column[1]) ** 2
                + (tile[2:3, :] - column[2]) ** 2
                + CORE_SQUARE
            )
            influences[source, target] = (column[3] * inverse).astype(jnp.bfloat16)
            if target != source:
                other = columns[target * LANES : (target + 1) * LANES, 3 * LANES :]
                influences[target, source] = (other * inverse.T).astype(jnp.bfloat16)
    area_parts = in_parts(jnp.concatenate(areas, axis=1))
    velocity_parts = in_parts(
        jnp.concatenate([velocity_ref[...], jnp.zeros((1, load_count), jnp.float32)], axis=0)
    )
    pairs = ((0, 0), (0, 1), (1, 0), (1, 1), (0, 2), (2, 0), (1, 2), (2, 1))
    boundary = dot_rows(
        jnp.concatenate([velocity_parts[k] for k, _ in pairs], axis=0),
        jnp.concatenate([area_parts[k] for _, k in pairs], axis=0),
    )
    first = boundary.astype(jnp.bfloat16)
    influence = jnp.concatenate(
        [
            jnp.concatenate([influences[q, p] for p in range(tiles)], axis=1)
            for q in range(tiles)
        ],
        axis=0,
    )
    induced = jnp.dot(first, influence, preferred_element_type=jnp.float32)
    second = (first.astype(jnp.float32) + (boundary - induced)).astype(jnp.bfloat16)
    pressure = jnp.dot(second, influence, preferred_element_type=jnp.float32)
    stations_all = STATIONS * owners
    own_loads = jnp.zeros((load_count, LANES), jnp.float32)
    prior_loads = jnp.zeros((load_count, LANES), jnp.float32)
    prior_arms = jnp.zeros((load_count, LANES), jnp.float32)
    rank = lax.broadcasted_iota(jnp.int32, (1, LANES), 1).astype(jnp.float32)
    for q, tile in enumerate(areas):
        force = pressure[:, q * LANES : (q + 1) * LANES] * tile[2:3, :]
        owner = tile[3:4, :]
        prior = owner < 0.0
        place = (owner * STATIONS + rank) * (1.0 / stations_all)
        own_loads = own_loads + jnp.where(owner == 0.0, force, 0.0)
        prior_loads = prior_loads + jnp.where(prior, force, 0.0)
        prior_arms = prior_arms + force * jnp.where(prior, place, 0.0)
    prior_total = jnp.sum(prior_loads, axis=1, keepdims=True)
    prior_arm = jnp.sum(prior_arms, axis=1, keepdims=True)
    station = lax.broadcasted_iota(jnp.int32, (STATIONS, 2 * STATIONS), 0)
    place = lax.broadcasted_iota(jnp.int32, (STATIONS, 2 * STATIONS), 1)
    arm = place - STATIONS - station
    steps = jnp.where(
        place < STATIONS, (station <= place).astype(jnp.int32), jnp.maximum(arm, 0)
    ).astype(jnp.float32).astype(jnp.bfloat16)
    high = own_loads.astype(jnp.bfloat16)
    rest = own_loads - high.astype(jnp.float32)
    middle = rest.astype(jnp.bfloat16)
    low = (rest - middle.astype(jnp.float32)).astype(jnp.bfloat16)
    sums = jnp.dot(
        jnp.concatenate([high, middle, low], axis=0), steps, preferred_element_type=jnp.float32
    )
    sums = sums[:load_count] + (sums[load_count : 2 * load_count] + sums[2 * load_count :])
    inv_root = 1.0 / math.sqrt(panels_total)
    shear_ref[0] = (prior_total + sums[:, :STATIONS]) * inv_root
    moment_ref[0] = (
        (rank * (1.0 / stations_all)) * prior_total
        - prior_arm
        + sums[:, STATIONS:] * (1.0 / stations_all)
    ) * inv_root


def shards_whole(
    base_points,
    control_points,
    morph_weights,
    connectivity,
    free_flags,
    station_owner,
    variant_order,
    load_velocity,
):
    owners = lax.axis_size(("panels", "cols"))
    vert_dev = base_points.shape[1]
    pan_dev = connectivity.shape[1]
    load_count = load_velocity.shape[0]
    panels_total = pan_dev * owners
    phases = lax.axis_size("phase")
    members = owners * phases
    variants = morph_weights.shape[0]
    control = control_points.shape[1]
    height = 8 * pan_dev // LANES
    order = [owner * phases + k for owner in range(owners)[::-1] for k in range(phases)]
    kernel_scale = 1.0 / (4.0 * math.pi * math.sqrt(panels_total))
    vmem = pl.BlockSpec(memory_space=pltpu.VMEM)
    anywhere = pl.BlockSpec(memory_space=pl.ANY)
    rows = pl.pallas_call(
        functools.partial(geometry_kernel, vert_dev, phases, order, kernel_scale),
        out_shape=pltpu.VMEM((members, height, LANES), jnp.float32),
        in_specs=[anywhere] * 7,
        out_specs=vmem,
        scratch_shapes=[
            pltpu.SMEM((variants,), jnp.int32),
            pltpu.VMEM((3, vert_dev), jnp.float32),
            pltpu.VMEM((3, control), jnp.float32),
            pltpu.VMEM((3, variants, control), jnp.float32),
            pltpu.VMEM((3, pan_dev), jnp.int32),
            pltpu.VMEM((1, pan_dev), jnp.int32),
            pltpu.VMEM((1, pan_dev), jnp.int32),
            pltpu.SemaphoreType.DMA((7,)),
        ],
        name="geometry",
    )(
        variant_order,
        base_points,
        control_points,
        morph_weights.transpose(1, 0, 2),
        connectivity,
        free_flags.reshape(1, pan_dev),
        station_owner.reshape(1, pan_dev),
    )
    rows = lax.all_to_all(
        rows, ("panels", "cols", "phase"), split_axis=0, concat_axis=0, axis_index_groups=[order]
    )
    places = [order.index(owner * phases + phases - 1) for owner in range(owners)]
    out = jax.ShapeDtypeStruct((1, load_count, STATIONS), jnp.float32)
    return pl.pallas_call(
        functools.partial(loads_kernel, pan_dev, places),
        out_shape=(out, out),
        in_specs=[vmem] * 3,
        out_specs=(vmem, vmem),
        compiler_params=pltpu.CompilerParams(vmem_limit_bytes=32 * 1024 * 1024),
        name="loads",
    )(
        rows,
        load_velocity.T,
        jnp.asarray(spread_matrix(), jnp.bfloat16),
    )


def shards(
    base_points,
    control_points,
    morph_weights,
    connectivity,
    free_flags,
    station_owner,
    variant_order,
    load_velocity,
):
    owners = lax.axis_size(("panels", "cols"))
    pan_dev = connectivity.shape[1]
    panels_total = owners * pan_dev
    whole = (
        panels_total <= PANELS_ON_ONE
        and panels_total % LANES == 0
        and LANES % pan_dev == 0
        and 8 * pan_dev % LANES == 0
        and STATIONS == LANES
        and variant_order.shape[0] == lax.axis_size("phase")
        and morph_weights.shape[0] * pan_dev == LANES
        and control_points.shape[1] % LANES == 0
        and load_velocity.shape[0] % 16 == 0
    )
    return (shards_whole if whole else shards_split)(
        base_points,
        control_points,
        morph_weights,
        connectivity,
        free_flags,
        station_owner,
        variant_order,
        load_velocity,
    )


def solution(mesh):
    return jax.shard_map(
        shards,
        mesh=mesh,
        in_specs=(
            P(None, ("groups", "panels", "cols")),
            P(),
            P("groups", None, None),
            P(None, ("groups", "panels", "cols")),
            P(("groups", "panels", "cols")),
            P(("groups", "panels", "cols"), None),
            P("groups"),
            P(),
        ),
        out_specs=(
            P(("groups", "phase"), None, ("panels", "cols")),
            P(("groups", "phase"), None, ("panels", "cols")),
        ),
        check_vma=False,
    )
```

```python
import functools
import math

import jax
import jax.numpy as jnp
import numpy as np
from jax import lax
from jax.experimental import pallas as pl
from jax.experimental.pallas import tpu as pltpu
from jax.sharding import PartitionSpec as P

STATIONS = 128
LANES = 128
PANELS_ON_ONE = 1024


HIGH = lax.Precision.HIGHEST
CORE_SQUARE = 0.0025
SKIN_SQUARE = 0.01


def prefix(shard, axis, combine, identity):
    length, index = (lax.axis_size(axis), lax.axis_index(axis))
    everything = jax.tree.map(lambda part: lax.all_gather(part, axis), shard)
    start = jax.tree.map(
        lambda part, zero: jnp.broadcast_to(jnp.asarray(zero, part.dtype), part.shape),
        shard,
        identity,
    )

    def step(k, before):
        reached = k < index
        new = combine(before, jax.tree.map(lambda part: part[k], everything))
        return jax.tree.map(lambda a, b: jnp.where(reached, a, b), new, before)

    return lax.fori_loop(0, length, step, start)


def panel_shape(moved_points, corner_rows):
    first_corner = jnp.take(moved_points, corner_rows[0], axis=2)
    second_corner = jnp.take(moved_points, corner_rows[1], axis=2)
    third_corner = jnp.take(moved_points, corner_rows[2], axis=2)
    centroid = (first_corner + second_corner + third_corner) / 3.0
    edge_one = second_corner - first_corner
    edge_two = third_corner - first_corner
    cross_x = edge_one[:, 1] * edge_two[:, 2] - edge_one[:, 2] * edge_two[:, 1]
    cross_y = edge_one[:, 2] * edge_two[:, 0] - edge_one[:, 0] * edge_two[:, 2]
    cross_z = edge_one[:, 0] * edge_two[:, 1] - edge_one[:, 1] * edge_two[:, 0]
    area = 0.5 * jnp.stack([cross_x, cross_y, cross_z], axis=1)
    weight = jnp.sqrt(jnp.sum(area * area, axis=1) + SKIN_SQUARE)
    return (centroid, area, weight)


def tile_block(targets, sources, strengths, kernel_scale):
    distance = (
        (targets[:, 0, :, None] - sources[:, 0, None, :]) ** 2
        + (targets[:, 1, :, None] - sources[:, 1, None, :]) ** 2
        + (targets[:, 2, :, None] - sources[:, 2, None, :]) ** 2
    )
    influence = (sources[:, 3, None, :] * kernel_scale * lax.rsqrt(distance + CORE_SQUARE)).astype(
        jnp.bfloat16
    )
    return jnp.einsum("mrn,mkn->mkr", influence, strengths, preferred_element_type=jnp.float32)


def tile_product(carry_sum, targets, sources, strengths, kernel_scale):
    columns = strengths.shape[2]
    block_width = columns
    for candidate in (2048, 1024, 512):
        if columns > candidate and columns % candidate == 0:
            block_width = candidate
            break
    if block_width == columns:
        return carry_sum + tile_block(targets, sources, strengths, kernel_scale)

    def block_step(step_index, running_sum):
        column_start = step_index * block_width
        part_sources = lax.dynamic_slice_in_dim(sources, column_start, block_width, 2)
        part_strengths = lax.dynamic_slice_in_dim(strengths, column_start, block_width, 2)
        return running_sum + tile_block(targets, part_sources, part_strengths, kernel_scale)

    return lax.fori_loop(0, columns // block_width, block_step, carry_sum)


def add_pairs(earlier, later):
    return (earlier[0] + later[0], earlier[1] + later[1])


def shards_split(
    base_points,
    control_points,
    morph_weights,
    connectivity,
    free_flags,
    station_owner,
    variant_order,
    load_velocity,
):
    owners = lax.axis_size(("panels", "cols"))
    owner_index = lax.axis_index(("panels", "cols"))
    phase_index = lax.axis_index("phase")
    variant_dev = variant_order.shape[0] // lax.axis_size("phase")
    vert_dev = base_points.shape[1]
    pan_dev = connectivity.shape[1]
    load_count = load_velocity.shape[0]
    panels_total = pan_dev * owners
    own_variants = lax.dynamic_slice_in_dim(
        variant_order, phase_index * variant_dev, variant_dev, 0
    )
    picker = (
        own_variants[:, None] == jnp.arange(variant_order.shape[0], dtype=jnp.int32)[None, :]
    ).astype(jnp.float32)
    chosen = jnp.einsum("mv,vac->mac", picker, morph_weights, precision=HIGH)
    distance = (
        (control_points[0][:, None] - base_points[0][None, :]) ** 2
        + (control_points[1][:, None] - base_points[1][None, :]) ** 2
        + (control_points[2][:, None] - base_points[2][None, :]) ** 2
    )
    basis_values = lax.rsqrt(1.0 + distance)
    moved_points = base_points[None] + jnp.einsum(
        "mac,cn->man", chosen, basis_values, precision=HIGH
    )
    local_corners = connectivity - owner_index * vert_dev
    centroid, area, weight = panel_shape(moved_points, local_corners)
    hull_mask = (1 - free_flags).astype(jnp.float32)
    boundary = (
        jnp.einsum("ka,man->mkn", load_velocity, area, precision=HIGH) * hull_mask[None, None, :]
    )
    first_strengths = boundary.astype(jnp.bfloat16)
    kernel_scale = 1.0 / (4.0 * math.pi * math.sqrt(panels_total))
    own_geometry = jnp.concatenate([centroid, weight[:, None, :]], axis=1)
    sources = lax.all_gather(own_geometry, "panels", axis=2, tiled=True)
    row_targets = lax.all_gather(centroid, "cols", axis=2, tiled=True)

    def apply_influence(strengths):
        empty_sum = jnp.zeros((variant_dev, load_count, row_targets.shape[2]), jnp.float32)
        partial_sums = tile_product(
            empty_sum,
            row_targets,
            sources,
            lax.all_gather(strengths, "panels", axis=2, tiled=True),
            kernel_scale,
        )
        return lax.psum_scatter(partial_sums, "cols", scatter_dimension=2, tiled=True)

    induced = apply_influence(first_strengths)
    second_strengths = (first_strengths.astype(jnp.float32) + (boundary - induced)).astype(
        jnp.bfloat16
    )
    pressure = apply_influence(second_strengths)
    panel_force = pressure * (area[:, 2, :] * hull_mask[None, :])[:, None, :]
    force_rows = panel_force.reshape(-1, pan_dev)
    capacity = max(2, 5 * pan_dev // (2 * owners))
    target_owner = station_owner[:, 0]
    panel_order = jnp.arange(pan_dev, dtype=jnp.int32)
    ahead = (target_owner[:, None] == target_owner[None, :]) & (
        panel_order[None, :] < panel_order[:, None]
    )
    slot_rank = jnp.sum(ahead.astype(jnp.int32), axis=1)
    slot_index = target_owner * capacity + slot_rank
    all_slots = jnp.arange(owners * capacity, dtype=jnp.int32)
    placed = slot_index[:, None] == all_slots[None, :]
    send_values = jnp.dot(force_rows, placed.astype(jnp.float32), precision=HIGH)
    station_bins = (owner_index * pan_dev + panel_order) % STATIONS
    send_bins = jnp.max(jnp.where(placed, station_bins[:, None], -1), axis=0)[None, :]
    recv_values, recv_bins = (
        lax.all_to_all(send_values, ("panels", "cols"), split_axis=1, concat_axis=1, tiled=True),
        lax.all_to_all(send_bins, ("panels", "cols"), split_axis=1, concat_axis=1, tiled=True),
    )
    matches = (recv_bins[0][:, None] == jnp.arange(STATIONS, dtype=jnp.int32)[None, :]).astype(
        jnp.float32
    )
    station_loads = jnp.dot(recv_values, matches, precision=HIGH)
    station_place = (owner_index * STATIONS + jnp.arange(STATIONS, dtype=jnp.int32)).astype(
        jnp.float32
    ) / (STATIONS * owners)
    placed_loads = station_loads * station_place[None, :]
    own_total = jnp.sum(station_loads, axis=1)
    own_arm = jnp.sum(placed_loads, axis=1)
    zero_row = jnp.zeros_like(own_total)
    prior_total, prior_arm = prefix(
        (own_total, own_arm), ("panels", "cols"), add_pairs, (zero_row, zero_row)
    )
    station_rank = jnp.arange(STATIONS, dtype=jnp.int32)
    inclusive = (station_rank[:, None] <= station_rank[None, :]).astype(jnp.float32)
    strict = (station_rank[:, None] < station_rank[None, :]).astype(jnp.float32)
    running = prior_total[:, None] + jnp.dot(station_loads, inclusive, precision=HIGH)
    earlier = prior_total[:, None] + jnp.dot(station_loads, strict, precision=HIGH)
    moment_arm = prior_arm[:, None] + jnp.dot(placed_loads, strict, precision=HIGH)
    inv_root = 1.0 / math.sqrt(panels_total)
    shear = (running * inv_root).reshape(variant_dev, load_count, STATIONS)
    moment = ((station_place[None, :] * earlier - moment_arm) * inv_root).reshape(
        variant_dev, load_count, STATIONS
    )
    return (shear, moment)


def geometry_kernel(
    vert_dev,
    phases,
    order,
    kernel_scale,
    order_hbm,
    base_hbm,
    control_hbm,
    weights_hbm,
    corner_hbm,
    flags_hbm,
    owner_hbm,
    out_ref,
    order_ref,
    base_ref,
    control_ref,
    weights_ref,
    corner_ref,
    flags_ref,
    owner_ref,
    arrived,
):
    @pl.when(lax.axis_index("phase") == phases - 1)
    def _():
        sources = (
            weights_hbm,
            control_hbm,
            base_hbm,
            corner_hbm,
            flags_hbm,
            owner_hbm,
            order_hbm,
        )
        places = (
            weights_ref,
            control_ref,
            base_ref,
            corner_ref,
            flags_ref,
            owner_ref,
            order_ref,
        )
        copies = [
            pltpu.make_async_copy(source, place, arrived.at[k])
            for k, (source, place) in enumerate(zip(sources, places))
        ]
        for copy in copies:
            copy.start()
        for copy in copies:
            copy.wait()
        panel_rows(
            vert_dev,
            phases,
            order,
            kernel_scale,
            order_ref,
            base_ref,
            control_ref,
            weights_ref,
            corner_ref,
            flags_ref,
            owner_ref,
            out_ref,
        )


def panel_rows(
    vert_dev,
    phases,
    order,
    kernel_scale,
    order_ref,
    base_ref,
    control_ref,
    weights_ref,
    corner_ref,
    flags_ref,
    owner_ref,
    out_ref,
):
    pan_dev = corner_ref.shape[1]
    variants = weights_ref.shape[1]
    diagonal = lax.broadcasted_iota(jnp.int32, (vert_dev, vert_dev), 0) == lax.broadcasted_iota(
        jnp.int32, (vert_dev, vert_dev), 1
    )
    base = [
        jnp.sum(jnp.where(diagonal, base_ref[a : a + 1, :], 0.0), axis=1, keepdims=True)
        for a in range(3)
    ]
    totals = [[None] * 3 for _ in range(variants)]
    for start in range(0, control_ref.shape[1], LANES):
        part = pl.ds(start, LANES)
        distance = (
            (control_ref[0:1, part] - base[0]) ** 2
            + (control_ref[1:2, part] - base[1]) ** 2
            + (control_ref[2:3, part] - base[2]) ** 2
        )
        basis = lax.rsqrt(1.0 + distance)
        for v in range(variants):
            for a in range(3):
                term = weights_ref[a, v : v + 1, part] * basis
                totals[v][a] = term if start == 0 else totals[v][a] + term
    lane = lax.broadcasted_iota(jnp.int32, (vert_dev, LANES), 1)
    moved = []
    for a in range(3):
        shift = jnp.sum(totals[0][a], axis=1, keepdims=True)
        for v in range(1, variants):
            own = jnp.sum(totals[v][a], axis=1, keepdims=True)
            shift = jnp.where(lane >= v * pan_dev, own, shift)
        moved.append(base[a] + shift)

    def repeated(row):
        return jnp.concatenate([row] * variants, axis=1)

    vertex = lax.broadcasted_iota(jnp.int32, (vert_dev, LANES), 0)
    corners = []
    for k in range(3):
        chosen = vertex == lax.rem(repeated(corner_ref[k : k + 1, :]), vert_dev)
        corners.append(
            [jnp.sum(jnp.where(chosen, moved[a], 0.0), axis=0, keepdims=True) for a in range(3)]
        )
    first, second, third = corners
    centroid = [(first[a] + second[a] + third[a]) * (1.0 / 3.0) for a in range(3)]
    one = [second[a] - first[a] for a in range(3)]
    two = [third[a] - first[a] for a in range(3)]
    area = [
        0.5 * (one[1] * two[2] - one[2] * two[1]),
        0.5 * (one[2] * two[0] - one[0] * two[2]),
        0.5 * (one[0] * two[1] - one[1] * two[0]),
    ]
    weight = (
        jnp.sqrt(area[0] * area[0] + area[1] * area[1] + area[2] * area[2] + SKIN_SQUARE)
        * kernel_scale
    )
    hull = (1 - repeated(flags_ref[...])).astype(jnp.float32)
    owner = repeated(owner_ref[...]).astype(jnp.float32)
    rows = centroid + [weight] + [hull * area[a] for a in range(3)] + [owner]
    height = out_ref.shape[1]
    shared = LANES // pan_dev
    pieces = [jnp.concatenate(rows[k : k + height], axis=0) for k in range(0, len(rows), height)]
    turned = [
        [pltpu.roll(piece, t * pan_dev, 1) if t else piece for t in range(shared)]
        for piece in pieces
    ]
    lane = lax.broadcasted_iota(jnp.int32, (height, LANES), 1)
    row = lax.broadcasted_iota(jnp.int32, (height, LANES), 0)
    cols = lax.axis_size("cols")
    place_here = (lax.axis_index("panels") * cols + lax.axis_index("cols")) % shared
    begin = (place_here + shared - 1) % shared * pan_dev
    last = (row == height - 1) & (lane >= begin) & (lane < begin + pan_dev)
    blocks = [None] * variants
    for h in range(shared):
        slots = [(k + h) % shared for k in range(shared)]
        for v in range(variants):
            block = turned[slots.index(0)][-v % shared]
            for slot in range(1, shared):
                piece = turned[slots.index(slot)][(slot - v) % shared]
                block = jnp.where(lane >= slot * pan_dev, piece, block)
            blocks[v] = block if h == 0 else jnp.where(place_here == h, block, blocks[v])
    for slot in range(phases):
        block = blocks[0]
        for v in range(1, variants):
            block = jnp.where(order_ref[slot] == v, blocks[v], block)
        for place, member in enumerate(order):
            if member % phases == slot:
                out_ref[place] = jnp.where(last, block - float(member // phases), block)


def in_parts(values):
    high = values.astype(jnp.bfloat16).astype(jnp.float32)
    rest = values - high
    middle = rest.astype(jnp.bfloat16).astype(jnp.float32)
    return high, middle, rest - middle


def dot_rows(left, right):
    return lax.dot_general(
        left.astype(jnp.bfloat16),
        right.astype(jnp.bfloat16),
        (((0,), (0,)), ((), ())),
        preferred_element_type=jnp.float32,
    )


def spread_matrix():
    spread = np.zeros((16, 4 * LANES), np.float32)
    for row in range(12):
        spread[row, row % 4 * LANES : (row % 4 + 1) * LANES] = 1.0
    return spread


def loads_kernel(
    pan_dev,
    places,
    rows_ref,
    velocity_ref,
    spread_ref,
    shear_ref,
    moment_ref,
):
    owners = len(places)
    shared = LANES // pan_dev
    tiles = owners // shared
    panels_total = owners * pan_dev
    load_count = velocity_ref.shape[1]
    height = rows_ref.shape[1]
    lane = lax.broadcasted_iota(jnp.int32, (height, LANES), 1)
    panels = []
    for q in range(tiles):
        blocks = [rows_ref[places[q * shared + h]] for h in range(shared)]
        pieces = []
        for k in range(shared):
            piece = blocks[-k % shared]
            for slot in range(1, shared):
                piece = jnp.where(lane >= slot * pan_dev, blocks[(slot - k) % shared], piece)
            pieces.append(pltpu.roll(piece, LANES - k * pan_dev, 1) if k else piece)
        panels.append(pieces)

    def tile_rows(q, begin, end):
        if height < end - begin:
            return jnp.concatenate(panels[q][begin // height : end // height], axis=0)
        return panels[q][begin // height][begin % height : begin % height + end - begin, :]

    centres = [tile_rows(q, 0, 4) for q in range(tiles)]
    areas = [tile_rows(q, 4, 8) for q in range(tiles)]
    high, middle, low = in_parts(jnp.concatenate(centres, axis=1))
    columns = dot_rows(
        jnp.concatenate([high, middle, low, jnp.zeros_like(low)], axis=0), spread_ref[...]
    )
    influences = {}
    for source in range(tiles):
        for target in range(source, tiles):
            tile = centres[target]
            column = columns[source * LANES : (source + 1) * LANES, :]
            column = [column[:, a * LANES : (a + 1) * LANES] for a in range(4)]
            inverse = lax.rsqrt(
                (tile[0:1, :] - column[0]) ** 2
                + (tile[1:2, :] - column[1]) ** 2
                + (tile[2:3, :] - column[2]) ** 2
                + CORE_SQUARE
            )
            influences[source, target] = (column[3] * inverse).astype(jnp.bfloat16)
            if target != source:
                other = columns[target * LANES : (target + 1) * LANES, 3 * LANES :]
                influences[target, source] = (other * inverse.T).astype(jnp.bfloat16)
    area_parts = in_parts(jnp.concatenate(areas, axis=1))
    velocity_parts = in_parts(
        jnp.concatenate([velocity_ref[...], jnp.zeros((1, load_count), jnp.float32)], axis=0)
    )
    pairs = ((0, 0), (0, 1), (1, 0), (1, 1), (0, 2), (2, 0), (1, 2), (2, 1))
    boundary = dot_rows(
        jnp.concatenate([velocity_parts[k] for k, _ in pairs], axis=0),
        jnp.concatenate([area_parts[k] for _, k in pairs], axis=0),
    )
    first = boundary.astype(jnp.bfloat16)
    influence = jnp.concatenate(
        [
            jnp.concatenate([influences[q, p] for p in range(tiles)], axis=1)
            for q in range(tiles)
        ],
        axis=0,
    )
    induced = jnp.dot(first, influence, preferred_element_type=jnp.float32)
    second = (first.astype(jnp.float32) + (boundary - induced)).astype(jnp.bfloat16)
    pressure = jnp.dot(second, influence, preferred_element_type=jnp.float32)
    stations_all = STATIONS * owners
    own_loads = jnp.zeros((load_count, LANES), jnp.float32)
    prior_loads = jnp.zeros((load_count, LANES), jnp.float32)
    prior_arms = jnp.zeros((load_count, LANES), jnp.float32)
    rank = lax.broadcasted_iota(jnp.int32, (1, LANES), 1).astype(jnp.float32)
    for q, tile in enumerate(areas):
        force = pressure[:, q * LANES : (q + 1) * LANES] * tile[2:3, :]
        owner = tile[3:4, :]
        prior = owner < 0.0
        place = (owner * STATIONS + rank) * (1.0 / stations_all)
        own_loads = own_loads + jnp.where(owner == 0.0, force, 0.0)
        prior_loads = prior_loads + jnp.where(prior, force, 0.0)
        prior_arms = prior_arms + force * jnp.where(prior, place, 0.0)
    prior_total = jnp.sum(prior_loads, axis=1, keepdims=True)
    prior_arm = jnp.sum(prior_arms, axis=1, keepdims=True)
    station = lax.broadcasted_iota(jnp.int32, (STATIONS, 2 * STATIONS), 0)
    place = lax.broadcasted_iota(jnp.int32, (STATIONS, 2 * STATIONS), 1)
    arm = place - STATIONS - station
    steps = jnp.where(
        place < STATIONS, (station <= place).astype(jnp.int32), jnp.maximum(arm, 0)
    ).astype(jnp.float32).astype(jnp.bfloat16)
    high = own_loads.astype(jnp.bfloat16)
    rest = own_loads - high.astype(jnp.float32)
    middle = rest.astype(jnp.bfloat16)
    low = (rest - middle.astype(jnp.float32)).astype(jnp.bfloat16)
    sums = jnp.dot(
        jnp.concatenate([high, middle, low], axis=0), steps, preferred_element_type=jnp.float32
    )
    sums = sums[:load_count] + (sums[load_count : 2 * load_count] + sums[2 * load_count :])
    inv_root = 1.0 / math.sqrt(panels_total)
    shear_ref[0] = (prior_total + sums[:, :STATIONS]) * inv_root
    moment_ref[0] = (
        (rank * (1.0 / stations_all)) * prior_total
        - prior_arm
        + sums[:, STATIONS:] * (1.0 / stations_all)
    ) * inv_root


def shards_whole(
    base_points,
    control_points,
    morph_weights,
    connectivity,
    free_flags,
    station_owner,
    variant_order,
    load_velocity,
):
    owners = lax.axis_size(("panels", "cols"))
    vert_dev = base_points.shape[1]
    pan_dev = connectivity.shape[1]
    load_count = load_velocity.shape[0]
    panels_total = pan_dev * owners
    phases = lax.axis_size("phase")
    members = owners * phases
    variants = morph_weights.shape[0]
    control = control_points.shape[1]
    height = 8 * pan_dev // LANES
    head = (owners - 1) * phases
    order = [head] + [member for member in range(members) if member != head]
    kernel_scale = 1.0 / (4.0 * math.pi * math.sqrt(panels_total))
    vmem = pl.BlockSpec(memory_space=pltpu.VMEM)
    anywhere = pl.BlockSpec(memory_space=pl.ANY)
    rows = pl.pallas_call(
        functools.partial(geometry_kernel, vert_dev, phases, order, kernel_scale),
        out_shape=pltpu.VMEM((members, height, LANES), jnp.float32),
        in_specs=[anywhere] * 7,
        out_specs=vmem,
        scratch_shapes=[
            pltpu.SMEM((variants,), jnp.int32),
            pltpu.VMEM((3, vert_dev), jnp.float32),
            pltpu.VMEM((3, control), jnp.float32),
            pltpu.VMEM((3, variants, control), jnp.float32),
            pltpu.VMEM((3, pan_dev), jnp.int32),
            pltpu.VMEM((1, pan_dev), jnp.int32),
            pltpu.VMEM((1, pan_dev), jnp.int32),
            pltpu.SemaphoreType.DMA((7,)),
        ],
        name="geometry",
    )(
        variant_order,
        base_points,
        control_points,
        morph_weights.transpose(1, 0, 2),
        connectivity,
        free_flags.reshape(1, pan_dev),
        station_owner.reshape(1, pan_dev),
    )
    rows = lax.all_to_all(
        rows, ("panels", "cols", "phase"), split_axis=0, concat_axis=0, axis_index_groups=[order]
    )
    places = [order.index(owner * phases + phases - 1) for owner in range(owners)]
    out = jax.ShapeDtypeStruct((1, load_count, STATIONS), jnp.float32)
    return pl.pallas_call(
        functools.partial(loads_kernel, pan_dev, places),
        out_shape=(out, out),
        in_specs=[vmem] * 3,
        out_specs=(vmem, vmem),
        compiler_params=pltpu.CompilerParams(vmem_limit_bytes=32 * 1024 * 1024),
        name="loads",
    )(
        rows,
        load_velocity.T,
        jnp.asarray(spread_matrix(), jnp.bfloat16),
    )


def shards(
    base_points,
    control_points,
    morph_weights,
    connectivity,
    free_flags,
    station_owner,
    variant_order,
    load_velocity,
):
    owners = lax.axis_size(("panels", "cols"))
    pan_dev = connectivity.shape[1]
    panels_total = owners * pan_dev
    whole = (
        panels_total <= PANELS_ON_ONE
        and panels_total % LANES == 0
        and LANES % pan_dev == 0
        and 8 * pan_dev % LANES == 0
        and STATIONS == LANES
        and variant_order.shape[0] == lax.axis_size("phase")
        and morph_weights.shape[0] * pan_dev == LANES
        and control_points.shape[1] % LANES == 0
        and load_velocity.shape[0] % 16 == 0
    )
    return (shards_whole if whole else shards_split)(
        base_points,
        control_points,
        morph_weights,
        connectivity,
        free_flags,
        station_owner,
        variant_order,
        load_velocity,
    )


def solution(mesh):
    return jax.shard_map(
        shards,
        mesh=mesh,
        in_specs=(
            P(None, ("groups", "panels", "cols")),
            P(),
            P("groups", None, None),
            P(None, ("groups", "panels", "cols")),
            P(("groups", "panels", "cols")),
            P(("groups", "panels", "cols"), None),
            P("groups"),
            P(),
        ),
        out_specs=(
            P(("groups", "phase"), None, ("panels", "cols")),
            P(("groups", "phase"), None, ("panels", "cols")),
        ),
        check_vma=False,
    )
```

```python
import functools
import math

import jax
import jax.numpy as jnp
import numpy as np
from jax import lax
from jax.experimental import pallas as pl
from jax.experimental.pallas import tpu as pltpu
from jax.sharding import PartitionSpec as P

STATIONS = 128
LANES = 128
PANELS_ON_ONE = 1024


HIGH = lax.Precision.HIGHEST
CORE_SQUARE = 0.0025
SKIN_SQUARE = 0.01


def prefix(shard, axis, combine, identity):
    length, index = (lax.axis_size(axis), lax.axis_index(axis))
    everything = jax.tree.map(lambda part: lax.all_gather(part, axis), shard)
    start = jax.tree.map(
        lambda part, zero: jnp.broadcast_to(jnp.asarray(zero, part.dtype), part.shape),
        shard,
        identity,
    )

    def step(k, before):
        reached = k < index
        new = combine(before, jax.tree.map(lambda part: part[k], everything))
        return jax.tree.map(lambda a, b: jnp.where(reached, a, b), new, before)

    return lax.fori_loop(0, length, step, start)


def panel_shape(moved_points, corner_rows):
    first_corner = jnp.take(moved_points, corner_rows[0], axis=2)
    second_corner = jnp.take(moved_points, corner_rows[1], axis=2)
    third_corner = jnp.take(moved_points, corner_rows[2], axis=2)
    centroid = (first_corner + second_corner + third_corner) / 3.0
    edge_one = second_corner - first_corner
    edge_two = third_corner - first_corner
    cross_x = edge_one[:, 1] * edge_two[:, 2] - edge_one[:, 2] * edge_two[:, 1]
    cross_y = edge_one[:, 2] * edge_two[:, 0] - edge_one[:, 0] * edge_two[:, 2]
    cross_z = edge_one[:, 0] * edge_two[:, 1] - edge_one[:, 1] * edge_two[:, 0]
    area = 0.5 * jnp.stack([cross_x, cross_y, cross_z], axis=1)
    weight = jnp.sqrt(jnp.sum(area * area, axis=1) + SKIN_SQUARE)
    return (centroid, area, weight)


def tile_block(targets, sources, strengths, kernel_scale):
    distance = (
        (targets[:, 0, :, None] - sources[:, 0, None, :]) ** 2
        + (targets[:, 1, :, None] - sources[:, 1, None, :]) ** 2
        + (targets[:, 2, :, None] - sources[:, 2, None, :]) ** 2
    )
    influence = (sources[:, 3, None, :] * kernel_scale * lax.rsqrt(distance + CORE_SQUARE)).astype(
        jnp.bfloat16
    )
    return jnp.einsum("mrn,mkn->mkr", influence, strengths, preferred_element_type=jnp.float32)


def tile_product(carry_sum, targets, sources, strengths, kernel_scale):
    columns = strengths.shape[2]
    block_width = columns
    for candidate in (2048, 1024, 512):
        if columns > candidate and columns % candidate == 0:
            block_width = candidate
            break
    if block_width == columns:
        return carry_sum + tile_block(targets, sources, strengths, kernel_scale)

    def block_step(step_index, running_sum):
        column_start = step_index * block_width
        part_sources = lax.dynamic_slice_in_dim(sources, column_start, block_width, 2)
        part_strengths = lax.dynamic_slice_in_dim(strengths, column_start, block_width, 2)
        return running_sum + tile_block(targets, part_sources, part_strengths, kernel_scale)

    return lax.fori_loop(0, columns // block_width, block_step, carry_sum)


def add_pairs(earlier, later):
    return (earlier[0] + later[0], earlier[1] + later[1])


def shards_split(
    base_points,
    control_points,
    morph_weights,
    connectivity,
    free_flags,
    station_owner,
    variant_order,
    load_velocity,
):
    owners = lax.axis_size(("panels", "cols"))
    owner_index = lax.axis_index(("panels", "cols"))
    phase_index = lax.axis_index("phase")
    variant_dev = variant_order.shape[0] // lax.axis_size("phase")
    vert_dev = base_points.shape[1]
    pan_dev = connectivity.shape[1]
    load_count = load_velocity.shape[0]
    panels_total = pan_dev * owners
    own_variants = lax.dynamic_slice_in_dim(
        variant_order, phase_index * variant_dev, variant_dev, 0
    )
    picker = (
        own_variants[:, None] == jnp.arange(variant_order.shape[0], dtype=jnp.int32)[None, :]
    ).astype(jnp.float32)
    chosen = jnp.einsum("mv,vac->mac", picker, morph_weights, precision=HIGH)
    distance = (
        (control_points[0][:, None] - base_points[0][None, :]) ** 2
        + (control_points[1][:, None] - base_points[1][None, :]) ** 2
        + (control_points[2][:, None] - base_points[2][None, :]) ** 2
    )
    basis_values = lax.rsqrt(1.0 + distance)
    moved_points = base_points[None] + jnp.einsum(
        "mac,cn->man", chosen, basis_values, precision=HIGH
    )
    local_corners = connectivity - owner_index * vert_dev
    centroid, area, weight = panel_shape(moved_points, local_corners)
    hull_mask = (1 - free_flags).astype(jnp.float32)
    boundary = (
        jnp.einsum("ka,man->mkn", load_velocity, area, precision=HIGH) * hull_mask[None, None, :]
    )
    first_strengths = boundary.astype(jnp.bfloat16)
    kernel_scale = 1.0 / (4.0 * math.pi * math.sqrt(panels_total))
    own_geometry = jnp.concatenate([centroid, weight[:, None, :]], axis=1)
    sources = lax.all_gather(own_geometry, "panels", axis=2, tiled=True)
    row_targets = lax.all_gather(centroid, "cols", axis=2, tiled=True)

    def apply_influence(strengths):
        empty_sum = jnp.zeros((variant_dev, load_count, row_targets.shape[2]), jnp.float32)
        partial_sums = tile_product(
            empty_sum,
            row_targets,
            sources,
            lax.all_gather(strengths, "panels", axis=2, tiled=True),
            kernel_scale,
        )
        return lax.psum_scatter(partial_sums, "cols", scatter_dimension=2, tiled=True)

    induced = apply_influence(first_strengths)
    second_strengths = (first_strengths.astype(jnp.float32) + (boundary - induced)).astype(
        jnp.bfloat16
    )
    pressure = apply_influence(second_strengths)
    panel_force = pressure * (area[:, 2, :] * hull_mask[None, :])[:, None, :]
    force_rows = panel_force.reshape(-1, pan_dev)
    capacity = max(2, 5 * pan_dev // (2 * owners))
    target_owner = station_owner[:, 0]
    panel_order = jnp.arange(pan_dev, dtype=jnp.int32)
    ahead = (target_owner[:, None] == target_owner[None, :]) & (
        panel_order[None, :] < panel_order[:, None]
    )
    slot_rank = jnp.sum(ahead.astype(jnp.int32), axis=1)
    slot_index = target_owner * capacity + slot_rank
    all_slots = jnp.arange(owners * capacity, dtype=jnp.int32)
    placed = slot_index[:, None] == all_slots[None, :]
    send_values = jnp.dot(force_rows, placed.astype(jnp.float32), precision=HIGH)
    station_bins = (owner_index * pan_dev + panel_order) % STATIONS
    send_bins = jnp.max(jnp.where(placed, station_bins[:, None], -1), axis=0)[None, :]
    recv_values, recv_bins = (
        lax.all_to_all(send_values, ("panels", "cols"), split_axis=1, concat_axis=1, tiled=True),
        lax.all_to_all(send_bins, ("panels", "cols"), split_axis=1, concat_axis=1, tiled=True),
    )
    matches = (recv_bins[0][:, None] == jnp.arange(STATIONS, dtype=jnp.int32)[None, :]).astype(
        jnp.float32
    )
    station_loads = jnp.dot(recv_values, matches, precision=HIGH)
    station_place = (owner_index * STATIONS + jnp.arange(STATIONS, dtype=jnp.int32)).astype(
        jnp.float32
    ) / (STATIONS * owners)
    placed_loads = station_loads * station_place[None, :]
    own_total = jnp.sum(station_loads, axis=1)
    own_arm = jnp.sum(placed_loads, axis=1)
    zero_row = jnp.zeros_like(own_total)
    prior_total, prior_arm = prefix(
        (own_total, own_arm), ("panels", "cols"), add_pairs, (zero_row, zero_row)
    )
    station_rank = jnp.arange(STATIONS, dtype=jnp.int32)
    inclusive = (station_rank[:, None] <= station_rank[None, :]).astype(jnp.float32)
    strict = (station_rank[:, None] < station_rank[None, :]).astype(jnp.float32)
    running = prior_total[:, None] + jnp.dot(station_loads, inclusive, precision=HIGH)
    earlier = prior_total[:, None] + jnp.dot(station_loads, strict, precision=HIGH)
    moment_arm = prior_arm[:, None] + jnp.dot(placed_loads, strict, precision=HIGH)
    inv_root = 1.0 / math.sqrt(panels_total)
    shear = (running * inv_root).reshape(variant_dev, load_count, STATIONS)
    moment = ((station_place[None, :] * earlier - moment_arm) * inv_root).reshape(
        variant_dev, load_count, STATIONS
    )
    return (shear, moment)


def geometry_kernel(
    vert_dev,
    phases,
    order,
    kernel_scale,
    order_hbm,
    base_hbm,
    control_hbm,
    weights_hbm,
    corner_hbm,
    flags_hbm,
    owner_hbm,
    out_ref,
    order_ref,
    base_ref,
    control_ref,
    weights_ref,
    corner_ref,
    flags_ref,
    owner_ref,
    arrived,
):
    @pl.when(lax.axis_index("phase") == phases - 1)
    def _():
        sources = (
            weights_hbm,
            control_hbm,
            base_hbm,
            corner_hbm,
            flags_hbm,
            owner_hbm,
            order_hbm,
        )
        places = (
            weights_ref,
            control_ref,
            base_ref,
            corner_ref,
            flags_ref,
            owner_ref,
            order_ref,
        )
        copies = [
            pltpu.make_async_copy(source, place, arrived.at[k])
            for k, (source, place) in enumerate(zip(sources, places))
        ]
        for copy in copies:
            copy.start()
        for copy in copies:
            copy.wait()
        panel_rows(
            vert_dev,
            phases,
            order,
            kernel_scale,
            order_ref,
            base_ref,
            control_ref,
            weights_ref,
            corner_ref,
            flags_ref,
            owner_ref,
            out_ref,
        )


def panel_rows(
    vert_dev,
    phases,
    order,
    kernel_scale,
    order_ref,
    base_ref,
    control_ref,
    weights_ref,
    corner_ref,
    flags_ref,
    owner_ref,
    out_ref,
):
    pan_dev = corner_ref.shape[1]
    variants = weights_ref.shape[1]
    diagonal = lax.broadcasted_iota(jnp.int32, (vert_dev, vert_dev), 0) == lax.broadcasted_iota(
        jnp.int32, (vert_dev, vert_dev), 1
    )
    base = [
        jnp.sum(jnp.where(diagonal, base_ref[a : a + 1, :], 0.0), axis=1, keepdims=True)
        for a in range(3)
    ]
    totals = [[None] * 3 for _ in range(variants)]
    for start in range(0, control_ref.shape[1], LANES):
        part = pl.ds(start, LANES)
        distance = (
            (control_ref[0:1, part] - base[0]) ** 2
            + (control_ref[1:2, part] - base[1]) ** 2
            + (control_ref[2:3, part] - base[2]) ** 2
        )
        basis = lax.rsqrt(1.0 + distance)
        for v in range(variants):
            for a in range(3):
                term = weights_ref[a, v : v + 1, part] * basis
                totals[v][a] = term if start == 0 else totals[v][a] + term
    lane = lax.broadcasted_iota(jnp.int32, (vert_dev, LANES), 1)
    moved = []
    for a in range(3):
        shift = jnp.sum(totals[0][a], axis=1, keepdims=True)
        for v in range(1, variants):
            own = jnp.sum(totals[v][a], axis=1, keepdims=True)
            shift = jnp.where(lane >= v * pan_dev, own, shift)
        moved.append(base[a] + shift)

    def repeated(row):
        return jnp.concatenate([row] * variants, axis=1)

    vertex = lax.broadcasted_iota(jnp.int32, (vert_dev, LANES), 0)
    corners = []
    for k in range(3):
        chosen = vertex == lax.rem(repeated(corner_ref[k : k + 1, :]), vert_dev)
        corners.append(
            [jnp.sum(jnp.where(chosen, moved[a], 0.0), axis=0, keepdims=True) for a in range(3)]
        )
    first, second, third = corners
    centroid = [(first[a] + second[a] + third[a]) * (1.0 / 3.0) for a in range(3)]
    one = [second[a] - first[a] for a in range(3)]
    two = [third[a] - first[a] for a in range(3)]
    area = [
        0.5 * (one[1] * two[2] - one[2] * two[1]),
        0.5 * (one[2] * two[0] - one[0] * two[2]),
        0.5 * (one[0] * two[1] - one[1] * two[0]),
    ]
    weight = (
        jnp.sqrt(area[0] * area[0] + area[1] * area[1] + area[2] * area[2] + SKIN_SQUARE)
        * kernel_scale
    )
    hull = (1 - repeated(flags_ref[...])).astype(jnp.float32)
    owner = repeated(owner_ref[...]).astype(jnp.float32)
    rows = centroid + [weight] + [hull * area[a] for a in range(3)] + [owner]
    height = out_ref.shape[1]
    shared = LANES // pan_dev
    pieces = [jnp.concatenate(rows[k : k + height], axis=0) for k in range(0, len(rows), height)]
    turned = [
        [pltpu.roll(piece, t * pan_dev, 1) if t else piece for t in range(shared)]
        for piece in pieces
    ]
    lane = lax.broadcasted_iota(jnp.int32, (height, LANES), 1)
    row = lax.broadcasted_iota(jnp.int32, (height, LANES), 0)
    cols = lax.axis_size("cols")
    place_here = (lax.axis_index("panels") * cols + lax.axis_index("cols")) % shared
    begin = (place_here + shared - 1) % shared * pan_dev
    last = (row == height - 1) & (lane >= begin) & (lane < begin + pan_dev)
    blocks = [None] * variants
    for h in range(shared):
        slots = [(k + h) % shared for k in range(shared)]
        for v in range(variants):
            block = turned[slots.index(0)][-v % shared]
            for slot in range(1, shared):
                piece = turned[slots.index(slot)][(slot - v) % shared]
                block = jnp.where(lane >= slot * pan_dev, piece, block)
            blocks[v] = block if h == 0 else jnp.where(place_here == h, block, blocks[v])
    for slot in range(phases):
        block = blocks[0]
        for v in range(1, variants):
            block = jnp.where(order_ref[slot] == v, blocks[v], block)
        for place, member in enumerate(order):
            if member % phases == slot:
                out_ref[place] = jnp.where(last, block - float(member // phases), block)


def in_parts(values):
    high = values.astype(jnp.bfloat16).astype(jnp.float32)
    rest = values - high
    middle = rest.astype(jnp.bfloat16).astype(jnp.float32)
    return high, middle, rest - middle


def dot_rows(left, right):
    return lax.dot_general(
        left.astype(jnp.bfloat16),
        right.astype(jnp.bfloat16),
        (((0,), (0,)), ((), ())),
        preferred_element_type=jnp.float32,
    )


def spread_matrix():
    spread = np.zeros((16, 4 * LANES), np.float32)
    for row in range(12):
        spread[row, row % 4 * LANES : (row % 4 + 1) * LANES] = 1.0
    return spread


def loads_kernel(
    pan_dev,
    places,
    rows_ref,
    velocity_ref,
    spread_ref,
    shear_ref,
    moment_ref,
):
    owners = len(places)
    shared = LANES // pan_dev
    tiles = owners // shared
    panels_total = owners * pan_dev
    load_count = velocity_ref.shape[1]
    height = rows_ref.shape[1]
    lane = lax.broadcasted_iota(jnp.int32, (height, LANES), 1)
    panels = []
    for q in range(tiles):
        blocks = [rows_ref[places[q * shared + h]] for h in range(shared)]
        pieces = []
        for k in range(shared):
            piece = blocks[-k % shared]
            for slot in range(1, shared):
                piece = jnp.where(lane >= slot * pan_dev, blocks[(slot - k) % shared], piece)
            pieces.append(pltpu.roll(piece, LANES - k * pan_dev, 1) if k else piece)
        panels.append(pieces)

    def tile_rows(q, begin, end):
        if height < end - begin:
            return jnp.concatenate(panels[q][begin // height : end // height], axis=0)
        return panels[q][begin // height][begin % height : begin % height + end - begin, :]

    centres = [tile_rows(q, 0, 4) for q in range(tiles)]
    areas = [tile_rows(q, 4, 8) for q in range(tiles)]
    high, middle, low = in_parts(jnp.concatenate(centres, axis=1))
    columns = dot_rows(
        jnp.concatenate([high, middle, low, jnp.zeros_like(low)], axis=0), spread_ref[...]
    )
    influences = {}
    for source in range(tiles):
        for target in range(source, tiles):
            tile = centres[target]
            column = columns[source * LANES : (source + 1) * LANES, :]
            column = [column[:, a * LANES : (a + 1) * LANES] for a in range(4)]
            inverse = lax.rsqrt(
                (tile[0:1, :] - column[0]) ** 2
                + (tile[1:2, :] - column[1]) ** 2
                + (tile[2:3, :] - column[2]) ** 2
                + CORE_SQUARE
            )
            influences[source, target] = (column[3] * inverse).astype(jnp.bfloat16)
            if target != source:
                other = columns[target * LANES : (target + 1) * LANES, 3 * LANES :]
                influences[target, source] = (other * inverse.T).astype(jnp.bfloat16)
    area_parts = in_parts(jnp.concatenate(areas, axis=1))
    velocity_parts = in_parts(
        jnp.concatenate([velocity_ref[...], jnp.zeros((1, load_count), jnp.float32)], axis=0)
    )
    pairs = ((0, 0), (0, 1), (1, 0), (1, 1), (0, 2), (2, 0), (1, 2), (2, 1))
    boundary = dot_rows(
        jnp.concatenate([velocity_parts[k] for k, _ in pairs], axis=0),
        jnp.concatenate([area_parts[k] for _, k in pairs], axis=0),
    )
    first = boundary.astype(jnp.bfloat16)
    influence = jnp.concatenate(
        [
            jnp.concatenate([influences[q, p] for p in range(tiles)], axis=1)
            for q in range(tiles)
        ],
        axis=0,
    )
    induced = jnp.dot(first, influence, preferred_element_type=jnp.float32)
    second = (first.astype(jnp.float32) + (boundary - induced)).astype(jnp.bfloat16)
    pressure = jnp.dot(second, influence, preferred_element_type=jnp.float32)
    stations_all = STATIONS * owners
    inv_root = 1.0 / math.sqrt(panels_total)
    rank = lax.broadcasted_iota(jnp.int32, (1, LANES), 1).astype(jnp.float32)
    own_loads, prior_loads, prior_arms = None, None, None
    for q, tile in enumerate(areas):
        pushed = pressure[:, q * LANES : (q + 1) * LANES]
        area = tile[2:3, :] * inv_root
        owner = tile[3:4, :]
        prior = jnp.where(owner < 0.0, area, 0.0)
        place = (owner * STATIONS + rank) * (1.0 / stations_all)
        own_load = pushed * jnp.where(owner == 0.0, area, 0.0)
        prior_load = pushed * prior
        prior_arm = pushed * (prior * place)
        own_loads = own_load if q == 0 else own_loads + own_load
        prior_loads = prior_load if q == 0 else prior_loads + prior_load
        prior_arms = prior_arm if q == 0 else prior_arms + prior_arm
    prior_total = jnp.sum(prior_loads, axis=1, keepdims=True)
    prior_arm = jnp.sum(prior_arms, axis=1, keepdims=True)
    station = lax.broadcasted_iota(jnp.int32, (STATIONS, 2 * STATIONS), 0)
    place = lax.broadcasted_iota(jnp.int32, (STATIONS, 2 * STATIONS), 1)
    arm = place - STATIONS - station
    steps = jnp.where(
        place < STATIONS, (station <= place).astype(jnp.int32), jnp.maximum(arm, 0)
    ).astype(jnp.float32).astype(jnp.bfloat16)
    high = own_loads.astype(jnp.bfloat16)
    rest = own_loads - high.astype(jnp.float32)
    middle = rest.astype(jnp.bfloat16)
    low = (rest - middle.astype(jnp.float32)).astype(jnp.bfloat16)
    sums = jnp.dot(
        jnp.concatenate([high, middle, low], axis=1),
        jnp.concatenate([steps] * 3, axis=0),
        preferred_element_type=jnp.float32,
    )
    shear_ref[0] = prior_total + sums[:, :STATIONS]
    moment_ref[0] = (
        (rank * (1.0 / stations_all)) * prior_total
        - prior_arm
        + sums[:, STATIONS:] * (1.0 / stations_all)
    )


def shards_whole(
    base_points,
    control_points,
    morph_weights,
    connectivity,
    free_flags,
    station_owner,
    variant_order,
    load_velocity,
):
    owners = lax.axis_size(("panels", "cols"))
    vert_dev = base_points.shape[1]
    pan_dev = connectivity.shape[1]
    load_count = load_velocity.shape[0]
    panels_total = pan_dev * owners
    phases = lax.axis_size("phase")
    members = owners * phases
    variants = morph_weights.shape[0]
    control = control_points.shape[1]
    height = 8 * pan_dev // LANES
    head = (owners - 1) * phases
    order = [head] + [member for member in range(members) if member != head]
    kernel_scale = 1.0 / (4.0 * math.pi * math.sqrt(panels_total))
    vmem = pl.BlockSpec(memory_space=pltpu.VMEM)
    anywhere = pl.BlockSpec(memory_space=pl.ANY)
    rows = pl.pallas_call(
        functools.partial(geometry_kernel, vert_dev, phases, order, kernel_scale),
        out_shape=pltpu.VMEM((members, height, LANES), jnp.float32),
        in_specs=[anywhere] * 7,
        out_specs=vmem,
        scratch_shapes=[
            pltpu.SMEM((variants,), jnp.int32),
            pltpu.VMEM((3, vert_dev), jnp.float32),
            pltpu.VMEM((3, control), jnp.float32),
            pltpu.VMEM((3, variants, control), jnp.float32),
            pltpu.VMEM((3, pan_dev), jnp.int32),
            pltpu.VMEM((1, pan_dev), jnp.int32),
            pltpu.VMEM((1, pan_dev), jnp.int32),
            pltpu.SemaphoreType.DMA((7,)),
        ],
        name="geometry",
    )(
        variant_order,
        base_points,
        control_points,
        morph_weights.transpose(1, 0, 2),
        connectivity,
        free_flags.reshape(1, pan_dev),
        station_owner.reshape(1, pan_dev),
    )
    rows = lax.all_to_all(
        rows, ("panels", "cols", "phase"), split_axis=0, concat_axis=0, axis_index_groups=[order]
    )
    places = [order.index(owner * phases + phases - 1) for owner in range(owners)]
    out = jax.ShapeDtypeStruct((1, load_count, STATIONS), jnp.float32)
    return pl.pallas_call(
        functools.partial(loads_kernel, pan_dev, places),
        out_shape=(out, out),
        in_specs=[vmem] * 3,
        out_specs=(vmem, vmem),
        compiler_params=pltpu.CompilerParams(vmem_limit_bytes=32 * 1024 * 1024),
        name="loads",
    )(
        rows,
        load_velocity.T,
        jnp.asarray(spread_matrix(), jnp.bfloat16),
    )


def shards(
    base_points,
    control_points,
    morph_weights,
    connectivity,
    free_flags,
    station_owner,
    variant_order,
    load_velocity,
):
    owners = lax.axis_size(("panels", "cols"))
    pan_dev = connectivity.shape[1]
    panels_total = owners * pan_dev
    whole = (
        panels_total <= PANELS_ON_ONE
        and panels_total % LANES == 0
        and LANES % pan_dev == 0
        and 8 * pan_dev % LANES == 0
        and STATIONS == LANES
        and variant_order.shape[0] == lax.axis_size("phase")
        and morph_weights.shape[0] * pan_dev == LANES
        and control_points.shape[1] % LANES == 0
        and load_velocity.shape[0] % 16 == 0
    )
    return (shards_whole if whole else shards_split)(
        base_points,
        control_points,
        morph_weights,
        connectivity,
        free_flags,
        station_owner,
        variant_order,
        load_velocity,
    )


def solution(mesh):
    return jax.shard_map(
        shards,
        mesh=mesh,
        in_specs=(
            P(None, ("groups", "panels", "cols")),
            P(),
            P("groups", None, None),
            P(None, ("groups", "panels", "cols")),
            P(("groups", "panels", "cols")),
            P(("groups", "panels", "cols"), None),
            P("groups"),
            P(),
        ),
        out_specs=(
            P(("groups", "phase"), None, ("panels", "cols")),
            P(("groups", "phase"), None, ("panels", "cols")),
        ),
        check_vma=False,
    )
```

```python
import functools
import math

import jax
import jax.numpy as jnp
import numpy as np
from jax import lax
from jax.experimental import pallas as pl
from jax.experimental.pallas import tpu as pltpu
from jax.sharding import PartitionSpec as P

STATIONS = 128
LANES = 128
PANELS_ON_ONE = 1024


HIGH = lax.Precision.HIGHEST
CORE_SQUARE = 0.0025
SKIN_SQUARE = 0.01


def prefix(shard, axis, combine, identity):
    length, index = (lax.axis_size(axis), lax.axis_index(axis))
    everything = jax.tree.map(lambda part: lax.all_gather(part, axis), shard)
    start = jax.tree.map(
        lambda part, zero: jnp.broadcast_to(jnp.asarray(zero, part.dtype), part.shape),
        shard,
        identity,
    )

    def step(k, before):
        reached = k < index
        new = combine(before, jax.tree.map(lambda part: part[k], everything))
        return jax.tree.map(lambda a, b: jnp.where(reached, a, b), new, before)

    return lax.fori_loop(0, length, step, start)


def panel_shape(moved_points, corner_rows):
    first_corner = jnp.take(moved_points, corner_rows[0], axis=2)
    second_corner = jnp.take(moved_points, corner_rows[1], axis=2)
    third_corner = jnp.take(moved_points, corner_rows[2], axis=2)
    centroid = (first_corner + second_corner + third_corner) / 3.0
    edge_one = second_corner - first_corner
    edge_two = third_corner - first_corner
    cross_x = edge_one[:, 1] * edge_two[:, 2] - edge_one[:, 2] * edge_two[:, 1]
    cross_y = edge_one[:, 2] * edge_two[:, 0] - edge_one[:, 0] * edge_two[:, 2]
    cross_z = edge_one[:, 0] * edge_two[:, 1] - edge_one[:, 1] * edge_two[:, 0]
    area = 0.5 * jnp.stack([cross_x, cross_y, cross_z], axis=1)
    weight = jnp.sqrt(jnp.sum(area * area, axis=1) + SKIN_SQUARE)
    return (centroid, area, weight)


def tile_block(targets, sources, strengths, kernel_scale):
    distance = (
        (targets[:, 0, :, None] - sources[:, 0, None, :]) ** 2
        + (targets[:, 1, :, None] - sources[:, 1, None, :]) ** 2
        + (targets[:, 2, :, None] - sources[:, 2, None, :]) ** 2
    )
    influence = (sources[:, 3, None, :] * kernel_scale * lax.rsqrt(distance + CORE_SQUARE)).astype(
        jnp.bfloat16
    )
    return jnp.einsum("mrn,mkn->mkr", influence, strengths, preferred_element_type=jnp.float32)


def tile_product(carry_sum, targets, sources, strengths, kernel_scale):
    columns = strengths.shape[2]
    block_width = columns
    for candidate in (2048, 1024, 512):
        if columns > candidate and columns % candidate == 0:
            block_width = candidate
            break
    if block_width == columns:
        return carry_sum + tile_block(targets, sources, strengths, kernel_scale)

    def block_step(step_index, running_sum):
        column_start = step_index * block_width
        part_sources = lax.dynamic_slice_in_dim(sources, column_start, block_width, 2)
        part_strengths = lax.dynamic_slice_in_dim(strengths, column_start, block_width, 2)
        return running_sum + tile_block(targets, part_sources, part_strengths, kernel_scale)

    return lax.fori_loop(0, columns // block_width, block_step, carry_sum)


def add_pairs(earlier, later):
    return (earlier[0] + later[0], earlier[1] + later[1])


def shards_split(
    base_points,
    control_points,
    morph_weights,
    connectivity,
    free_flags,
    station_owner,
    variant_order,
    load_velocity,
):
    owners = lax.axis_size(("panels", "cols"))
    owner_index = lax.axis_index(("panels", "cols"))
    phase_index = lax.axis_index("phase")
    variant_dev = variant_order.shape[0] // lax.axis_size("phase")
    vert_dev = base_points.shape[1]
    pan_dev = connectivity.shape[1]
    load_count = load_velocity.shape[0]
    panels_total = pan_dev * owners
    own_variants = lax.dynamic_slice_in_dim(
        variant_order, phase_index * variant_dev, variant_dev, 0
    )
    picker = (
        own_variants[:, None] == jnp.arange(variant_order.shape[0], dtype=jnp.int32)[None, :]
    ).astype(jnp.float32)
    chosen = jnp.einsum("mv,vac->mac", picker, morph_weights, precision=HIGH)
    distance = (
        (control_points[0][:, None] - base_points[0][None, :]) ** 2
        + (control_points[1][:, None] - base_points[1][None, :]) ** 2
        + (control_points[2][:, None] - base_points[2][None, :]) ** 2
    )
    basis_values = lax.rsqrt(1.0 + distance)
    moved_points = base_points[None] + jnp.einsum(
        "mac,cn->man", chosen, basis_values, precision=HIGH
    )
    local_corners = connectivity - owner_index * vert_dev
    centroid, area, weight = panel_shape(moved_points, local_corners)
    hull_mask = (1 - free_flags).astype(jnp.float32)
    boundary = (
        jnp.einsum("ka,man->mkn", load_velocity, area, precision=HIGH) * hull_mask[None, None, :]
    )
    first_strengths = boundary.astype(jnp.bfloat16)
    kernel_scale = 1.0 / (4.0 * math.pi * math.sqrt(panels_total))
    own_geometry = jnp.concatenate([centroid, weight[:, None, :]], axis=1)
    sources = lax.all_gather(own_geometry, "panels", axis=2, tiled=True)
    row_targets = lax.all_gather(centroid, "cols", axis=2, tiled=True)

    def apply_influence(strengths):
        empty_sum = jnp.zeros((variant_dev, load_count, row_targets.shape[2]), jnp.float32)
        partial_sums = tile_product(
            empty_sum,
            row_targets,
            sources,
            lax.all_gather(strengths, "panels", axis=2, tiled=True),
            kernel_scale,
        )
        return lax.psum_scatter(partial_sums, "cols", scatter_dimension=2, tiled=True)

    induced = apply_influence(first_strengths)
    second_strengths = (first_strengths.astype(jnp.float32) + (boundary - induced)).astype(
        jnp.bfloat16
    )
    pressure = apply_influence(second_strengths)
    panel_force = pressure * (area[:, 2, :] * hull_mask[None, :])[:, None, :]
    force_rows = panel_force.reshape(-1, pan_dev)
    capacity = max(2, 5 * pan_dev // (2 * owners))
    target_owner = station_owner[:, 0]
    panel_order = jnp.arange(pan_dev, dtype=jnp.int32)
    ahead = (target_owner[:, None] == target_owner[None, :]) & (
        panel_order[None, :] < panel_order[:, None]
    )
    slot_rank = jnp.sum(ahead.astype(jnp.int32), axis=1)
    slot_index = target_owner * capacity + slot_rank
    all_slots = jnp.arange(owners * capacity, dtype=jnp.int32)
    placed = slot_index[:, None] == all_slots[None, :]
    send_values = jnp.dot(force_rows, placed.astype(jnp.float32), precision=HIGH)
    station_bins = (owner_index * pan_dev + panel_order) % STATIONS
    send_bins = jnp.max(jnp.where(placed, station_bins[:, None], -1), axis=0)[None, :]
    recv_values, recv_bins = (
        lax.all_to_all(send_values, ("panels", "cols"), split_axis=1, concat_axis=1, tiled=True),
        lax.all_to_all(send_bins, ("panels", "cols"), split_axis=1, concat_axis=1, tiled=True),
    )
    matches = (recv_bins[0][:, None] == jnp.arange(STATIONS, dtype=jnp.int32)[None, :]).astype(
        jnp.float32
    )
    station_loads = jnp.dot(recv_values, matches, precision=HIGH)
    station_place = (owner_index * STATIONS + jnp.arange(STATIONS, dtype=jnp.int32)).astype(
        jnp.float32
    ) / (STATIONS * owners)
    placed_loads = station_loads * station_place[None, :]
    own_total = jnp.sum(station_loads, axis=1)
    own_arm = jnp.sum(placed_loads, axis=1)
    zero_row = jnp.zeros_like(own_total)
    prior_total, prior_arm = prefix(
        (own_total, own_arm), ("panels", "cols"), add_pairs, (zero_row, zero_row)
    )
    station_rank = jnp.arange(STATIONS, dtype=jnp.int32)
    inclusive = (station_rank[:, None] <= station_rank[None, :]).astype(jnp.float32)
    strict = (station_rank[:, None] < station_rank[None, :]).astype(jnp.float32)
    running = prior_total[:, None] + jnp.dot(station_loads, inclusive, precision=HIGH)
    earlier = prior_total[:, None] + jnp.dot(station_loads, strict, precision=HIGH)
    moment_arm = prior_arm[:, None] + jnp.dot(placed_loads, strict, precision=HIGH)
    inv_root = 1.0 / math.sqrt(panels_total)
    shear = (running * inv_root).reshape(variant_dev, load_count, STATIONS)
    moment = ((station_place[None, :] * earlier - moment_arm) * inv_root).reshape(
        variant_dev, load_count, STATIONS
    )
    return (shear, moment)


def geometry_kernel(
    vert_dev,
    phases,
    order,
    kernel_scale,
    order_hbm,
    base_hbm,
    control_hbm,
    weights_hbm,
    corner_hbm,
    flags_hbm,
    owner_hbm,
    out_ref,
    order_ref,
    base_ref,
    control_ref,
    weights_ref,
    corner_ref,
    flags_ref,
    owner_ref,
    arrived,
):
    @pl.when(lax.axis_index("phase") == phases - 1)
    def _():
        sources = (
            weights_hbm,
            control_hbm,
            base_hbm,
            corner_hbm,
            flags_hbm,
            owner_hbm,
            order_hbm,
        )
        places = (
            weights_ref,
            control_ref,
            base_ref,
            corner_ref,
            flags_ref,
            owner_ref,
            order_ref,
        )
        copies = [
            pltpu.make_async_copy(source, place, arrived.at[k])
            for k, (source, place) in enumerate(zip(sources, places))
        ]
        for copy in copies:
            copy.start()
        for copy in copies:
            copy.wait()
        panel_rows(
            vert_dev,
            phases,
            order,
            kernel_scale,
            order_ref,
            base_ref,
            control_ref,
            weights_ref,
            corner_ref,
            flags_ref,
            owner_ref,
            out_ref,
        )


def panel_rows(
    vert_dev,
    phases,
    order,
    kernel_scale,
    order_ref,
    base_ref,
    control_ref,
    weights_ref,
    corner_ref,
    flags_ref,
    owner_ref,
    out_ref,
):
    pan_dev = corner_ref.shape[1]
    variants = weights_ref.shape[1]
    diagonal = lax.broadcasted_iota(jnp.int32, (vert_dev, vert_dev), 0) == lax.broadcasted_iota(
        jnp.int32, (vert_dev, vert_dev), 1
    )
    base = [
        jnp.sum(jnp.where(diagonal, base_ref[a : a + 1, :], 0.0), axis=1, keepdims=True)
        for a in range(3)
    ]
    totals = [[None] * 3 for _ in range(variants)]
    for start in range(0, control_ref.shape[1], LANES):
        part = pl.ds(start, LANES)
        distance = (
            (control_ref[0:1, part] - base[0]) ** 2
            + (control_ref[1:2, part] - base[1]) ** 2
            + (control_ref[2:3, part] - base[2]) ** 2
        )
        basis = lax.rsqrt(1.0 + distance)
        for v in range(variants):
            for a in range(3):
                term = weights_ref[a, v : v + 1, part] * basis
                totals[v][a] = term if start == 0 else totals[v][a] + term
    lane = lax.broadcasted_iota(jnp.int32, (vert_dev, LANES), 1)
    moved = []
    for a in range(3):
        shift = jnp.sum(totals[0][a], axis=1, keepdims=True)
        for v in range(1, variants):
            own = jnp.sum(totals[v][a], axis=1, keepdims=True)
            shift = jnp.where(lane >= v * pan_dev, own, shift)
        moved.append(base[a] + shift)

    def repeated(row):
        return jnp.concatenate([row] * variants, axis=1)

    vertex = lax.broadcasted_iota(jnp.int32, (vert_dev, LANES), 0)
    corners = []
    for k in range(3):
        chosen = vertex == lax.rem(repeated(corner_ref[k : k + 1, :]), vert_dev)
        corners.append(
            [jnp.sum(jnp.where(chosen, moved[a], 0.0), axis=0, keepdims=True) for a in range(3)]
        )
    first, second, third = corners
    centroid = [(first[a] + second[a] + third[a]) * (1.0 / 3.0) for a in range(3)]
    one = [second[a] - first[a] for a in range(3)]
    two = [third[a] - first[a] for a in range(3)]
    area = [
        0.5 * (one[1] * two[2] - one[2] * two[1]),
        0.5 * (one[2] * two[0] - one[0] * two[2]),
        0.5 * (one[0] * two[1] - one[1] * two[0]),
    ]
    weight = (
        jnp.sqrt(area[0] * area[0] + area[1] * area[1] + area[2] * area[2] + SKIN_SQUARE)
        * kernel_scale
    )
    hull = (1 - repeated(flags_ref[...])).astype(jnp.float32)
    owner = repeated(owner_ref[...]).astype(jnp.float32)
    rows = centroid + [weight] + [hull * area[a] for a in range(3)] + [owner]
    height = out_ref.shape[1]
    shared = LANES // pan_dev
    pieces = [jnp.concatenate(rows[k : k + height], axis=0) for k in range(0, len(rows), height)]
    turned = [
        [pltpu.roll(piece, t * pan_dev, 1) if t else piece for t in range(shared)]
        for piece in pieces
    ]
    lane = lax.broadcasted_iota(jnp.int32, (height, LANES), 1)
    row = lax.broadcasted_iota(jnp.int32, (height, LANES), 0)
    cols = lax.axis_size("cols")
    place_here = (lax.axis_index("panels") * cols + lax.axis_index("cols")) % shared
    begin = (place_here + shared - 1) % shared * pan_dev
    last = (row == height - 1) & (lane >= begin) & (lane < begin + pan_dev)
    blocks = [None] * variants
    for h in range(shared):
        slots = [(k + h) % shared for k in range(shared)]
        for v in range(variants):
            block = turned[slots.index(0)][-v % shared]
            for slot in range(1, shared):
                piece = turned[slots.index(slot)][(slot - v) % shared]
                block = jnp.where(lane >= slot * pan_dev, piece, block)
            blocks[v] = block if h == 0 else jnp.where(place_here == h, block, blocks[v])
    for slot in range(phases):
        block = blocks[0]
        for v in range(1, variants):
            block = jnp.where(order_ref[slot] == v, blocks[v], block)
        for place, member in enumerate(order):
            if member % phases == slot:
                out_ref[place] = jnp.where(last, block - float(member // phases), block)


def in_parts(values):
    high = values.astype(jnp.bfloat16).astype(jnp.float32)
    rest = values - high
    middle = rest.astype(jnp.bfloat16).astype(jnp.float32)
    return high, middle, rest - middle


def dot_rows(left, right):
    return lax.dot_general(
        left.astype(jnp.bfloat16),
        right.astype(jnp.bfloat16),
        (((0,), (0,)), ((), ())),
        preferred_element_type=jnp.float32,
    )


def spread_matrix():
    spread = np.zeros((16, 4 * LANES), np.float32)
    for row in range(12):
        spread[row, row % 4 * LANES : (row % 4 + 1) * LANES] = 1.0
    return spread


def loads_kernel(
    pan_dev,
    places,
    rows_ref,
    velocity_ref,
    spread_ref,
    shear_ref,
    moment_ref,
):
    owners = len(places)
    shared = LANES // pan_dev
    tiles = owners // shared
    panels_total = owners * pan_dev
    load_count = velocity_ref.shape[1]
    height = rows_ref.shape[1]
    lane = lax.broadcasted_iota(jnp.int32, (height, LANES), 1)
    panels = []
    for q in range(tiles):
        blocks = [rows_ref[places[q * shared + h]] for h in range(shared)]
        pieces = []
        for k in range(shared):
            piece = blocks[-k % shared]
            for slot in range(1, shared):
                piece = jnp.where(lane >= slot * pan_dev, blocks[(slot - k) % shared], piece)
            pieces.append(pltpu.roll(piece, LANES - k * pan_dev, 1) if k else piece)
        panels.append(pieces)

    def tile_rows(q, begin, end):
        if height < end - begin:
            return jnp.concatenate(panels[q][begin // height : end // height], axis=0)
        return panels[q][begin // height][begin % height : begin % height + end - begin, :]

    centres = [tile_rows(q, 0, 4) for q in range(tiles)]
    areas = [tile_rows(q, 4, 8) for q in range(tiles)]
    high, middle, low = in_parts(jnp.concatenate(centres, axis=1))
    columns = dot_rows(
        jnp.concatenate([high, middle, low, jnp.zeros_like(low)], axis=0), spread_ref[...]
    )
    influences = {}
    for target in range(tiles):
        for source in range(target + 1):
            tile = centres[target]
            column = columns[source * LANES : (source + 1) * LANES, :]
            column = [column[:, a * LANES : (a + 1) * LANES] for a in range(4)]
            inverse = lax.rsqrt(
                (tile[0:1, :] - column[0]) ** 2
                + (tile[1:2, :] - column[1]) ** 2
                + (tile[2:3, :] - column[2]) ** 2
                + CORE_SQUARE
            )
            influences[source, target] = (column[3] * inverse).astype(jnp.bfloat16)
            if target != source:
                other = columns[target * LANES : (target + 1) * LANES, 3 * LANES :]
                influences[target, source] = (other * inverse.T).astype(jnp.bfloat16)
    area_parts = in_parts(jnp.concatenate(areas, axis=1))
    velocity_parts = in_parts(
        jnp.concatenate([velocity_ref[...], jnp.zeros((1, load_count), jnp.float32)], axis=0)
    )
    pairs = ((0, 0), (0, 1), (1, 0), (1, 1), (0, 2), (2, 0), (1, 2), (2, 1))
    boundary = dot_rows(
        jnp.concatenate([velocity_parts[k] for k, _ in pairs], axis=0),
        jnp.concatenate([area_parts[k] for _, k in pairs], axis=0),
    )
    first = boundary.astype(jnp.bfloat16)
    influence = jnp.concatenate(
        [
            jnp.concatenate([influences[q, p] for p in range(tiles)], axis=1)
            for q in range(tiles)
        ],
        axis=0,
    )
    induced = jnp.dot(first, influence, preferred_element_type=jnp.float32)
    second = (first.astype(jnp.float32) + (boundary - induced)).astype(jnp.bfloat16)
    pressure = jnp.dot(second, influence, preferred_element_type=jnp.float32)
    stations_all = STATIONS * owners
    inv_root = 1.0 / math.sqrt(panels_total)
    rank = lax.broadcasted_iota(jnp.int32, (1, LANES), 1).astype(jnp.float32)
    own_loads, prior_loads, prior_arms = None, None, None
    for q, tile in enumerate(areas):
        pushed = pressure[:, q * LANES : (q + 1) * LANES]
        area = tile[2:3, :] * inv_root
        owner = tile[3:4, :]
        prior = jnp.where(owner < 0.0, area, 0.0)
        place = (owner * STATIONS + rank) * (1.0 / stations_all)
        own_load = pushed * jnp.where(owner == 0.0, area, 0.0)
        prior_load = pushed * prior
        prior_arm = pushed * (prior * place)
        own_loads = own_load if q == 0 else own_loads + own_load
        prior_loads = prior_load if q == 0 else prior_loads + prior_load
        prior_arms = prior_arm if q == 0 else prior_arms + prior_arm
    prior_total = jnp.sum(prior_loads, axis=1, keepdims=True)
    prior_arm = jnp.sum(prior_arms, axis=1, keepdims=True)
    station = lax.broadcasted_iota(jnp.int32, (STATIONS, 2 * STATIONS), 0)
    place = lax.broadcasted_iota(jnp.int32, (STATIONS, 2 * STATIONS), 1)
    arm = place - STATIONS - station
    steps = jnp.where(
        place < STATIONS, (station <= place).astype(jnp.int32), jnp.maximum(arm, 0)
    ).astype(jnp.float32).astype(jnp.bfloat16)
    high = own_loads.astype(jnp.bfloat16)
    rest = own_loads - high.astype(jnp.float32)
    middle = rest.astype(jnp.bfloat16)
    low = (rest - middle.astype(jnp.float32)).astype(jnp.bfloat16)
    sums = jnp.dot(
        jnp.concatenate([high, middle, low], axis=1),
        jnp.concatenate([steps] * 3, axis=0),
        preferred_element_type=jnp.float32,
    )
    shear_ref[0] = prior_total + sums[:, :STATIONS]
    moment_ref[0] = (
        (rank * (1.0 / stations_all)) * prior_total
        - prior_arm
        + sums[:, STATIONS:] * (1.0 / stations_all)
    )


def shards_whole(
    base_points,
    control_points,
    morph_weights,
    connectivity,
    free_flags,
    station_owner,
    variant_order,
    load_velocity,
):
    owners = lax.axis_size(("panels", "cols"))
    vert_dev = base_points.shape[1]
    pan_dev = connectivity.shape[1]
    load_count = load_velocity.shape[0]
    panels_total = pan_dev * owners
    phases = lax.axis_size("phase")
    members = owners * phases
    variants = morph_weights.shape[0]
    control = control_points.shape[1]
    height = 8 * pan_dev // LANES
    head = (owners - 1) * phases
    order = [head] + [member for member in range(members) if member != head]
    kernel_scale = 1.0 / (4.0 * math.pi * math.sqrt(panels_total))
    vmem = pl.BlockSpec(memory_space=pltpu.VMEM)
    anywhere = pl.BlockSpec(memory_space=pl.ANY)
    rows = pl.pallas_call(
        functools.partial(geometry_kernel, vert_dev, phases, order, kernel_scale),
        out_shape=pltpu.VMEM((members, height, LANES), jnp.float32),
        in_specs=[anywhere] * 7,
        out_specs=vmem,
        scratch_shapes=[
            pltpu.SMEM((variants,), jnp.int32),
            pltpu.VMEM((3, vert_dev), jnp.float32),
            pltpu.VMEM((3, control), jnp.float32),
            pltpu.VMEM((3, variants, control), jnp.float32),
            pltpu.VMEM((3, pan_dev), jnp.int32),
            pltpu.VMEM((1, pan_dev), jnp.int32),
            pltpu.VMEM((1, pan_dev), jnp.int32),
            pltpu.SemaphoreType.DMA((7,)),
        ],
        name="geometry",
    )(
        variant_order,
        base_points,
        control_points,
        morph_weights.transpose(1, 0, 2),
        connectivity,
        free_flags.reshape(1, pan_dev),
        station_owner.reshape(1, pan_dev),
    )
    rows = lax.all_to_all(
        rows, ("panels", "cols", "phase"), split_axis=0, concat_axis=0, axis_index_groups=[order]
    )
    places = [order.index(owner * phases + phases - 1) for owner in range(owners)]
    out = jax.ShapeDtypeStruct((1, load_count, STATIONS), jnp.float32)
    return pl.pallas_call(
        functools.partial(loads_kernel, pan_dev, places),
        out_shape=(out, out),
        in_specs=[vmem] * 3,
        out_specs=(vmem, vmem),
        compiler_params=pltpu.CompilerParams(vmem_limit_bytes=32 * 1024 * 1024),
        name="loads",
    )(
        rows,
        load_velocity.T,
        jnp.asarray(spread_matrix(), jnp.bfloat16),
    )


def shards(
    base_points,
    control_points,
    morph_weights,
    connectivity,
    free_flags,
    station_owner,
    variant_order,
    load_velocity,
):
    owners = lax.axis_size(("panels", "cols"))
    pan_dev = connectivity.shape[1]
    panels_total = owners * pan_dev
    whole = (
        panels_total <= PANELS_ON_ONE
        and panels_total % LANES == 0
        and LANES % pan_dev == 0
        and 8 * pan_dev % LANES == 0
        and STATIONS == LANES
        and variant_order.shape[0] == lax.axis_size("phase")
        and morph_weights.shape[0] * pan_dev == LANES
        and control_points.shape[1] % LANES == 0
        and load_velocity.shape[0] % 16 == 0
    )
    return (shards_whole if whole else shards_split)(
        base_points,
        control_points,
        morph_weights,
        connectivity,
        free_flags,
        station_owner,
        variant_order,
        load_velocity,
    )


def solution(mesh):
    return jax.shard_map(
        shards,
        mesh=mesh,
        in_specs=(
            P(None, ("groups", "panels", "cols")),
            P(),
            P("groups", None, None),
            P(None, ("groups", "panels", "cols")),
            P(("groups", "panels", "cols")),
            P(("groups", "panels", "cols"), None),
            P("groups"),
            P(),
        ),
        out_specs=(
            P(("groups", "phase"), None, ("panels", "cols")),
            P(("groups", "phase"), None, ("panels", "cols")),
        ),
        check_vma=False,
    )
```
